512 devices in a mesh: tm: 32 (over z, x_hi), height: 16 (over x_lo, y, core).
Axes of the slice: x: 4 (x_hi: 2, x_lo: 2; x = x_hi * 2 + x_lo), y: 4, z: 16, core: 2. Of those that a mesh axis runs over, the one named last changes fastest.
Arguments:
- clip: bfloat16 [64, 64, 32, 128], P('tm', 'height'), may hold values from -6 to 6
- first_filter: bfloat16 [3, 3, 3, 128, 256], replicated, may hold values from -0.109375 to 0.109375
- second_filter: bfloat16 [3, 3, 3, 256, 256], P(None, None, None, None, 'height'), may hold values from -0.078125 to 0.078125
- upstream: bfloat16 [32, 32, 16, 256], P('tm', 'height'), may hold values from -6 to 6
Outputs:
- grad_clip: bfloat16 [64, 64, 32, 128], P('tm', 'height')
- grad_filter: float32 [3, 3, 3, 128, 256], P(None, None, None, 'tm', 'height')
The draws below stay inside these ranges and needn't reach their ends.
All inputs are finite; a program needn't handle non-finite values.
Results may differ from the reference program's by a relative error of at most 0.0049.
Values may be sent and summed in bfloat16 or wider, within the bound.
No kernel may reach another device: no remote copies, remote signals or barrier semaphores. Data moves between devices by JAX's collectives and lax.ppermute only.
A program may use at most 64 MiB of HBM per device.

```python
import jax
import jax.numpy as jnp
from jax import lax

C0 = 128
C1 = 256
C2 = 256
WIDTH = 32
FRAMES = 64
ROWS = 64


def raised(entries, key, source, target, shards_of, factor):
    owner, partner = [(jnp.arange(entries.shape[position]) // (entries.shape[position] // shards_of)).reshape([-1 if axis == position else 1 for axis in range(entries.ndim)]) for position in (source, target)]
    chosen = jax.random.permutation(key, shards_of)[partner]
    strong = (owner == chosen) | (owner == (partner + shards_of // 2) % shards_of)
    return jnp.where(strong, factor * entries, entries)


def shard_levels(rng, extent, shards, low, top_value):
    gain, own = 1.0, jax.random.fold_in(rng, 6)
    for dim, blocks in shards:
        steps = jnp.exp(jax.random.uniform(jax.random.fold_in(own, dim), (blocks,), jnp.float32, low / len(shards), top_value / len(shards)))
        gain = gain * jnp.repeat(steps, extent[dim] // blocks).reshape([-1 if axis == dim else 1 for axis in range(len(extent))])
    return gain


def gaussian(key, shape, scale, limit, split=(), held_as=jnp.bfloat16):
    gain = shard_levels(key, shape, split, -0.22, 0.18) if split else 1.0
    array = jax.random.normal(key, shape, jnp.float32) * scale * gain
    return jnp.minimum(jnp.maximum(array, -limit), limit).astype(held_as)


def gaussian_with(own_key, extent, scale, limit, pieces, heavy, dtype=jnp.bfloat16):
    result = scale * jax.random.normal(own_key, extent, jnp.float32)
    if pieces:
        result = result * shard_levels(own_key, extent, pieces, -0.22, 0.18)
    return jnp.clip(raised(result, jax.random.fold_in(own_key, 3), *heavy), -limit, limit).astype(dtype)


def setup_inputs(seed: int = 0) -> dict:
    arg_keys = jax.random.split(jax.random.key(seed), 5)
    clip = gaussian_with(arg_keys[0], (FRAMES, ROWS, WIDTH, C0), 1.0, 6.0, ((0, 32), (1, 16)), (0, 3, 32, 2.75))
    first_filter = gaussian(arg_keys[1], (3, 3, 3, C0, C1), (27 * C0) ** -0.5, 0.109375)
    second_filter = gaussian(arg_keys[2], (3, 3, 3, C1, C2), (27 * C1) ** -0.5, 0.078125, ((4, 16),))
    upstream = gaussian(arg_keys[3], (FRAMES // 2, ROWS // 2, WIDTH // 2, C2), 1.0, 6.0, ((0, 32), (1, 16)))
    return dict(clip=clip, first_filter=first_filter, second_filter=second_filter, upstream=upstream)


def conv_taps(padded, filt, frames, rows, width):
    cin = padded.shape[3]
    total = jnp.zeros((frames * rows * width, filt.shape[4]), jnp.float32)
    for tap_a in range(3):
        for tap_b in range(3):
            for tap_c in range(3):
                piece = padded[tap_a:tap_a + frames, tap_b:tap_b + rows, tap_c:tap_c + width].reshape(-1, cin)
                total = total + jnp.dot(piece, filt[tap_a, tap_b, tap_c], preferred_element_type=jnp.float32)
    return total.reshape(frames, rows, width, -1)


def reference(clip, first_filter, second_filter, upstream):
    frames, rows, width, cin = clip.shape
    chans = first_filter.shape[4]
    padded = jnp.pad(clip, ((2, 0), (1, 1), (1, 1), (0, 0)))
    preact = conv_taps(padded, first_filter, frames, rows, width)
    ext = jnp.pad(upstream, ((0, 1), (0, 1), (0, 0), (0, 0)))
    out_t, out_r, out_w = ext.shape[0], ext.shape[1], ext.shape[2]
    flat = ext.reshape(-1, ext.shape[3])
    buffer = jnp.zeros((frames + 3, rows + 3, width + 2, chans), jnp.float32)
    for tap_a in range(3):
        for tap_b in range(3):
            for tap_c in range(3):
                contrib = jnp.dot(flat, second_filter[tap_a, tap_b, tap_c].T, preferred_element_type=jnp.float32)
                contrib = contrib.reshape(out_t, out_r, out_w, chans)
                buffer = buffer.at[tap_a:tap_a + 2 * out_t:2, tap_b:tap_b + 2 * out_r:2, tap_c:tap_c + 2 * out_w:2].add(contrib)
    grad_act = buffer[2:frames + 2, 1:rows + 1, 1:width + 1]
    sig = jax.nn.sigmoid(preact)
    grad_pre = (grad_act * sig * (1.0 + preact * (1.0 - sig))).astype(jnp.bfloat16)
    dflat = grad_pre.reshape(-1, chans)
    parts = []
    for tap_a in range(3):
        for tap_b in range(3):
            for tap_c in range(3):
                piece = padded[tap_a:tap_a + frames, tap_b:tap_b + rows, tap_c:tap_c + width].reshape(-1, cin)
                parts.append(lax.dot_general(piece, dflat, (((0,), (0,)), ((), ())), preferred_element_type=jnp.float32))
    scale = 1.0 / float(frames * rows * width) ** 0.5
    grad_filter = jnp.stack(parts).reshape(3, 3, 3, cin, chans) * scale
    padded_grad = jnp.pad(grad_pre, ((0, 2), (1, 1), (1, 1), (0, 0)))
    total = jnp.zeros((frames * rows * width, cin), jnp.float32)
    for tap_a in range(3):
        for tap_b in range(3):
            for tap_c in range(3):
                piece = padded_grad[2 - tap_a:2 - tap_a + frames, 2 - tap_b:2 - tap_b + rows, 2 - tap_c:2 - tap_c + width].reshape(-1, chans)
                total = total + jnp.dot(piece, first_filter[tap_a, tap_b, tap_c].T, preferred_element_type=jnp.float32)
    grad_clip = total.reshape(frames, rows, width, cin).astype(jnp.bfloat16)
    return grad_clip, grad_filter
```

```python
import functools

import jax
import jax.numpy as jnp
from jax import lax
from jax.experimental import pallas as pl
from jax.experimental.pallas import tpu as pltpu
from jax.sharding import PartitionSpec as P

F32, BF16 = jnp.float32, jnp.bfloat16
CORES = 2
OWN = 64
FRAMES = 4
ROWS, SPAN = 8, 10
HIGH, HALF_HIGH, HALF = ROWS + 4, ROWS // 2 + 2, SPAN // 2
MIDDLE = (1, 2, 3, 0)

LONG = {0: ((2, 0),), 1: ((0, 0), (1, 1))}
WIDE = {0: ((1, 0), (2, 1)), 1: ((0, 1),)}


def shift_classes():
    classes = []
    for t in (1, 0):
        for h in (1, 0):
            for w in (0, 1):
                taps = tuple(
                    ((a, b, c), (fp, ip, jp))
                    for a, fp in LONG[t]
                    for b, ip in LONG[h]
                    for c, jp in WIDE[w]
                )
                classes.append(((t, h, w), taps))
    return classes


CLASSES = shift_classes()
TAP_ORDER = [tap for _, taps in CLASSES for tap, _ in taps]


def mm(lhs, rhs):
    return jnp.dot(lhs, rhs, preferred_element_type=F32)


def one_hot(rows, cols, column_of):
    row = lax.broadcasted_iota(jnp.int32, (rows, cols), 0)
    col = lax.broadcasted_iota(jnp.int32, (rows, cols), 1)
    return jnp.where(column_of(row) == col, 1.0, 0.0).astype(BF16)


def call(kernel, out, args, scratch=(), fetch=(), idle=(), alias=None, flops=0, limit=16):
    n_in, n_out, n_scratch = len(args), len(out), len(scratch)

    def run(*refs):
        ins, outs = list(refs[:n_in]), refs[n_in : n_in + n_out]
        rest = refs[n_in + n_out :]
        if fetch:
            landing, sems = rest[n_scratch:-1], rest[-1]
            copies = [
                pltpu.make_async_copy(ins[i], landing[k], sems.at[k]) for k, i in enumerate(fetch)
            ]
            for copy in copies:
                copy.start()
            for copy in copies:
                copy.wait()
            for k, i in enumerate(fetch):
                ins[i] = landing[k]
        kernel(*ins, *outs, *rest[:n_scratch])

    spec = pl.BlockSpec(memory_space=pltpu.VMEM)
    far = pl.BlockSpec(memory_space=pl.ANY)
    moved = sum(x.size * x.dtype.itemsize for x in list(args) + list(out))
    extra = [pltpu.VMEM(args[i].shape, args[i].dtype) for i in fetch]
    if fetch:
        extra.append(pltpu.SemaphoreType.DMA((len(fetch),)))
    return pl.pallas_call(
        run,
        out_shape=tuple(out),
        in_specs=[far if i in fetch or i in idle else spec for i in range(n_in)],
        out_specs=tuple([far if i in (alias or {}).values() else spec for i in range(n_out)]),
        input_output_aliases=dict(alias or {}),
        scratch_shapes=list(scratch) + extra,
        compiler_params=pltpu.CompilerParams(vmem_limit_bytes=limit * 1024 * 1024),
        cost_estimate=pl.CostEstimate(flops=flops, bytes_accessed=moved, transcendentals=0),
    )(*args)


def shaped(shape, dtype):
    return jax.ShapeDtypeStruct(shape, dtype)


def own_channel(place, x, core):
    return (2 * (place // 8) + core) * 16 + 8 * x + place % 8


def filter_pieces_kernel(second, out):
    taps, depth, chans = second.shape
    x = lax.axis_index("tm") % 2
    row = lax.broadcasted_iota(jnp.int32, (chans, 2 * OWN), 0)
    col = lax.broadcasted_iota(jnp.int32, (chans, 2 * OWN), 1)
    order = jnp.where(own_channel(col % OWN, x, col // OWN) == row, 1.0, 0.0).astype(BF16)
    moved = mm(second[...].reshape(taps * depth, chans), order).astype(BF16)
    moved = moved.reshape(taps, depth, 2 * OWN)
    for place in range(0, len(TAP_ORDER), 2):
        pair = TAP_ORDER[place : place + 2]
        for core in range(CORES):
            lanes = slice(core * OWN, (core + 1) * OWN)
            piece = jnp.concatenate([moved[a * 9 + b * 3 + c, :, lanes] for a, b, c in pair], 1)
            for p in range(core, out.shape[0], CORES):
                out[p, :, place * OWN : place * OWN + piece.shape[1]] = piece


def own_filter_kernel(first, band, turned):
    chans = first.shape[1]
    x, core = lax.axis_index("tm") % 2, lax.axis_index("height") % CORES

    def source(place):
        return own_channel(place % OWN, x, core)

    row = lax.broadcasted_iota(jnp.int32, (chans, 2 * OWN), 0)
    col = lax.broadcasted_iota(jnp.int32, (chans, 2 * OWN), 1)
    pick = jnp.where(source(col) == row, 1.0, 0.0).astype(BF16)
    twice = mm(first[...], pick)
    lane = lax.broadcasted_iota(jnp.int32, (128, 2 * OWN), 1)
    for ab in range(9):
        for s in range(4):
            left = twice[(ab * 3 + s) * 128 : (ab * 3 + s + 1) * 128] if s < 3 else 0.0
            right = twice[(ab * 3 + s - 1) * 128 : (ab * 3 + s) * 128] if s > 0 else 0.0
            both = jnp.where(lane < OWN, left, right)
            band[ab, s * 128 : (s + 1) * 128] = both.astype(BF16)
    row = lax.broadcasted_iota(jnp.int32, (OWN, chans), 0)
    col = lax.broadcasted_iota(jnp.int32, (OWN, chans), 1)
    pick = jnp.where(source(row) == col, 1.0, 0.0).astype(BF16)
    flat = lax.dot_general(
        pick, first[...], (((1,), (1,)), ((), ())), preferred_element_type=F32
    ).astype(BF16)
    for ab in range(9):
        for slot, s in enumerate(MIDDLE):
            for jp in range(2):
                c = jp + 2 - s
                if 0 <= c <= 2:
                    piece = flat[:, (ab * 3 + c) * 128 : (ab * 3 + c + 1) * 128]
                else:
                    piece = jnp.zeros((OWN, 128), BF16)
                turned[ab, slot * OWN : (slot + 1) * OWN, jp * 128 : (jp + 1) * 128] = piece


def stack_kernel(clip, up, out):
    for f in range(2):
        out[4 * f : 4 * f + 4] = clip[f]
    for half in range(2):
        out[8:10, 16 * half : 16 * half + 16] = up[0, :, :, 128 * half : 128 * half + 128]


def pack_kernel(here, pair, odd, even, _, packed, edge, __):
    first = lax.axis_index("tm") % 2 == 0
    at_top = lax.axis_index("height") % CORES == 0
    one = jnp.where(first, here[...], pair[...])
    two = jnp.where(first, pair[...], here[...])
    past = jnp.where(first, odd[...], even[...])
    next_up = jnp.where(first, even[8:10], odd[8:10])
    for f in range(6):
        src = (past, one, two)[f // 2][4 * (f % 2) : 4 * (f % 2) + 4]
        packed[4 * f : 4 * f + 4] = src
        edge[2 * f : 2 * f + 2] = jnp.where(at_top, src[:2], src[2:])
    for t, src in enumerate((one[8:10], two[8:10], next_up)):
        packed[24 + 2 * t : 26 + 2 * t] = src
        edge[12 + t] = jnp.where(at_top, src[0], src[1])


def preact_kernel(own, other, near, far, filters, wide, ups, pre, band, ext):
    member = lax.axis_index("height") % CORES
    even = member == 0
    above = jnp.where(even, near[...], far[...])
    below = jnp.where(even, far[...], near[...])
    for f in range(6):
        base = f * HIGH
        band[pl.ds(base + 2 + 4 * member, 4)] = own[4 * f : 4 * f + 4]
        band[pl.ds(base + 6 - 4 * member, 4)] = other[4 * f : 4 * f + 4]
        band[base : base + 2] = above[2 * f : 2 * f + 2]
        band[base + ROWS + 2 : base + ROWS + 4] = below[2 * f : 2 * f + 2]
    for t in range(3):
        base, unit = t * HALF_HIGH, 24 + 2 * t
        for half in range(2):
            lanes = slice(128 * half, 128 * half + 128)
            subs = slice(16 * half, 16 * half + 16)
            ext[pl.ds(base + 1 + 2 * member, 2), :, lanes] = own[unit : unit + 2, subs]
            ext[pl.ds(base + 3 - 2 * member, 2), :, lanes] = other[unit : unit + 2, subs]
            ext[base, :, lanes] = above[12 + t, subs]
            ext[base + HALF_HIGH - 1, :, lanes] = below[12 + t, subs]
    units = ext.shape[0]
    flat = ext[...].reshape(units * 16, 256)
    shift = one_hot(units * 16, units * 16, lambda r: jnp.where(r % 16 == 15, -1, r + 1))
    ups[0] = flat.reshape(units, 16, 256)
    ups[1] = mm(shift, flat).astype(BF16).reshape(units, 16, 256)

    def column(r):
        s, unit, w = r // 128, (r // 16) % 8, 2 * (r % 16) + r // 128 - 1
        return jnp.where((w >= 0) & (w < 32), unit * 32 + w, -1)

    matrix = one_hot(512, 256, column)
    for g in range(band.shape[0] // 8):
        moved = mm(matrix, band[8 * g : 8 * g + 8].reshape(256, 128)).astype(BF16)
        for s in range(4):
            piece = moved[128 * s : 128 * s + 128].reshape(8, 16, 128)
            wide[8 * g : 8 * g + 8, :, s * 128 : (s + 1) * 128] = piece
    total = jnp.zeros((FRAMES * SPAN * 16, 2 * OWN), F32)
    for a in range(3):
        for b in range(3):
            tops = [(a + f) * HIGH + b for f in range(FRAMES)]
            win = jnp.concatenate([wide[x : x + SPAN] for x in tops], 0)
            total = total + mm(win.reshape(FRAMES * SPAN * 16, 512), filters[a * 3 + b])
    total = total.reshape(FRAMES, SPAN, 16, 2 * OWN)
    for f in range(FRAMES):
        for r in range(SPAN):
            pre[f % 2, r % 2, f // 2, r // 2] = total[f, r]


def gradient_kernel(second, ups, pre, wide, grad, parts):
    group = lax.axis_index("height") // CORES
    first_band = group == 0
    last_band = group == lax.axis_size("height") // CORES - 1
    even, odd = {}, {}
    offset = 0
    for (t, h, w), taps in CLASSES:
        tops = [(t + q) * HALF_HIGH + h for q in range(2)]
        lhs = jnp.concatenate([ups[w, x : x + HALF] for x in tops], 0).reshape(32 * HALF, 256)
        prod = mm(lhs, second[:, offset : offset + len(taps) * OWN])
        offset += len(taps) * OWN
        total, step = (odd, 1) if w else (even, 2)
        for k in range(0, len(taps), step):
            key = taps[k][1][:2]
            piece = prod[:, k * OWN : (k + step) * OWN]
            total[key] = total[key] + piece if key in total else piece
    blank = jnp.zeros((32 * HALF, OWN), F32)
    for (fp, ip), act in even.items():
        act = act + jnp.concatenate([blank, odd[fp, ip]], 1)
        x = pre[fp, ip].reshape(32 * HALF, 2 * OWN)
        sig = jax.nn.sigmoid(x)
        g = (act * sig * (1.0 + x * (1.0 - sig))).reshape(2, HALF, 16, 2 * OWN)
        for q in range(2):
            for p in range(HALF):
                piece, r = g[q, p], 2 * p + ip
                if r == 0:
                    piece = jnp.where(first_band, 0.0, piece)
                if r == SPAN - 1:
                    piece = jnp.where(last_band, 0.0, piece)
                grad[2 * q + fp, r] = piece.astype(BF16)
    turned = grad[:, 1 : 1 + ROWS].reshape(FRAMES * ROWS * 16, 2 * OWN).T
    strips = []
    for a in range(3):
        for b in range(3):
            tops = [(a + f) * HIGH + 1 + b for f in range(FRAMES)]
            win = jnp.concatenate([wide[x : x + ROWS] for x in tops], 0)
            prod = mm(turned, win.reshape(FRAMES * ROWS * 16, 512))
            for c in range(3):
                piece = prod[:OWN, 128 * c : 128 * c + 128]
                piece = piece + prod[OWN:, 128 * c + 128 : 128 * c + 256]
                strips.append(piece.astype(BF16))
    strips.append(jnp.zeros_like(strips[0]))
    row = lax.broadcasted_iota(jnp.int32, (256, 256), 0)
    col = lax.broadcasted_iota(jnp.int32, (256, 256), 1)
    x, tap, z, e = col // 128, (col // 64) % 2, (col // 4) % 16, col % 4
    order = jnp.where(tap * 128 + 8 * z + 4 * x + e == row, 1.0, 0.0).astype(BF16)
    blocks = OWN // 8
    for k in range(7):
        pairs = [jnp.concatenate(strips[i : i + 2], 1) for i in (4 * k, 4 * k + 2)]
        pairs = [mm(pair, order).reshape(blocks, 8, 256) for pair in pairs]
        both = jnp.concatenate(pairs, 1).astype(BF16)
        for x in range(2):
            parts[x * blocks : (x + 1) * blocks, k] = both[:, :, 128 * x : 128 * x + 128]


def sum_turn_kernel(parts, out):
    blank = jnp.zeros((16, 128), F32)
    blocks = parts.shape[0] // 2
    halves = []
    for x in range(2):
        total = parts[x * blocks].astype(F32)
        for i in range(1, blocks):
            total = total + parts[x * blocks + i].astype(F32)
        halves += [total.reshape(112, 128), blank]
    flat = jnp.concatenate(halves, 0).T
    for z in range(16):
        rows = [(tap * 64 + z * 4, x) for x in range(2) for tap in range(2)]
        block = [flat[r : r + 4, 128 * x : 128 * x + 128] for r, x in rows]
        out[z] = jnp.concatenate(block, 0).astype(BF16)


def finish_kernel(scale, parts, out):
    total = parts[0].astype(F32)
    for i in range(1, parts.shape[0]):
        total = total + parts[i].astype(F32)
    total = total * scale
    for k in range(27):
        lanes = slice(8 * (k // 2), 8 * (k // 2) + 8)
        rows = [8 * x + 4 * (k % 2) for x in range(2)]
        out[k] = jnp.concatenate([total[r : r + 4, lanes] for r in rows], 1)


def clip_kernel(grad, following, filters, _, keep, send, wide):
    lane = lax.broadcasted_iota(jnp.int32, (192, 2 * OWN), 1)
    up = one_hot(192, 192, lambda r: jnp.where(r % 16 == 15, -1, r + 1))
    down = one_hot(192, 192, lambda r: jnp.where(r % 16 == 0, -1, r - 1))
    for f in range(FRAMES + 2):
        src = grad[f] if f < FRAMES else following[f - FRAMES]
        wide[f * SPAN : (f + 1) * SPAN, :, : 2 * OWN] = src
    for g in range(0, (FRAMES + 2) * SPAN, 12):
        block = wide[g : g + 12, :, : 2 * OWN].reshape(192, 2 * OWN)
        moved = jnp.where(lane < OWN, mm(up, block), mm(down, block)).astype(BF16)
        wide[g : g + 12, :, 2 * OWN :] = moved.reshape(12, 16, 2 * OWN)
    total = jnp.zeros((FRAMES * ROWS * 16, 256), F32)
    for a in range(3):
        for b in range(3):
            tops = [(f + 2 - a) * SPAN + 2 - b for f in range(FRAMES)]
            win = jnp.concatenate([wide[x : x + ROWS] for x in tops], 0)
            total = total + mm(win.reshape(FRAMES * ROWS * 16, 4 * OWN), filters[a * 3 + b])
    total = total.reshape(FRAMES, ROWS, 16, 256)
    low, high = total[:, :4], total[:, 4:]
    even = lax.axis_index("height") % CORES == 0
    keep[...] = jnp.where(even, low, high)
    send[...] = jnp.where(even, high, low)


def halve_kernel(kept, got, keep, send):
    total = kept[...] + got[...]
    first = lax.axis_index("tm") % 2 == 0
    low, high = total[:2], total[2:]
    keep[...] = jnp.where(first, low, high)
    send[...] = jnp.where(first, high, low).astype(BF16)


def join_kernel(kept, got, out):
    total = (kept[...] + got[...].astype(F32)).astype(BF16).reshape(128, 256)
    low = one_hot(256, 128, lambda r: jnp.where(r % 2 == 0, (r // 32) * 16 + (r % 32) // 2, -1))
    high = one_hot(256, 128, lambda r: jnp.where(r % 2 == 1, (r // 32) * 16 + (r % 32) // 2, -1))
    moved = mm(low, total[:, :128]) + mm(high, total[:, 128:])
    out[...] = moved.astype(BF16).reshape(out.shape)


def inside(pairs, count):
    return [(i, k) for i, k in pairs if 0 <= k < count]


def body(clip, first_filter, second_filter, upstream):
    frames, rows, width, cin = clip.shape
    chans = first_filter.shape[4]
    tms, heights = lax.axis_size("tm"), lax.axis_size("height")
    lines = tms // 2
    siblings = [(i, i ^ 1) for i in range(heights)]
    blocks = [(t, t ^ 1) for t in range(tms)]

    (here,) = call(stack_kernel, [shaped((10, 32, 128), BF16)], [clip, upstream], fetch=(0, 1), limit=60)
    pair = lax.ppermute(here, "tm", blocks)
    odd_pairs = inside([(t, t + 1 if t % 2 else t - 1) for t in range(tms)], tms)
    even_pairs = inside([(t, t + 2 if t % 2 else t - 2) for t in range(tms)], tms)
    odd = lax.ppermute(here, "tm", odd_pairs)
    even = lax.ppermute(here, "tm", even_pairs)

    second = jnp.swapaxes(second_filter, 3, 4).reshape(27, chans // heights, chans)
    (pieces,) = call(
        filter_pieces_kernel,
        [shaped((heights, chans // heights, 27 * OWN), BF16)],
        [second],
        fetch=(0,),
        flops=2 * 27 * 16 * 256 * 128,
    )
    band, turned = call(
        own_filter_kernel,
        [shaped((9, 512, 2 * OWN), BF16), shaped((9, 4 * OWN, 2 * cin), BF16)],
        [first_filter.reshape(27 * cin, chans)],
        fetch=(0,),
        flops=4 * 27 * 128 * 256 * 128,
    )

    packed, edge, pieces = call(
        pack_kernel,
        [shaped((30, 32, 128), BF16), shaped((15, 32, 128), BF16), shaped(pieces.shape, BF16)],
        [here, pair, odd, even, pieces],
        fetch=(1, 2, 3),
        idle=(4,),
        alias={4: 2},
    )
    second = lax.all_to_all(pieces, "height", 0, 0).reshape(chans, 27 * OWN)
    near_pairs = inside([(i, i + 1 if i % 2 else i - 1) for i in range(heights)], heights)
    far_pairs = inside([(i, i + 2 if i % 2 else i - 2) for i in range(heights)], heights)
    other = lax.ppermute(packed, "height", siblings)
    near = lax.ppermute(edge, "height", near_pairs)
    far = lax.ppermute(edge, "height", far_pairs)

    units, up_units = 6 * HIGH, 3 * HALF_HIGH
    wide, ups, pre = call(
        preact_kernel,
        [
            shaped((units, 16, 512), BF16),
            shaped((2, up_units, 16, 256), BF16),
            shaped((2, 2, 2, HALF, 16, 2 * OWN), F32),
        ],
        [packed, other, near, far, band],
        scratch=[pltpu.VMEM((units, 32, 128), BF16), pltpu.VMEM((up_units, 16, 256), BF16)],
        fetch=(1, 2, 3),
        flops=2 * 640 * 9 * 512 * 128,
    )
    grad_pre, parts = call(
        gradient_kernel,
        [shaped((FRAMES, SPAN, 16, 2 * OWN), BF16), shaped((heights, 7, 16, cin), BF16)],
        [second, ups, pre, wide],
        fetch=(0,),
        flops=2 * 512 * 9 * 512 * 128,
    )

    planes = [
        [(2 * z + x) * heights + CORES * g + core for x in range(2) for g in range(heights // 2)]
        for z in range(lines)
        for core in range(CORES)
    ]
    parts = lax.all_to_all(parts, ("tm", "height"), 0, 0, axis_index_groups=planes)
    (sums,) = call(sum_turn_kernel, [shaped((lines, 16, 128), BF16)], [parts], fetch=(0,))
    columns = [[2 * z + x for z in range(lines)] for x in range(2)]
    summed = lax.all_to_all(sums, "tm", 0, 0, axis_index_groups=columns)
    count = frames * tms * rows * heights * width
    (grad_filter,) = call(
        functools.partial(finish_kernel, 1.0 / float(count) ** 0.5),
        [shaped((27, cin // tms, chans // heights), F32)],
        [summed],
        fetch=(0,),
    )
    grad_filter = grad_filter.reshape(3, 3, 3, cin // tms, chans // heights)

    back = inside([(t, t - 2) for t in range(tms)], tms)
    following = lax.ppermute(grad_pre[:2], "tm", back)
    keep, send = call(
        clip_kernel,
        [shaped((FRAMES, rows, 16, 2 * cin), F32)] * 2,
        [grad_pre, following, turned, sums],
        scratch=[pltpu.VMEM(((FRAMES + 2) * SPAN, 16, 4 * OWN), BF16)],
        fetch=(1,),
        idle=(3,),
        flops=2 * 512 * 9 * 256 * 256,
    )
    got = lax.ppermute(send, "height", siblings)
    keep, send = call(
        halve_kernel,
        [shaped((2, rows, 16, 2 * cin), F32), shaped((2, rows, 16, 2 * cin), BF16)],
        [keep, got],
        fetch=(1,),
    )
    got = lax.ppermute(send, "tm", blocks)
    (grad_clip,) = call(join_kernel, [shaped(clip.shape, BF16)], [keep, got], fetch=(1,))
    return (grad_clip, grad_filter)


def solution(mesh):
    in_specs = (
        P("tm", "height", None, None),
        P(),
        P(None, None, None, None, "height"),
        P("tm", "height", None, None),
    )
    out_specs = (P("tm", "height", None, None), P(None, None, None, "tm", "height"))
    return jax.shard_map(body, mesh=mesh, in_specs=in_specs, out_specs=out_specs, check_vma=False)
```

```python
import functools

import jax
import jax.numpy as jnp
from jax import lax
from jax.experimental import pallas as pl
from jax.experimental.pallas import tpu as pltpu
from jax.sharding import PartitionSpec as P

F32, BF16 = jnp.float32, jnp.bfloat16
CORES = 2
OWN = 64
FRAMES = 4
ROWS, SPAN = 8, 10
HIGH, HALF_HIGH, HALF = ROWS + 4, ROWS // 2 + 2, SPAN // 2
MIDDLE = (1, 2, 3, 0)

LONG = {0: ((2, 0),), 1: ((0, 0), (1, 1))}
WIDE = {0: ((1, 0), (2, 1)), 1: ((0, 1),)}


def shift_classes():
    classes = []
    for t in (1, 0):
        for h in (1, 0):
            for w in (0, 1):
                taps = tuple(
                    ((a, b, c), (fp, ip, jp))
                    for a, fp in LONG[t]
                    for b, ip in LONG[h]
                    for c, jp in WIDE[w]
                )
                classes.append(((t, h, w), taps))
    return classes


CLASSES = shift_classes()
TAP_ORDER = [tap for _, taps in CLASSES for tap, _ in taps]


def mm(lhs, rhs):
    return jnp.dot(lhs, rhs, preferred_element_type=F32)


def one_hot(rows, cols, column_of):
    row = lax.broadcasted_iota(jnp.int32, (rows, cols), 0)
    col = lax.broadcasted_iota(jnp.int32, (rows, cols), 1)
    return jnp.where(column_of(row) == col, 1.0, 0.0).astype(BF16)


def call(kernel, out, args, scratch=(), fetch=(), idle=(), flops=0, limit=16):
    n_in, n_out, n_scratch = len(args), len(out), len(scratch)

    def run(*refs):
        ins, outs = list(refs[:n_in]), refs[n_in : n_in + n_out]
        rest = refs[n_in + n_out :]
        if fetch:
            landing, sems = rest[n_scratch:-1], rest[-1]
            copies = [
                pltpu.make_async_copy(ins[i], landing[k], sems.at[k]) for k, i in enumerate(fetch)
            ]
            for copy in copies:
                copy.start()
            for copy in copies:
                copy.wait()
            for k, i in enumerate(fetch):
                ins[i] = landing[k]
        kernel(*ins, *outs, *rest[:n_scratch])

    spec = pl.BlockSpec(memory_space=pltpu.VMEM)
    far = pl.BlockSpec(memory_space=pl.ANY)
    moved = sum(x.size * x.dtype.itemsize for x in list(args) + list(out))
    extra = [pltpu.VMEM(args[i].shape, args[i].dtype) for i in fetch]
    if fetch:
        extra.append(pltpu.SemaphoreType.DMA((len(fetch),)))
    return pl.pallas_call(
        run,
        out_shape=tuple(out),
        in_specs=[far if i in fetch or i in idle else spec for i in range(n_in)],
        out_specs=tuple([spec] * n_out),
        scratch_shapes=list(scratch) + extra,
        compiler_params=pltpu.CompilerParams(vmem_limit_bytes=limit * 1024 * 1024),
        cost_estimate=pl.CostEstimate(flops=flops, bytes_accessed=moved, transcendentals=0),
    )(*args)


def shaped(shape, dtype):
    return jax.ShapeDtypeStruct(shape, dtype)


def own_channel(place, x, core):
    return (2 * (place // 8) + core) * 16 + 8 * x + place % 8


def filter_pieces_kernel(second, out):
    taps, depth, chans = second.shape
    x = lax.axis_index("tm") % 2
    row = lax.broadcasted_iota(jnp.int32, (chans, 2 * OWN), 0)
    col = lax.broadcasted_iota(jnp.int32, (chans, 2 * OWN), 1)
    order = jnp.where(own_channel(col % OWN, x, col // OWN) == row, 1.0, 0.0).astype(BF16)
    moved = mm(second[...].reshape(taps * depth, chans), order).astype(BF16)
    moved = moved.reshape(taps, depth, 2 * OWN)
    for place in range(0, len(TAP_ORDER), 2):
        pair = TAP_ORDER[place : place + 2]
        for core in range(CORES):
            lanes = slice(core * OWN, (core + 1) * OWN)
            piece = jnp.concatenate([moved[a * 9 + b * 3 + c, :, lanes] for a, b, c in pair], 1)
            for p in range(core, out.shape[0], CORES):
                out[p, :, place * OWN : place * OWN + piece.shape[1]] = piece


def own_filter_kernel(first, band, turned):
    chans = first.shape[1]
    x, core = lax.axis_index("tm") % 2, lax.axis_index("height") % CORES

    def source(place):
        return own_channel(place % OWN, x, core)

    row = lax.broadcasted_iota(jnp.int32, (chans, 2 * OWN), 0)
    col = lax.broadcasted_iota(jnp.int32, (chans, 2 * OWN), 1)
    pick = jnp.where(source(col) == row, 1.0, 0.0).astype(BF16)
    twice = mm(first[...], pick)
    lane = lax.broadcasted_iota(jnp.int32, (128, 2 * OWN), 1)
    for ab in range(9):
        for s in range(4):
            left = twice[(ab * 3 + s) * 128 : (ab * 3 + s + 1) * 128] if s < 3 else 0.0
            right = twice[(ab * 3 + s - 1) * 128 : (ab * 3 + s) * 128] if s > 0 else 0.0
            both = jnp.where(lane < OWN, left, right)
            band[ab, s * 128 : (s + 1) * 128] = both.astype(BF16)
    row = lax.broadcasted_iota(jnp.int32, (OWN, chans), 0)
    col = lax.broadcasted_iota(jnp.int32, (OWN, chans), 1)
    pick = jnp.where(source(row) == col, 1.0, 0.0).astype(BF16)
    flat = lax.dot_general(
        pick, first[...], (((1,), (1,)), ((), ())), preferred_element_type=F32
    ).astype(BF16)
    for ab in range(9):
        for slot, s in enumerate(MIDDLE):
            for jp in range(2):
                c = jp + 2 - s
                if 0 <= c <= 2:
                    piece = flat[:, (ab * 3 + c) * 128 : (ab * 3 + c + 1) * 128]
                else:
                    piece = jnp.zeros((OWN, 128), BF16)
                turned[ab, slot * OWN : (slot + 1) * OWN, jp * 128 : (jp + 1) * 128] = piece


def stack_kernel(clip, up, out):
    for f in range(2):
        out[4 * f : 4 * f + 4] = clip[f]
    for half in range(2):
        out[8:10, 16 * half : 16 * half + 16] = up[0, :, :, 128 * half : 128 * half + 128]


def pack_kernel(here, pair, odd, even, packed, edge):
    first = lax.axis_index("tm") % 2 == 0
    at_top = lax.axis_index("height") % CORES == 0
    one = jnp.where(first, here[...], pair[...])
    two = jnp.where(first, pair[...], here[...])
    past = jnp.where(first, odd[...], even[...])
    next_up = jnp.where(first, even[8:10], odd[8:10])
    for f in range(6):
        src = (past, one, two)[f // 2][4 * (f % 2) : 4 * (f % 2) + 4]
        packed[4 * f : 4 * f + 4] = src
        edge[2 * f : 2 * f + 2] = jnp.where(at_top, src[:2], src[2:])
    for t, src in enumerate((one[8:10], two[8:10], next_up)):
        packed[24 + 2 * t : 26 + 2 * t] = src
        edge[12 + t] = jnp.where(at_top, src[0], src[1])


def preact_kernel(own, other, near, far, filters, wide, ups, pre, band, ext):
    member = lax.axis_index("height") % CORES
    even = member == 0
    above = jnp.where(even, near[...], far[...])
    below = jnp.where(even, far[...], near[...])
    for f in range(6):
        base = f * HIGH
        band[pl.ds(base + 2 + 4 * member, 4)] = own[4 * f : 4 * f + 4]
        band[pl.ds(base + 6 - 4 * member, 4)] = other[4 * f : 4 * f + 4]
        band[base : base + 2] = above[2 * f : 2 * f + 2]
        band[base + ROWS + 2 : base + ROWS + 4] = below[2 * f : 2 * f + 2]
    for t in range(3):
        base, unit = t * HALF_HIGH, 24 + 2 * t
        for half in range(2):
            lanes = slice(128 * half, 128 * half + 128)
            subs = slice(16 * half, 16 * half + 16)
            ext[pl.ds(base + 1 + 2 * member, 2), :, lanes] = own[unit : unit + 2, subs]
            ext[pl.ds(base + 3 - 2 * member, 2), :, lanes] = other[unit : unit + 2, subs]
            ext[base, :, lanes] = above[12 + t, subs]
            ext[base + HALF_HIGH - 1, :, lanes] = below[12 + t, subs]
    units = ext.shape[0]
    flat = ext[...].reshape(units * 16, 256)
    shift = one_hot(units * 16, units * 16, lambda r: jnp.where(r % 16 == 15, -1, r + 1))
    ups[0] = flat.reshape(units, 16, 256)
    ups[1] = mm(shift, flat).astype(BF16).reshape(units, 16, 256)

    def column(r):
        s, unit, w = r // 128, (r // 16) % 8, 2 * (r % 16) + r // 128 - 1
        return jnp.where((w >= 0) & (w < 32), unit * 32 + w, -1)

    matrix = one_hot(512, 256, column)
    for g in range(band.shape[0] // 8):
        moved = mm(matrix, band[8 * g : 8 * g + 8].reshape(256, 128)).astype(BF16)
        for s in range(4):
            piece = moved[128 * s : 128 * s + 128].reshape(8, 16, 128)
            wide[8 * g : 8 * g + 8, :, s * 128 : (s + 1) * 128] = piece
    total = jnp.zeros((FRAMES * SPAN * 16, 2 * OWN), F32)
    for a in range(3):
        for b in range(3):
            tops = [(a + f) * HIGH + b for f in range(FRAMES)]
            win = jnp.concatenate([wide[x : x + SPAN] for x in tops], 0)
            total = total + mm(win.reshape(FRAMES * SPAN * 16, 512), filters[a * 3 + b])
    total = total.reshape(FRAMES, SPAN, 16, 2 * OWN)
    for f in range(FRAMES):
        for r in range(SPAN):
            pre[f % 2, r % 2, f // 2, r // 2] = total[f, r]


def gradient_kernel(second, ups, pre, wide, grad, parts):
    group = lax.axis_index("height") // CORES
    first_band = group == 0
    last_band = group == lax.axis_size("height") // CORES - 1
    even, odd = {}, {}
    offset = 0
    for (t, h, w), taps in CLASSES:
        tops = [(t + q) * HALF_HIGH + h for q in range(2)]
        lhs = jnp.concatenate([ups[w, x : x + HALF] for x in tops], 0).reshape(32 * HALF, 256)
        prod = mm(lhs, second[:, offset : offset + len(taps) * OWN])
        offset += len(taps) * OWN
        total, step = (odd, 1) if w else (even, 2)
        for k in range(0, len(taps), step):
            key = taps[k][1][:2]
            piece = prod[:, k * OWN : (k + step) * OWN]
            total[key] = total[key] + piece if key in total else piece
    blank = jnp.zeros((32 * HALF, OWN), F32)
    for (fp, ip), act in even.items():
        act = act + jnp.concatenate([blank, odd[fp, ip]], 1)
        x = pre[fp, ip].reshape(32 * HALF, 2 * OWN)
        sig = jax.nn.sigmoid(x)
        g = (act * sig * (1.0 + x * (1.0 - sig))).reshape(2, HALF, 16, 2 * OWN)
        for q in range(2):
            for p in range(HALF):
                piece, r = g[q, p], 2 * p + ip
                if r == 0:
                    piece = jnp.where(first_band, 0.0, piece)
                if r == SPAN - 1:
                    piece = jnp.where(last_band, 0.0, piece)
                grad[2 * q + fp, r] = piece.astype(BF16)
    turned = grad[:, 1 : 1 + ROWS].reshape(FRAMES * ROWS * 16, 2 * OWN).T
    strips = []
    for a in range(3):
        for b in range(3):
            tops = [(a + f) * HIGH + 1 + b for f in range(FRAMES)]
            win = jnp.concatenate([wide[x : x + ROWS] for x in tops], 0)
            prod = mm(turned, win.reshape(FRAMES * ROWS * 16, 512))
            for c in range(3):
                piece = prod[:OWN, 128 * c : 128 * c + 128]
                piece = piece + prod[OWN:, 128 * c + 128 : 128 * c + 256]
                strips.append(piece.astype(BF16))
    strips.append(jnp.zeros_like(strips[0]))
    row = lax.broadcasted_iota(jnp.int32, (256, 256), 0)
    col = lax.broadcasted_iota(jnp.int32, (256, 256), 1)
    x, tap, z, e = col // 128, (col // 64) % 2, (col // 4) % 16, col % 4
    order = jnp.where(tap * 128 + 8 * z + 4 * x + e == row, 1.0, 0.0).astype(BF16)
    blocks = OWN // 8
    for k in range(7):
        pairs = [jnp.concatenate(strips[i : i + 2], 1) for i in (4 * k, 4 * k + 2)]
        pairs = [mm(pair, order).reshape(blocks, 8, 256) for pair in pairs]
        both = jnp.concatenate(pairs, 1).astype(BF16)
        for x in range(2):
            parts[x * blocks : (x + 1) * blocks, k] = both[:, :, 128 * x : 128 * x + 128]


def sum_turn_kernel(parts, out):
    blank = jnp.zeros((16, 128), F32)
    blocks = parts.shape[0] // 2
    halves = []
    for x in range(2):
        total = parts[x * blocks].astype(F32)
        for i in range(1, blocks):
            total = total + parts[x * blocks + i].astype(F32)
        halves += [total.reshape(112, 128), blank]
    flat = jnp.concatenate(halves, 0).T
    for i in range(16):
        z = (i + 8) % 16
        rows = [(tap * 64 + z * 4, x) for x in range(2) for tap in range(2)]
        block = [flat[r : r + 4, 128 * x : 128 * x + 128] for r, x in rows]
        out[i] = jnp.concatenate(block, 0).astype(BF16)


def finish_kernel(scale, parts, _, out):
    total = parts[0].astype(F32)
    for i in range(1, parts.shape[0]):
        total = total + parts[i].astype(F32)
    total = total * scale
    for k in range(27):
        lanes = slice(8 * (k // 2), 8 * (k // 2) + 8)
        rows = [8 * x + 4 * (k % 2) for x in range(2)]
        out[k] = jnp.concatenate([total[r : r + 4, lanes] for r in rows], 1)


def clip_kernel(grad, following, filters, _, keep, core_send, block_send, cross_send, wide):
    lane = lax.broadcasted_iota(jnp.int32, (192, 2 * OWN), 1)
    up = one_hot(192, 192, lambda r: jnp.where(r % 16 == 15, -1, r + 1))
    down = one_hot(192, 192, lambda r: jnp.where(r % 16 == 0, -1, r - 1))
    for f in range(FRAMES + 2):
        src = grad[f] if f < FRAMES else following[f - FRAMES]
        wide[f * SPAN : (f + 1) * SPAN, :, : 2 * OWN] = src
    for g in range(0, (FRAMES + 2) * SPAN, 12):
        block = wide[g : g + 12, :, : 2 * OWN].reshape(192, 2 * OWN)
        moved = jnp.where(lane < OWN, mm(up, block), mm(down, block)).astype(BF16)
        wide[g : g + 12, :, 2 * OWN :] = moved.reshape(12, 16, 2 * OWN)
    total = jnp.zeros((FRAMES * ROWS * 16, 256), F32)
    for a in range(3):
        for b in range(3):
            tops = [(f + 2 - a) * SPAN + 2 - b for f in range(FRAMES)]
            win = jnp.concatenate([wide[x : x + ROWS] for x in tops], 0)
            total = total + mm(win.reshape(FRAMES * ROWS * 16, 4 * OWN), filters[a * 3 + b])
    total = total.reshape(FRAMES, ROWS, 16, 256)
    low, high = total[:, :4], total[:, 4:]
    even = lax.axis_index("height") % CORES == 0
    first = lax.axis_index("tm") % 2 == 0
    mine, other = jnp.where(even, low, high), jnp.where(even, high, low)
    keep[...] = jnp.where(first, mine[:2], mine[2:])
    block_send[...] = jnp.where(first, mine[2:], mine[:2]).astype(BF16)
    core_send[...] = jnp.where(first, other[:2], other[2:]).astype(BF16)
    cross_send[...] = jnp.where(first, other[2:], other[:2]).astype(BF16)


def join_kernel(kept, core_got, block_got, cross_got, out, mark):
    total = kept[...] + core_got[...].astype(F32)
    total = total + block_got[...].astype(F32) + cross_got[...].astype(F32)
    total = total.astype(BF16).reshape(128, 256)
    low = one_hot(256, 128, lambda r: jnp.where(r % 2 == 0, (r // 32) * 16 + (r % 32) // 2, -1))
    high = one_hot(256, 128, lambda r: jnp.where(r % 2 == 1, (r // 32) * 16 + (r % 32) // 2, -1))
    moved = mm(low, total[:, :128]) + mm(high, total[:, 128:])
    out[...] = moved.astype(BF16).reshape(out.shape)
    mark[...] = jnp.zeros_like(mark)


def inside(pairs, count):
    return [(i, k) for i, k in pairs if 0 <= k < count]


def body(clip, first_filter, second_filter, upstream):
    frames, rows, width, cin = clip.shape
    chans = first_filter.shape[4]
    tms, heights = lax.axis_size("tm"), lax.axis_size("height")
    lines = tms // 2
    siblings = [(i, i ^ 1) for i in range(heights)]
    blocks = [(t, t ^ 1) for t in range(tms)]

    second = jnp.swapaxes(second_filter, 3, 4).reshape(27, chans // heights, chans)
    (pieces,) = call(
        filter_pieces_kernel,
        [shaped((heights, chans // heights, 27 * OWN), BF16)],
        [second],
        fetch=(0,),
        flops=2 * 27 * 16 * 256 * 128,
    )
    second = lax.all_to_all(pieces, "height", 0, 0).reshape(chans, 27 * OWN)

    (here,) = call(stack_kernel, [shaped((10, 32, 128), BF16)], [clip, upstream], fetch=(0, 1), limit=60)
    pair = lax.ppermute(here, "tm", blocks)
    odd_pairs = inside([(t, t + 1 if t % 2 else t - 1) for t in range(tms)], tms)
    even_pairs = inside([(t, t + 2 if t % 2 else t - 2) for t in range(tms)], tms)
    odd = lax.ppermute(here, "tm", odd_pairs)
    even = lax.ppermute(here, "tm", even_pairs)

    band, turned = call(
        own_filter_kernel,
        [shaped((9, 512, 2 * OWN), BF16), shaped((9, 4 * OWN, 2 * cin), BF16)],
        [first_filter.reshape(27 * cin, chans)],
        fetch=(0,),
        flops=4 * 27 * 128 * 256 * 128,
    )

    packed, edge = call(
        pack_kernel,
        [shaped((30, 32, 128), BF16), shaped((15, 32, 128), BF16)],
        [here, pair, odd, even],
        fetch=(1, 2, 3),
    )
    near_pairs = inside([(i, i + 1 if i % 2 else i - 1) for i in range(heights)], heights)
    far_pairs = inside([(i, i + 2 if i % 2 else i - 2) for i in range(heights)], heights)
    other = lax.ppermute(packed, "height", siblings)
    near = lax.ppermute(edge, "height", near_pairs)
    far = lax.ppermute(edge, "height", far_pairs)

    units, up_units = 6 * HIGH, 3 * HALF_HIGH
    wide, ups, pre = call(
        preact_kernel,
        [
            shaped((units, 16, 512), BF16),
            shaped((2, up_units, 16, 256), BF16),
            shaped((2, 2, 2, HALF, 16, 2 * OWN), F32),
        ],
        [packed, other, near, far, band],
        scratch=[pltpu.VMEM((units, 32, 128), BF16), pltpu.VMEM((up_units, 16, 256), BF16)],
        fetch=(1, 2, 3),
        flops=2 * 640 * 9 * 512 * 128,
    )
    grad_pre, parts = call(
        gradient_kernel,
        [shaped((FRAMES, SPAN, 16, 2 * OWN), BF16), shaped((heights, 7, 16, cin), BF16)],
        [second, ups, pre, wide],
        fetch=(0,),
        flops=2 * 512 * 9 * 512 * 128,
    )

    planes = [
        [(2 * z + x) * heights + CORES * g + core for x in range(2) for g in range(heights // 2)]
        for z in range(lines)
        for core in range(CORES)
    ]
    parts = lax.all_to_all(parts, ("tm", "height"), 0, 0, axis_index_groups=planes)
    (sums,) = call(sum_turn_kernel, [shaped((lines, 16, 128), BF16)], [parts], fetch=(0,))
    columns = [[2 * ((i + 8) % lines) + x for i in range(lines)] for x in range(2)]
    summed = lax.all_to_all(sums, "tm", 0, 0, axis_index_groups=columns)

    back = inside([(t, t - 2) for t in range(tms)], tms)
    following = lax.ppermute(grad_pre[:2], "tm", back)
    part = (2, rows, 16, 2 * cin)
    keep, core_send, block_send, cross_send = call(
        clip_kernel,
        [shaped(part, F32)] + [shaped(part, BF16)] * 3,
        [grad_pre, following, turned, sums],
        scratch=[pltpu.VMEM(((FRAMES + 2) * SPAN, 16, 4 * OWN), BF16)],
        fetch=(1,),
        idle=(3,),
        flops=2 * 512 * 9 * 256 * 256,
    )
    crosses = [(t * heights + h, k * heights + i) for t, k in blocks for h, i in siblings]
    core_got = lax.ppermute(core_send, "height", siblings)
    block_got = lax.ppermute(block_send, "tm", blocks)
    cross_got = lax.ppermute(cross_send, ("tm", "height"), crosses)
    grad_clip, mark = call(
        join_kernel,
        [shaped(clip.shape, BF16), shaped((8, 128), F32)],
        [keep, core_got, block_got, cross_got],
        fetch=(1, 2, 3),
    )

    count = frames * tms * rows * heights * width
    (grad_filter,) = call(
        functools.partial(finish_kernel, 1.0 / float(count) ** 0.5),
        [shaped((27, cin // tms, chans // heights), F32)],
        [summed, mark],
        fetch=(0,),
        idle=(1,),
    )
    grad_filter = grad_filter.reshape(3, 3, 3, cin // tms, chans // heights)
    return (grad_clip, grad_filter)


def solution(mesh):
    in_specs = (
        P("tm", "height", None, None),
        P(),
        P(None, None, None, None, "height"),
        P("tm", "height", None, None),
    )
    out_specs = (P("tm", "height", None, None), P(None, None, None, "tm", "height"))
    return jax.shard_map(body, mesh=mesh, in_specs=in_specs, out_specs=out_specs, check_vma=False)
```

```python
import functools

import jax
import jax.numpy as jnp
from jax import lax
from jax.experimental import pallas as pl
from jax.experimental.pallas import tpu as pltpu
from jax.sharding import PartitionSpec as P

F32, BF16 = jnp.float32, jnp.bfloat16
CORES = 2
OWN = 64
FRAMES = 4
ROWS, SPAN = 8, 10
HIGH, HALF_HIGH, HALF = ROWS + 4, ROWS // 2 + 2, SPAN // 2
MIDDLE = (1, 2, 3, 0)

LONG = {0: ((2, 0),), 1: ((0, 0), (1, 1))}
WIDE = {0: ((1, 0), (2, 1)), 1: ((0, 1),)}


def shift_classes():
    classes = []
    for t in (1, 0):
        for h in (1, 0):
            for w in (0, 1):
                taps = tuple(
                    ((a, b, c), (fp, ip, jp))
                    for a, fp in LONG[t]
                    for b, ip in LONG[h]
                    for c, jp in WIDE[w]
                )
                classes.append(((t, h, w), taps))
    return classes


CLASSES = shift_classes()
TAP_ORDER = [tap for _, taps in CLASSES for tap, _ in taps]


def mm(lhs, rhs):
    return jnp.dot(lhs, rhs, preferred_element_type=F32)


def one_hot(rows, cols, column_of):
    row = lax.broadcasted_iota(jnp.int32, (rows, cols), 0)
    col = lax.broadcasted_iota(jnp.int32, (rows, cols), 1)
    return jnp.where(column_of(row) == col, 1.0, 0.0).astype(BF16)


def call(kernel, out, args, scratch=(), fetch=(), idle=(), alias=None, flops=0, limit=16):
    n_in, n_out, n_scratch = len(args), len(out), len(scratch)

    def run(*refs):
        ins, outs = list(refs[:n_in]), refs[n_in : n_in + n_out]
        rest = refs[n_in + n_out :]
        if fetch:
            landing, sems = rest[n_scratch:-1], rest[-1]
            copies = [
                pltpu.make_async_copy(ins[i], landing[k], sems.at[k]) for k, i in enumerate(fetch)
            ]
            for copy in copies:
                copy.start()
            for copy in copies:
                copy.wait()
            for k, i in enumerate(fetch):
                ins[i] = landing[k]
        kernel(*ins, *outs, *rest[:n_scratch])

    spec = pl.BlockSpec(memory_space=pltpu.VMEM)
    far = pl.BlockSpec(memory_space=pl.ANY)
    moved = sum(x.size * x.dtype.itemsize for x in list(args) + list(out))
    extra = [pltpu.VMEM(args[i].shape, args[i].dtype) for i in fetch]
    if fetch:
        extra.append(pltpu.SemaphoreType.DMA((len(fetch),)))
    return pl.pallas_call(
        run,
        out_shape=tuple(out),
        in_specs=[far if i in fetch or i in idle else spec for i in range(n_in)],
        out_specs=tuple([far if i in (alias or {}).values() else spec for i in range(n_out)]),
        input_output_aliases=dict(alias or {}),
        scratch_shapes=list(scratch) + extra,
        compiler_params=pltpu.CompilerParams(vmem_limit_bytes=limit * 1024 * 1024),
        cost_estimate=pl.CostEstimate(flops=flops, bytes_accessed=moved, transcendentals=0),
    )(*args)


def shaped(shape, dtype):
    return jax.ShapeDtypeStruct(shape, dtype)


def own_channel(place, x, core):
    return (2 * (place // 8) + core) * 16 + 8 * x + place % 8


def filter_pieces_kernel(second, out):
    taps, depth, chans = second.shape
    x = lax.axis_index("tm") % 2
    row = lax.broadcasted_iota(jnp.int32, (chans, 2 * OWN), 0)
    col = lax.broadcasted_iota(jnp.int32, (chans, 2 * OWN), 1)
    order = jnp.where(own_channel(col % OWN, x, col // OWN) == row, 1.0, 0.0).astype(BF16)
    moved = mm(second[...].reshape(taps * depth, chans), order).astype(BF16)
    moved = moved.reshape(taps, depth, 2 * OWN)
    for place in range(0, len(TAP_ORDER), 2):
        pair = TAP_ORDER[place : place + 2]
        for core in range(CORES):
            lanes = slice(core * OWN, (core + 1) * OWN)
            piece = jnp.concatenate([moved[a * 9 + b * 3 + c, :, lanes] for a, b, c in pair], 1)
            for p in range(core, out.shape[0], CORES):
                out[p, :, place * OWN : place * OWN + piece.shape[1]] = piece


def band_kernel(first, band):
    chans = first.shape[1]
    x, core = lax.axis_index("tm") % 2, lax.axis_index("height") % CORES
    row = lax.broadcasted_iota(jnp.int32, (chans, 2 * OWN), 0)
    col = lax.broadcasted_iota(jnp.int32, (chans, 2 * OWN), 1)
    pick = jnp.where(own_channel(col % OWN, x, core) == row, 1.0, 0.0).astype(BF16)
    twice = mm(first[...], pick)
    lane = lax.broadcasted_iota(jnp.int32, (128, 2 * OWN), 1)
    for ab in range(9):
        for s in range(4):
            left = twice[(ab * 3 + s) * 128 : (ab * 3 + s + 1) * 128] if s < 3 else 0.0
            right = twice[(ab * 3 + s - 1) * 128 : (ab * 3 + s) * 128] if s > 0 else 0.0
            both = jnp.where(lane < OWN, left, right)
            band[ab, s * 128 : (s + 1) * 128] = both.astype(BF16)


def turned_kernel(first, _, turned):
    chans = first.shape[1]
    x, core = lax.axis_index("tm") % 2, lax.axis_index("height") % CORES
    row = lax.broadcasted_iota(jnp.int32, (OWN, chans), 0)
    col = lax.broadcasted_iota(jnp.int32, (OWN, chans), 1)
    pick = jnp.where(own_channel(row, x, core) == col, 1.0, 0.0).astype(BF16)
    flat = lax.dot_general(
        pick, first[...], (((1,), (1,)), ((), ())), preferred_element_type=F32
    ).astype(BF16)
    for ab in range(9):
        for slot, s in enumerate(MIDDLE):
            for jp in range(2):
                c = jp + 2 - s
                if 0 <= c <= 2:
                    piece = flat[:, (ab * 3 + c) * 128 : (ab * 3 + c + 1) * 128]
                else:
                    piece = jnp.zeros((OWN, 128), BF16)
                turned[ab, slot * OWN : (slot + 1) * OWN, jp * 128 : (jp + 1) * 128] = piece


def stack_kernel(clip, up, here, edge):
    at_top = lax.axis_index("height") % CORES == 0
    for f in range(2):
        here[4 * f : 4 * f + 4] = clip[f]
        edge[2 * f : 2 * f + 2] = jnp.where(at_top, clip[f, :2], clip[f, 2:])
    for half in range(2):
        subs = slice(16 * half, 16 * half + 16)
        src = up[0, :, :, 128 * half : 128 * half + 128]
        here[8:10, subs] = src
        edge[4, subs] = jnp.where(at_top, src[0], src[1])


def append_kernel(here, edge, _, out, __, sems):
    copies = [
        pltpu.make_async_copy(here, out.at[:10], sems.at[0]),
        pltpu.make_async_copy(edge, out.at[10:], sems.at[1]),
    ]
    for copy in copies:
        copy.start()
    for copy in copies:
        copy.wait()


def pack_kernel(here, pair, odd, even, packed):
    first = lax.axis_index("tm") % 2 == 0
    one = jnp.where(first, here[...], pair[...])
    two = jnp.where(first, pair[...], here[...])
    past = jnp.where(first, odd[...], even[...])
    after = jnp.where(first, even[...], odd[...])
    for k, src in enumerate((past, one, two)):
        packed[8 * k : 8 * k + 8] = src[:8]
        packed[30 + 4 * k : 34 + 4 * k] = src[10:14]
    for t, src in enumerate((one, two, after)):
        packed[24 + 2 * t : 26 + 2 * t] = src[8:10]
        packed[42 + t] = src[14]


def preact_kernel(own, other, filters, wide, ups, pre, band, ext):
    member = lax.axis_index("height") % CORES
    even = member == 0
    above = jnp.where(even, own[30:45], other[30:45])
    below = jnp.where(even, other[30:45], own[30:45])
    for f in range(6):
        base = f * HIGH
        band[pl.ds(base + 2 + 4 * member, 4)] = own[4 * f : 4 * f + 4]
        band[pl.ds(base + 6 - 4 * member, 4)] = other[4 * f : 4 * f + 4]
        band[base : base + 2] = above[2 * f : 2 * f + 2]
        band[base + ROWS + 2 : base + ROWS + 4] = below[2 * f : 2 * f + 2]
    for t in range(3):
        base, unit = t * HALF_HIGH, 24 + 2 * t
        for half in range(2):
            lanes = slice(128 * half, 128 * half + 128)
            subs = slice(16 * half, 16 * half + 16)
            ext[pl.ds(base + 1 + 2 * member, 2), :, lanes] = own[unit : unit + 2, subs]
            ext[pl.ds(base + 3 - 2 * member, 2), :, lanes] = other[unit : unit + 2, subs]
            ext[base, :, lanes] = above[12 + t, subs]
            ext[base + HALF_HIGH - 1, :, lanes] = below[12 + t, subs]
    units = ext.shape[0]
    flat = ext[...].reshape(units * 16, 256)
    shift = one_hot(units * 16, units * 16, lambda r: jnp.where(r % 16 == 15, -1, r + 1))
    ups[0] = flat.reshape(units, 16, 256)
    ups[1] = mm(shift, flat).astype(BF16).reshape(units, 16, 256)

    def column(r):
        s, unit, w = r // 128, (r // 16) % 8, 2 * (r % 16) + r // 128 - 1
        return jnp.where((w >= 0) & (w < 32), unit * 32 + w, -1)

    matrix = one_hot(512, 256, column)
    for g in range(band.shape[0] // 8):
        moved = mm(matrix, band[8 * g : 8 * g + 8].reshape(256, 128)).astype(BF16)
        for s in range(4):
            piece = moved[128 * s : 128 * s + 128].reshape(8, 16, 128)
            wide[8 * g : 8 * g + 8, :, s * 128 : (s + 1) * 128] = piece
    total = jnp.zeros((FRAMES * SPAN * 16, 2 * OWN), F32)
    for a in range(3):
        for b in range(3):
            tops = [(a + f) * HIGH + b for f in range(FRAMES)]
            win = jnp.concatenate([wide[x : x + SPAN] for x in tops], 0)
            total = total + mm(win.reshape(FRAMES * SPAN * 16, 512), filters[a * 3 + b])
    total = total.reshape(FRAMES, SPAN, 16, 2 * OWN)
    for f in range(FRAMES):
        for r in range(SPAN):
            pre[f % 2, r % 2, f // 2, r // 2] = total[f, r]


def gradient_kernel(second, ups, pre, wide, grad, parts):
    group = lax.axis_index("height") // CORES
    first_band = group == 0
    last_band = group == lax.axis_size("height") // CORES - 1
    even, odd = {}, {}
    offset = 0
    for (t, h, w), taps in CLASSES:
        tops = [(t + q) * HALF_HIGH + h for q in range(2)]
        lhs = jnp.concatenate([ups[w, x : x + HALF] for x in tops], 0).reshape(32 * HALF, 256)
        prod = mm(lhs, second[:, offset : offset + len(taps) * OWN])
        offset += len(taps) * OWN
        total, step = (odd, 1) if w else (even, 2)
        for k in range(0, len(taps), step):
            key = taps[k][1][:2]
            piece = prod[:, k * OWN : (k + step) * OWN]
            total[key] = total[key] + piece if key in total else piece
    blank = jnp.zeros((32 * HALF, OWN), F32)
    for (fp, ip), act in even.items():
        act = act + jnp.concatenate([blank, odd[fp, ip]], 1)
        x = pre[fp, ip].reshape(32 * HALF, 2 * OWN)
        sig = jax.nn.sigmoid(x)
        g = (act * sig * (1.0 + x * (1.0 - sig))).reshape(2, HALF, 16, 2 * OWN)
        for q in range(2):
            for p in range(HALF):
                piece, r = g[q, p], 2 * p + ip
                if r == 0:
                    piece = jnp.where(first_band, 0.0, piece)
                if r == SPAN - 1:
                    piece = jnp.where(last_band, 0.0, piece)
                grad[2 * q + fp, r] = piece.astype(BF16)
    turned = grad[:, 1 : 1 + ROWS].reshape(FRAMES * ROWS * 16, 2 * OWN).T
    strips = []
    for a in range(3):
        for b in range(3):
            tops = [(a + f) * HIGH + 1 + b for f in range(FRAMES)]
            win = jnp.concatenate([wide[x : x + ROWS] for x in tops], 0)
            prod = mm(turned, win.reshape(FRAMES * ROWS * 16, 512))
            for c in range(3):
                piece = prod[:OWN, 128 * c : 128 * c + 128]
                piece = piece + prod[OWN:, 128 * c + 128 : 128 * c + 256]
                strips.append(piece.astype(BF16))
    strips.append(jnp.zeros_like(strips[0]))
    row = lax.broadcasted_iota(jnp.int32, (256, 256), 0)
    col = lax.broadcasted_iota(jnp.int32, (256, 256), 1)
    x, tap, z, e = col // 128, (col // 64) % 2, (col // 4) % 16, col % 4
    order = jnp.where(tap * 128 + 8 * z + 4 * x + e == row, 1.0, 0.0).astype(BF16)
    blocks = OWN // 8
    for k in range(7):
        pairs = [jnp.concatenate(strips[i : i + 2], 1) for i in (4 * k, 4 * k + 2)]
        pairs = [mm(pair, order).reshape(blocks, 8, 256) for pair in pairs]
        both = jnp.concatenate(pairs, 1).astype(BF16)
        for x in range(2):
            parts[x * blocks : (x + 1) * blocks, k] = both[:, :, 128 * x : 128 * x + 128]


def sum_turn_kernel(parts, _, out):
    blank = jnp.zeros((16, 128), F32)
    blocks = parts.shape[0] // 2
    halves = []
    for x in range(2):
        total = parts[x * blocks].astype(F32)
        for i in range(1, blocks):
            total = total + parts[x * blocks + i].astype(F32)
        halves += [total.reshape(112, 128), blank]
    flat = jnp.concatenate(halves, 0).T
    for i in range(16):
        z = (i + 8) % 16
        rows = [(tap * 64 + z * 4, x) for x in range(2) for tap in range(2)]
        block = [flat[r : r + 4, 128 * x : 128 * x + 128] for r, x in rows]
        out[i] = jnp.concatenate(block, 0).astype(BF16)


def finish_kernel(scale, parts, out, mark):
    total = parts[0].astype(F32)
    for i in range(1, parts.shape[0]):
        total = total + parts[i].astype(F32)
    total = total * scale
    for k in range(27):
        lanes = slice(8 * (k // 2), 8 * (k // 2) + 8)
        rows = [8 * x + 4 * (k % 2) for x in range(2)]
        out[k] = jnp.concatenate([total[r : r + 4, lanes] for r in rows], 1)
    mark[...] = jnp.zeros_like(mark)


def clip_kernel(grad, following, filters, keep, send, wide):
    lane = lax.broadcasted_iota(jnp.int32, (192, 2 * OWN), 1)
    up = one_hot(192, 192, lambda r: jnp.where(r % 16 == 15, -1, r + 1))
    down = one_hot(192, 192, lambda r: jnp.where(r % 16 == 0, -1, r - 1))
    for f in range(FRAMES + 2):
        src = grad[f] if f < FRAMES else following[f - FRAMES]
        wide[f * SPAN : (f + 1) * SPAN, :, : 2 * OWN] = src
    for g in range(0, (FRAMES + 2) * SPAN, 12):
        block = wide[g : g + 12, :, : 2 * OWN].reshape(192, 2 * OWN)
        moved = jnp.where(lane < OWN, mm(up, block), mm(down, block)).astype(BF16)
        wide[g : g + 12, :, 2 * OWN :] = moved.reshape(12, 16, 2 * OWN)
    total = jnp.zeros((FRAMES * ROWS * 16, 256), F32)
    for a in range(3):
        for b in range(3):
            tops = [(f + 2 - a) * SPAN + 2 - b for f in range(FRAMES)]
            win = jnp.concatenate([wide[x : x + ROWS] for x in tops], 0)
            total = total + mm(win.reshape(FRAMES * ROWS * 16, 4 * OWN), filters[a * 3 + b])
    total = total.reshape(FRAMES, ROWS, 16, 256)
    low, high = total[:, :4], total[:, 4:]
    even = lax.axis_index("height") % CORES == 0
    keep[...] = jnp.where(even, low, high)
    send[...] = jnp.where(even, high, low)


def halve_kernel(kept, got, keep, send):
    total = kept[...] + got[...]
    first = lax.axis_index("tm") % 2 == 0
    low, high = total[:2], total[2:]
    keep[...] = jnp.where(first, low, high)
    send[...] = jnp.where(first, high, low).astype(BF16)


def join_kernel(kept, got, _, out):
    total = (kept[...] + got[...].astype(F32)).astype(BF16).reshape(128, 256)
    low = one_hot(256, 128, lambda r: jnp.where(r % 2 == 0, (r // 32) * 16 + (r % 32) // 2, -1))
    high = one_hot(256, 128, lambda r: jnp.where(r % 2 == 1, (r // 32) * 16 + (r % 32) // 2, -1))
    moved = mm(low, total[:, :128]) + mm(high, total[:, 128:])
    out[...] = moved.astype(BF16).reshape(out.shape)


def inside(pairs, count):
    return [(i, k) for i, k in pairs if 0 <= k < count]


def body(clip, first_filter, second_filter, upstream):
    frames, rows, width, cin = clip.shape
    chans = first_filter.shape[4]
    tms, heights = lax.axis_size("tm"), lax.axis_size("height")
    lines = tms // 2
    siblings = [(i, i ^ 1) for i in range(heights)]
    blocks = [(t, t ^ 1) for t in range(tms)]

    here, edge = call(
        stack_kernel,
        [shaped((10, 32, 128), BF16), shaped((5, 32, 128), BF16)],
        [clip, upstream],
        fetch=(0, 1),
        limit=60,
    )
    near_pairs = inside([(i, i + 1 if i % 2 else i - 1) for i in range(heights)], heights)
    edge = lax.ppermute(edge, "height", near_pairs)

    second = jnp.swapaxes(second_filter, 3, 4).reshape(27, chans // heights, chans)
    (pieces,) = call(
        filter_pieces_kernel,
        [shaped((heights, chans // heights, 27 * OWN), BF16)],
        [second],
        fetch=(0,),
        flops=2 * 27 * 16 * 256 * 128,
    )
    here, pieces = call(
        append_kernel,
        [shaped((15, 32, 128), BF16), shaped(pieces.shape, BF16)],
        [here, edge, pieces],
        scratch=[pltpu.SemaphoreType.DMA((2,))],
        idle=(0, 1, 2),
        alias={2: 1},
    )
    second = lax.all_to_all(pieces, "height", 0, 0).reshape(chans, 27 * OWN)

    pair = lax.ppermute(here, "tm", blocks)
    odd_pairs = inside([(t, t + 1 if t % 2 else t - 1) for t in range(tms)], tms)
    even_pairs = inside([(t, t + 2 if t % 2 else t - 2) for t in range(tms)], tms)
    odd = lax.ppermute(here, "tm", odd_pairs)
    even = lax.ppermute(here, "tm", even_pairs)

    first = first_filter.reshape(27 * cin, chans)
    (band,) = call(
        band_kernel,
        [shaped((9, 512, 2 * OWN), BF16)],
        [first],
        fetch=(0,),
        flops=2 * 27 * 128 * 256 * 128,
    )

    (packed,) = call(
        pack_kernel, [shaped((45, 32, 128), BF16)], [here, pair, odd, even], fetch=(1, 2, 3)
    )
    other = lax.ppermute(packed, "height", siblings)

    units, up_units = 6 * HIGH, 3 * HALF_HIGH
    wide, ups, pre = call(
        preact_kernel,
        [
            shaped((units, 16, 512), BF16),
            shaped((2, up_units, 16, 256), BF16),
            shaped((2, 2, 2, HALF, 16, 2 * OWN), F32),
        ],
        [packed, other, band],
        scratch=[pltpu.VMEM((units, 32, 128), BF16), pltpu.VMEM((up_units, 16, 256), BF16)],
        fetch=(0, 1),
        flops=2 * 640 * 9 * 512 * 128,
    )
    grad_pre, parts = call(
        gradient_kernel,
        [shaped((FRAMES, SPAN, 16, 2 * OWN), BF16), shaped((heights, 7, 16, cin), BF16)],
        [second, ups, pre, wide],
        fetch=(0,),
        flops=2 * 512 * 9 * 512 * 128,
    )

    planes = [
        [(2 * z + x) * heights + CORES * g + core for x in range(2) for g in range(heights // 2)]
        for z in range(lines)
        for core in range(CORES)
    ]
    parts = lax.all_to_all(parts, ("tm", "height"), 0, 0, axis_index_groups=planes)
    back = inside([(t, t - 2) for t in range(tms)], tms)
    following = lax.ppermute(grad_pre[:2], "tm", back)
    (turned,) = call(
        turned_kernel,
        [shaped((9, 4 * OWN, 2 * cin), BF16)],
        [first, grad_pre],
        fetch=(0,),
        idle=(1,),
        flops=2 * 27 * 128 * 256 * 64,
    )
    keep, send = call(
        clip_kernel,
        [shaped((FRAMES, rows, 16, 2 * cin), F32)] * 2,
        [grad_pre, following, turned],
        scratch=[pltpu.VMEM(((FRAMES + 2) * SPAN, 16, 4 * OWN), BF16)],
        fetch=(1,),
        flops=2 * 512 * 9 * 256 * 256,
    )

    (sums,) = call(
        sum_turn_kernel,
        [shaped((lines, 16, 128), BF16)],
        [parts, send],
        fetch=(0,),
        idle=(1,),
    )
    columns = [[2 * ((i + 8) % lines) + x for i in range(lines)] for x in range(2)]
    summed = lax.all_to_all(sums, "tm", 0, 0, axis_index_groups=columns)
    got = lax.ppermute(send, "height", siblings)
    keep, send = call(
        halve_kernel,
        [shaped((2, rows, 16, 2 * cin), F32), shaped((2, rows, 16, 2 * cin), BF16)],
        [keep, got],
        fetch=(1,),
    )
    got = lax.ppermute(send, "tm", blocks)
    count = frames * tms * rows * heights * width
    grad_filter, mark = call(
        functools.partial(finish_kernel, 1.0 / float(count) ** 0.5),
        [shaped((27, cin // tms, chans // heights), F32), shaped((8, 128), F32)],
        [summed],
        fetch=(0,),
    )
    (grad_clip,) = call(
        join_kernel,
        [shaped(clip.shape, BF16)],
        [keep, got, mark],
        fetch=(1,),
        idle=(2,),
    )
    grad_filter = grad_filter.reshape(3, 3, 3, cin // tms, chans // heights)
    return (grad_clip, grad_filter)


def solution(mesh):
    in_specs = (
        P("tm", "height", None, None),
        P(),
        P(None, None, None, None, "height"),
        P("tm", "height", None, None),
    )
    out_specs = (P("tm", "height", None, None), P(None, None, None, "tm", "height"))
    return jax.shard_map(body, mesh=mesh, in_specs=in_specs, out_specs=out_specs, check_vma=False)
```

```python
import functools

import jax
import jax.numpy as jnp
from jax import lax
from jax.experimental import pallas as pl
from jax.experimental.pallas import tpu as pltpu
from jax.sharding import PartitionSpec as P

F32, BF16 = jnp.float32, jnp.bfloat16
CORES = 2
OWN = 64
FRAMES = 4
ROWS, SPAN = 8, 10
HIGH, HALF_HIGH, HALF = ROWS + 4, ROWS // 2 + 2, SPAN // 2
MIDDLE = (1, 2, 3, 0)

LONG = {0: ((2, 0),), 1: ((0, 0), (1, 1))}
WIDE = {0: ((1, 0), (2, 1)), 1: ((0, 1),)}


def shift_classes():
    classes = []
    for t in (1, 0):
        for h in (1, 0):
            for w in (0, 1):
                taps = tuple(
                    ((a, b, c), (fp, ip, jp))
                    for a, fp in LONG[t]
                    for b, ip in LONG[h]
                    for c, jp in WIDE[w]
                )
                classes.append(((t, h, w), taps))
    return classes


CLASSES = shift_classes()
TAP_ORDER = [tap for _, taps in CLASSES for tap, _ in taps]


def mm(lhs, rhs):
    return jnp.dot(lhs, rhs, preferred_element_type=F32)


def one_hot(rows, cols, column_of):
    row = lax.broadcasted_iota(jnp.int32, (rows, cols), 0)
    col = lax.broadcasted_iota(jnp.int32, (rows, cols), 1)
    return jnp.where(column_of(row) == col, 1.0, 0.0).astype(BF16)


def call(kernel, out, args, scratch=(), fetch=(), idle=(), alias=None, flops=0, limit=16):
    n_in, n_out, n_scratch = len(args), len(out), len(scratch)

    def run(*refs):
        ins, outs = list(refs[:n_in]), refs[n_in : n_in + n_out]
        rest = refs[n_in + n_out :]
        if fetch:
            landing, sems = rest[n_scratch:-1], rest[-1]
            copies = [
                pltpu.make_async_copy(ins[i], landing[k], sems.at[k]) for k, i in enumerate(fetch)
            ]
            for copy in copies:
                copy.start()
            for copy in copies:
                copy.wait()
            for k, i in enumerate(fetch):
                ins[i] = landing[k]
        kernel(*ins, *outs, *rest[:n_scratch])

    spec = pl.BlockSpec(memory_space=pltpu.VMEM)
    far = pl.BlockSpec(memory_space=pl.ANY)
    moved = sum(x.size * x.dtype.itemsize for x in list(args) + list(out))
    extra = [pltpu.VMEM(args[i].shape, args[i].dtype) for i in fetch]
    if fetch:
        extra.append(pltpu.SemaphoreType.DMA((len(fetch),)))
    return pl.pallas_call(
        run,
        out_shape=tuple(out),
        in_specs=[far if i in fetch or i in idle else spec for i in range(n_in)],
        out_specs=tuple([far if i in (alias or {}).values() else spec for i in range(n_out)]),
        input_output_aliases=dict(alias or {}),
        scratch_shapes=list(scratch) + extra,
        compiler_params=pltpu.CompilerParams(vmem_limit_bytes=limit * 1024 * 1024),
        cost_estimate=pl.CostEstimate(flops=flops, bytes_accessed=moved, transcendentals=0),
    )(*args)


def shaped(shape, dtype):
    return jax.ShapeDtypeStruct(shape, dtype)


def own_channel(place, x, core):
    return (2 * (place // 8) + core) * 16 + 8 * x + place % 8


def filter_pieces_kernel(second, out):
    taps, depth, chans = second.shape
    x = lax.axis_index("tm") % 2
    row = lax.broadcasted_iota(jnp.int32, (chans, 2 * OWN), 0)
    col = lax.broadcasted_iota(jnp.int32, (chans, 2 * OWN), 1)
    order = jnp.where(own_channel(col % OWN, x, col // OWN) == row, 1.0, 0.0).astype(BF16)
    moved = mm(second[...].reshape(taps * depth, chans), order).astype(BF16)
    moved = moved.reshape(taps, depth, 2 * OWN)
    for place in range(0, len(TAP_ORDER), 2):
        pair = TAP_ORDER[place : place + 2]
        for core in range(CORES):
            lanes = slice(core * OWN, (core + 1) * OWN)
            piece = jnp.concatenate([moved[a * 9 + b * 3 + c, :, lanes] for a, b, c in pair], 1)
            for p in range(core, out.shape[0], CORES):
                out[p, :, place * OWN : place * OWN + piece.shape[1]] = piece


def band_kernel(first, band):
    chans = first.shape[1]
    x, core = lax.axis_index("tm") % 2, lax.axis_index("height") % CORES
    row = lax.broadcasted_iota(jnp.int32, (chans, 2 * OWN), 0)
    col = lax.broadcasted_iota(jnp.int32, (chans, 2 * OWN), 1)
    pick = jnp.where(own_channel(col % OWN, x, core) == row, 1.0, 0.0).astype(BF16)
    twice = mm(first[...], pick)
    lane = lax.broadcasted_iota(jnp.int32, (128, 2 * OWN), 1)
    for ab in range(9):
        for s in range(4):
            left = twice[(ab * 3 + s) * 128 : (ab * 3 + s + 1) * 128] if s < 3 else 0.0
            right = twice[(ab * 3 + s - 1) * 128 : (ab * 3 + s) * 128] if s > 0 else 0.0
            both = jnp.where(lane < OWN, left, right)
            band[ab, s * 128 : (s + 1) * 128] = both.astype(BF16)


def turned_kernel(first, _, turned):
    chans = first.shape[1]
    x, core = lax.axis_index("tm") % 2, lax.axis_index("height") % CORES
    row = lax.broadcasted_iota(jnp.int32, (OWN, chans), 0)
    col = lax.broadcasted_iota(jnp.int32, (OWN, chans), 1)
    pick = jnp.where(own_channel(row, x, core) == col, 1.0, 0.0).astype(BF16)
    flat = lax.dot_general(
        pick, first[...], (((1,), (1,)), ((), ())), preferred_element_type=F32
    ).astype(BF16)
    for ab in range(9):
        for slot, s in enumerate(MIDDLE):
            for jp in range(2):
                c = jp + 2 - s
                if 0 <= c <= 2:
                    piece = flat[:, (ab * 3 + c) * 128 : (ab * 3 + c + 1) * 128]
                else:
                    piece = jnp.zeros((OWN, 128), BF16)
                turned[ab, slot * OWN : (slot + 1) * OWN, jp * 128 : (jp + 1) * 128] = piece


def stack_kernel(clip, up, here, edge):
    at_top = lax.axis_index("height") % CORES == 0
    for f in range(2):
        here[4 * f : 4 * f + 4] = clip[f]
        edge[2 * f : 2 * f + 2] = jnp.where(at_top, clip[f, :2], clip[f, 2:])
    for half in range(2):
        subs = slice(16 * half, 16 * half + 16)
        src = up[0, :, :, 128 * half : 128 * half + 128]
        here[8:10, subs] = src
        edge[4, subs] = jnp.where(at_top, src[0], src[1])


def append_kernel(here, edge, _, out, __, sems):
    copies = [
        pltpu.make_async_copy(here, out.at[:10], sems.at[0]),
        pltpu.make_async_copy(edge, out.at[10:], sems.at[1]),
    ]
    for copy in copies:
        copy.start()
    for copy in copies:
        copy.wait()


def choose_kernel(here, pair, _, forward, backward, __):
    first = lax.axis_index("tm") % 2 == 0
    forward[:8] = jnp.where(first, pair[:8], here[:8])
    forward[8:12] = jnp.where(first, pair[10:14], here[10:14])
    backward[:2] = jnp.where(first, here[8:10], pair[8:10])
    backward[2] = jnp.where(first, here[14], pair[14])


def pack_kernel(here, pair, before, after, packed):
    first = lax.axis_index("tm") % 2 == 0
    one = jnp.where(first, here[...], pair[...])
    two = jnp.where(first, pair[...], here[...])
    packed[:8] = before[:8]
    packed[30:34] = before[8:12]
    for k, src in ((1, one), (2, two)):
        packed[8 * k : 8 * k + 8] = src[:8]
        packed[30 + 4 * k : 34 + 4 * k] = src[10:14]
    for t, src in enumerate((one[8:10], two[8:10], after[:2])):
        packed[24 + 2 * t : 26 + 2 * t] = src
    for t, src in enumerate((one[14], two[14], after[2])):
        packed[42 + t] = src


def preact_kernel(own, other, filters, wide, ups, pre, band, ext):
    member = lax.axis_index("height") % CORES
    even = member == 0
    above = jnp.where(even, own[30:45], other[30:45])
    below = jnp.where(even, other[30:45], own[30:45])
    for f in range(6):
        base = f * HIGH
        band[pl.ds(base + 2 + 4 * member, 4)] = own[4 * f : 4 * f + 4]
        band[pl.ds(base + 6 - 4 * member, 4)] = other[4 * f : 4 * f + 4]
        band[base : base + 2] = above[2 * f : 2 * f + 2]
        band[base + ROWS + 2 : base + ROWS + 4] = below[2 * f : 2 * f + 2]
    for t in range(3):
        base, unit = t * HALF_HIGH, 24 + 2 * t
        for half in range(2):
            lanes = slice(128 * half, 128 * half + 128)
            subs = slice(16 * half, 16 * half + 16)
            ext[pl.ds(base + 1 + 2 * member, 2), :, lanes] = own[unit : unit + 2, subs]
            ext[pl.ds(base + 3 - 2 * member, 2), :, lanes] = other[unit : unit + 2, subs]
            ext[base, :, lanes] = above[12 + t, subs]
            ext[base + HALF_HIGH - 1, :, lanes] = below[12 + t, subs]
    units = ext.shape[0]
    flat = ext[...].reshape(units * 16, 256)
    shift = one_hot(units * 16, units * 16, lambda r: jnp.where(r % 16 == 15, -1, r + 1))
    ups[0] = flat.reshape(units, 16, 256)
    ups[1] = mm(shift, flat).astype(BF16).reshape(units, 16, 256)

    def column(r):
        s, unit, w = r // 128, (r // 16) % 8, 2 * (r % 16) + r // 128 - 1
        return jnp.where((w >= 0) & (w < 32), unit * 32 + w, -1)

    matrix = one_hot(512, 256, column)
    for g in range(band.shape[0] // 8):
        moved = mm(matrix, band[8 * g : 8 * g + 8].reshape(256, 128)).astype(BF16)
        for s in range(4):
            piece = moved[128 * s : 128 * s + 128].reshape(8, 16, 128)
            wide[8 * g : 8 * g + 8, :, s * 128 : (s + 1) * 128] = piece
    total = jnp.zeros((FRAMES * SPAN * 16, 2 * OWN), F32)
    for a in range(3):
        for b in range(3):
            tops = [(a + f) * HIGH + b for f in range(FRAMES)]
            win = jnp.concatenate([wide[x : x + SPAN] for x in tops], 0)
            total = total + mm(win.reshape(FRAMES * SPAN * 16, 512), filters[a * 3 + b])
    total = total.reshape(FRAMES, SPAN, 16, 2 * OWN)
    for f in range(FRAMES):
        for r in range(SPAN):
            pre[f % 2, r % 2, f // 2, r // 2] = total[f, r]


def gradient_kernel(second, ups, pre, wide, grad, parts):
    group = lax.axis_index("height") // CORES
    first_band = group == 0
    last_band = group == lax.axis_size("height") // CORES - 1
    even, odd = {}, {}
    offset = 0
    for (t, h, w), taps in CLASSES:
        tops = [(t + q) * HALF_HIGH + h for q in range(2)]
        lhs = jnp.concatenate([ups[w, x : x + HALF] for x in tops], 0).reshape(32 * HALF, 256)
        prod = mm(lhs, second[:, offset : offset + len(taps) * OWN])
        offset += len(taps) * OWN
        total, step = (odd, 1) if w else (even, 2)
        for k in range(0, len(taps), step):
            key = taps[k][1][:2]
            piece = prod[:, k * OWN : (k + step) * OWN]
            total[key] = total[key] + piece if key in total else piece
    blank = jnp.zeros((32 * HALF, OWN), F32)
    for (fp, ip), act in even.items():
        act = act + jnp.concatenate([blank, odd[fp, ip]], 1)
        x = pre[fp, ip].reshape(32 * HALF, 2 * OWN)
        sig = jax.nn.sigmoid(x)
        g = (act * sig * (1.0 + x * (1.0 - sig))).reshape(2, HALF, 16, 2 * OWN)
        for q in range(2):
            for p in range(HALF):
                piece, r = g[q, p], 2 * p + ip
                if r == 0:
                    piece = jnp.where(first_band, 0.0, piece)
                if r == SPAN - 1:
                    piece = jnp.where(last_band, 0.0, piece)
                grad[2 * q + fp, r] = piece.astype(BF16)
    turned = grad[:, 1 : 1 + ROWS].reshape(FRAMES * ROWS * 16, 2 * OWN).T
    strips = []
    for a in range(3):
        for b in range(3):
            tops = [(a + f) * HIGH + 1 + b for f in range(FRAMES)]
            win = jnp.concatenate([wide[x : x + ROWS] for x in tops], 0)
            prod = mm(turned, win.reshape(FRAMES * ROWS * 16, 512))
            for c in range(3):
                piece = prod[:OWN, 128 * c : 128 * c + 128]
                piece = piece + prod[OWN:, 128 * c + 128 : 128 * c + 256]
                strips.append(piece.astype(BF16))
    strips.append(jnp.zeros_like(strips[0]))
    row = lax.broadcasted_iota(jnp.int32, (256, 256), 0)
    col = lax.broadcasted_iota(jnp.int32, (256, 256), 1)
    x, tap, z, e = col // 128, (col // 64) % 2, (col // 4) % 16, col % 4
    order = jnp.where(tap * 128 + 8 * z + 4 * x + e == row, 1.0, 0.0).astype(BF16)
    blocks = OWN // 8
    for k in range(7):
        pairs = [jnp.concatenate(strips[i : i + 2], 1) for i in (4 * k, 4 * k + 2)]
        pairs = [mm(pair, order).reshape(blocks, 8, 256) for pair in pairs]
        both = jnp.concatenate(pairs, 1).astype(BF16)
        for x in range(2):
            parts[x * blocks : (x + 1) * blocks, k] = both[:, :, 128 * x : 128 * x + 128]


def middle_kernel(own, other, filters, second, grad, parts, wide, ups, pre, band, ext):
    preact_kernel(own, other, filters, wide, ups, pre, band, ext)
    gradient_kernel(second, ups, pre, wide, grad, parts)


def sum_turn_kernel(parts, _, out):
    blank = jnp.zeros((16, 128), F32)
    blocks = parts.shape[0] // 2
    halves = []
    for x in range(2):
        total = parts[x * blocks].astype(F32)
        for i in range(1, blocks):
            total = total + parts[x * blocks + i].astype(F32)
        halves += [total.reshape(112, 128), blank]
    flat = jnp.concatenate(halves, 0).T
    for i in range(16):
        z = (i + 8) % 16
        rows = [(tap * 64 + z * 4, x) for x in range(2) for tap in range(2)]
        block = [flat[r : r + 4, 128 * x : 128 * x + 128] for r, x in rows]
        out[i] = jnp.concatenate(block, 0).astype(BF16)


def finish_kernel(scale, parts, out, mark):
    total = parts[0].astype(F32)
    for i in range(1, parts.shape[0]):
        total = total + parts[i].astype(F32)
    total = total * scale
    for k in range(27):
        lanes = slice(8 * (k // 2), 8 * (k // 2) + 8)
        rows = [8 * x + 4 * (k % 2) for x in range(2)]
        out[k] = jnp.concatenate([total[r : r + 4, lanes] for r in rows], 1)
    mark[...] = jnp.zeros_like(mark)


def clip_kernel(grad, following, filters, keep, send, wide):
    lane = lax.broadcasted_iota(jnp.int32, (192, 2 * OWN), 1)
    up = one_hot(192, 192, lambda r: jnp.where(r % 16 == 15, -1, r + 1))
    down = one_hot(192, 192, lambda r: jnp.where(r % 16 == 0, -1, r - 1))
    for f in range(FRAMES + 2):
        src = grad[f] if f < FRAMES else following[f - FRAMES]
        wide[f * SPAN : (f + 1) * SPAN, :, : 2 * OWN] = src
    for g in range(0, (FRAMES + 2) * SPAN, 12):
        block = wide[g : g + 12, :, : 2 * OWN].reshape(192, 2 * OWN)
        moved = jnp.where(lane < OWN, mm(up, block), mm(down, block)).astype(BF16)
        wide[g : g + 12, :, 2 * OWN :] = moved.reshape(12, 16, 2 * OWN)
    total = jnp.zeros((FRAMES * ROWS * 16, 256), F32)
    for a in range(3):
        for b in range(3):
            tops = [(f + 2 - a) * SPAN + 2 - b for f in range(FRAMES)]
            win = jnp.concatenate([wide[x : x + ROWS] for x in tops], 0)
            total = total + mm(win.reshape(FRAMES * ROWS * 16, 4 * OWN), filters[a * 3 + b])
    total = total.reshape(FRAMES, ROWS, 16, 256)
    low, high = total[:, :4], total[:, 4:]
    even = lax.axis_index("height") % CORES == 0
    keep[...] = jnp.where(even, low, high)
    send[...] = jnp.where(even, high, low)


def halve_kernel(kept, got, keep, send):
    total = kept[...] + got[...]
    first = lax.axis_index("tm") % 2 == 0
    low, high = total[:2], total[2:]
    keep[...] = jnp.where(first, low, high)
    send[...] = jnp.where(first, high, low).astype(BF16)


def join_kernel(kept, got, _, out):
    total = (kept[...] + got[...].astype(F32)).astype(BF16).reshape(128, 256)
    low = one_hot(256, 128, lambda r: jnp.where(r % 2 == 0, (r // 32) * 16 + (r % 32) // 2, -1))
    high = one_hot(256, 128, lambda r: jnp.where(r % 2 == 1, (r // 32) * 16 + (r % 32) // 2, -1))
    moved = mm(low, total[:, :128]) + mm(high, total[:, 128:])
    out[...] = moved.astype(BF16).reshape(out.shape)


def inside(pairs, count):
    return [(i, k) for i, k in pairs if 0 <= k < count]


def body(clip, first_filter, second_filter, upstream):
    frames, rows, width, cin = clip.shape
    chans = first_filter.shape[4]
    tms, heights = lax.axis_size("tm"), lax.axis_size("height")
    lines = tms // 2
    siblings = [(i, i ^ 1) for i in range(heights)]
    blocks = [(t, t ^ 1) for t in range(tms)]

    here, edge = call(
        stack_kernel,
        [shaped((10, 32, 128), BF16), shaped((5, 32, 128), BF16)],
        [clip, upstream],
        fetch=(0, 1),
    )
    near_pairs = inside([(i, i + 1 if i % 2 else i - 1) for i in range(heights)], heights)
    edge = lax.ppermute(edge, "height", near_pairs)

    second = jnp.swapaxes(second_filter, 3, 4).reshape(27, chans // heights, chans)
    (pieces,) = call(
        filter_pieces_kernel,
        [shaped((heights, chans // heights, 27 * OWN), BF16)],
        [second],
        fetch=(0,),
        flops=2 * 27 * 16 * 256 * 128,
    )

    here, pieces = call(
        append_kernel,
        [shaped((15, 32, 128), BF16), shaped(pieces.shape, BF16)],
        [here, edge, pieces],
        scratch=[pltpu.SemaphoreType.DMA((2,))],
        idle=(0, 1, 2),
        alias={2: 1},
    )
    pair = lax.ppermute(here, "tm", blocks)
    forward, backward, pieces = call(
        choose_kernel,
        [shaped((12, 32, 128), BF16), shaped((3, 32, 128), BF16), shaped(pieces.shape, BF16)],
        [here, pair, pieces],
        fetch=(1,),
        idle=(2,),
        alias={2: 2},
    )
    second = lax.all_to_all(pieces, "height", 0, 0).reshape(chans, 27 * OWN)
    forth = inside([(t, t + 2) for t in range(tms)], tms)
    back = inside([(t, t - 2) for t in range(tms)], tms)
    before = lax.ppermute(forward, "tm", forth)
    after = lax.ppermute(backward, "tm", back)

    first = first_filter.reshape(27 * cin, chans)
    (band,) = call(
        band_kernel,
        [shaped((9, 512, 2 * OWN), BF16)],
        [first],
        fetch=(0,),
        flops=2 * 27 * 128 * 256 * 128,
    )

    (packed,) = call(
        pack_kernel, [shaped((45, 32, 128), BF16)], [here, pair, before, after], fetch=(1, 2, 3)
    )
    other = lax.ppermute(packed, "height", siblings)

    units, up_units = 6 * HIGH, 3 * HALF_HIGH
    grad_pre, parts = call(
        middle_kernel,
        [shaped((FRAMES, SPAN, 16, 2 * OWN), BF16), shaped((heights, 7, 16, cin), BF16)],
        [packed, other, band, second],
        scratch=[
            pltpu.VMEM((units, 16, 512), BF16),
            pltpu.VMEM((2, up_units, 16, 256), BF16),
            pltpu.VMEM((2, 2, 2, HALF, 16, 2 * OWN), F32),
            pltpu.VMEM((units, 32, 128), BF16),
            pltpu.VMEM((up_units, 16, 256), BF16),
        ],
        fetch=(0, 1, 3),
        flops=2 * 640 * 9 * 512 * 128 * 2,
    )

    planes = [
        [(2 * z + x) * heights + CORES * g + core for x in range(2) for g in range(heights // 2)]
        for z in range(lines)
        for core in range(CORES)
    ]
    parts = lax.all_to_all(parts, ("tm", "height"), 0, 0, axis_index_groups=planes)
    following = lax.ppermute(grad_pre[:2], "tm", back)
    (turned,) = call(
        turned_kernel,
        [shaped((9, 4 * OWN, 2 * cin), BF16)],
        [first, grad_pre],
        fetch=(0,),
        idle=(1,),
        flops=2 * 27 * 128 * 256 * 64,
    )
    keep, send = call(
        clip_kernel,
        [shaped((FRAMES, rows, 16, 2 * cin), F32)] * 2,
        [grad_pre, following, turned],
        scratch=[pltpu.VMEM(((FRAMES + 2) * SPAN, 16, 4 * OWN), BF16)],
        fetch=(1,),
        flops=2 * 512 * 9 * 256 * 256,
    )

    (sums,) = call(
        sum_turn_kernel,
        [shaped((lines, 16, 128), BF16)],
        [parts, send],
        fetch=(0,),
        idle=(1,),
    )
    columns = [[2 * ((i + 8) % lines) + x for i in range(lines)] for x in range(2)]
    summed = lax.all_to_all(sums, "tm", 0, 0, axis_index_groups=columns)
    got = lax.ppermute(send, "height", siblings)
    keep, send = call(
        halve_kernel,
        [shaped((2, rows, 16, 2 * cin), F32), shaped((2, rows, 16, 2 * cin), BF16)],
        [keep, got],
        fetch=(1,),
    )
    got = lax.ppermute(send, "tm", blocks)
    count = frames * tms * rows * heights * width
    grad_filter, mark = call(
        functools.partial(finish_kernel, 1.0 / float(count) ** 0.5),
        [shaped((27, cin // tms, chans // heights), F32), shaped((8, 128), F32)],
        [summed],
        fetch=(0,),
    )
    (grad_clip,) = call(
        join_kernel,
        [shaped(clip.shape, BF16)],
        [keep, got, mark],
        fetch=(1,),
        idle=(2,),
    )
    grad_filter = grad_filter.reshape(3, 3, 3, cin // tms, chans // heights)
    return (grad_clip, grad_filter)


def solution(mesh):
    in_specs = (
        P("tm", "height", None, None),
        P(),
        P(None, None, None, None, "height"),
        P("tm", "height", None, None),
    )
    out_specs = (P("tm", "height", None, None), P(None, None, None, "tm", "height"))
    return jax.shard_map(body, mesh=mesh, in_specs=in_specs, out_specs=out_specs, check_vma=False)
```

```python
import functools

import jax
import jax.numpy as jnp
from jax import lax
from jax.experimental import pallas as pl
from jax.experimental.pallas import tpu as pltpu
from jax.sharding import PartitionSpec as P

F32, BF16 = jnp.float32, jnp.bfloat16
CORES = 2
OWN = 64
FRAMES = 4
ROWS, SPAN = 8, 10
HIGH, HALF_HIGH, HALF = ROWS + 4, ROWS // 2 + 2, SPAN // 2
MIDDLE = (1, 2, 3, 0)

LONG = {0: ((2, 0),), 1: ((0, 0), (1, 1))}
WIDE = {0: ((1, 0), (2, 1)), 1: ((0, 1),)}


def shift_classes():
    classes = []
    for t in (1, 0):
        for h in (1, 0):
            for w in (0, 1):
                taps = tuple(
                    ((a, b, c), (fp, ip, jp))
                    for a, fp in LONG[t]
                    for b, ip in LONG[h]
                    for c, jp in WIDE[w]
                )
                classes.append(((t, h, w), taps))
    return classes


CLASSES = shift_classes()
TAP_ORDER = [tap for _, taps in CLASSES for tap, _ in taps]


def mm(lhs, rhs):
    return jnp.dot(lhs, rhs, preferred_element_type=F32)


def one_hot(rows, cols, column_of):
    row = lax.broadcasted_iota(jnp.int32, (rows, cols), 0)
    col = lax.broadcasted_iota(jnp.int32, (rows, cols), 1)
    return jnp.where(column_of(row) == col, 1.0, 0.0).astype(BF16)


def call(kernel, out, args, scratch=(), fetch=(), idle=(), alias=None, flops=0, limit=16):
    n_in, n_out, n_scratch = len(args), len(out), len(scratch)

    def run(*refs):
        ins, outs = list(refs[:n_in]), refs[n_in : n_in + n_out]
        rest = refs[n_in + n_out :]
        if fetch:
            landing, sems = rest[n_scratch:-1], rest[-1]
            copies = [
                pltpu.make_async_copy(ins[i], landing[k], sems.at[k]) for k, i in enumerate(fetch)
            ]
            for copy in copies:
                copy.start()
            for copy in copies:
                copy.wait()
            for k, i in enumerate(fetch):
                ins[i] = landing[k]
        kernel(*ins, *outs, *rest[:n_scratch])

    spec = pl.BlockSpec(memory_space=pltpu.VMEM)
    far = pl.BlockSpec(memory_space=pl.ANY)
    moved = sum(x.size * x.dtype.itemsize for x in list(args) + list(out))
    extra = [pltpu.VMEM(args[i].shape, args[i].dtype) for i in fetch]
    if fetch:
        extra.append(pltpu.SemaphoreType.DMA((len(fetch),)))
    return pl.pallas_call(
        run,
        out_shape=tuple(out),
        in_specs=[far if i in fetch or i in idle else spec for i in range(n_in)],
        out_specs=tuple([far if i in (alias or {}).values() else spec for i in range(n_out)]),
        input_output_aliases=dict(alias or {}),
        scratch_shapes=list(scratch) + extra,
        compiler_params=pltpu.CompilerParams(vmem_limit_bytes=limit * 1024 * 1024),
        cost_estimate=pl.CostEstimate(flops=flops, bytes_accessed=moved, transcendentals=0),
    )(*args)


def shaped(shape, dtype):
    return jax.ShapeDtypeStruct(shape, dtype)


def own_channel(place, x, core):
    return (2 * (place // 8) + core) * 16 + 8 * x + place % 8


def filter_pieces_kernel(second, out):
    taps, depth, chans = second.shape
    x = lax.axis_index("tm") % 2
    row = lax.broadcasted_iota(jnp.int32, (chans, 2 * OWN), 0)
    col = lax.broadcasted_iota(jnp.int32, (chans, 2 * OWN), 1)
    order = jnp.where(own_channel(col % OWN, x, col // OWN) == row, 1.0, 0.0).astype(BF16)
    moved = mm(second[...].reshape(taps * depth, chans), order).astype(BF16)
    moved = moved.reshape(taps, depth, 2 * OWN)
    for place in range(0, len(TAP_ORDER), 2):
        pair = TAP_ORDER[place : place + 2]
        for core in range(CORES):
            lanes = slice(core * OWN, (core + 1) * OWN)
            piece = jnp.concatenate([moved[a * 9 + b * 3 + c, :, lanes] for a, b, c in pair], 1)
            for p in range(core, out.shape[0], CORES):
                out[p, :, place * OWN : place * OWN + piece.shape[1]] = piece


def own_filter_kernel(first, band, flat):
    chans = first.shape[1]
    x, core = lax.axis_index("tm") % 2, lax.axis_index("height") % CORES
    row = lax.broadcasted_iota(jnp.int32, (chans, 2 * OWN), 0)
    col = lax.broadcasted_iota(jnp.int32, (chans, 2 * OWN), 1)
    pick = jnp.where(own_channel(col % OWN, x, core) == row, 1.0, 0.0).astype(BF16)
    twice = mm(first[...], pick)
    lane = lax.broadcasted_iota(jnp.int32, (128, 2 * OWN), 1)
    for ab in range(9):
        lanes = slice((ab % 3) * 128, (ab % 3 + 1) * 128)
        for s in range(4):
            left = twice[(ab * 3 + s) * 128 : (ab * 3 + s + 1) * 128] if s < 3 else 0.0
            right = twice[(ab * 3 + s - 1) * 128 : (ab * 3 + s) * 128] if s > 0 else 0.0
            both = jnp.where(lane < OWN, left, right)
            band[ab // 3, s * 128 : (s + 1) * 128, lanes] = both.astype(BF16)
    row = lax.broadcasted_iota(jnp.int32, (OWN, chans), 0)
    col = lax.broadcasted_iota(jnp.int32, (OWN, chans), 1)
    pick = jnp.where(own_channel(row, x, core) == col, 1.0, 0.0).astype(BF16)
    flat[...] = lax.dot_general(
        pick, first[...], (((1,), (1,)), ((), ())), preferred_element_type=F32
    ).astype(BF16)


def stack_kernel(clip, up, here, edge):
    at_top = lax.axis_index("height") % CORES == 0
    for f in range(2):
        here[4 * f : 4 * f + 4] = clip[f]
        edge[2 * f : 2 * f + 2] = jnp.where(at_top, clip[f, :2], clip[f, 2:])
    for half in range(2):
        subs = slice(16 * half, 16 * half + 16)
        src = up[0, :, :, 128 * half : 128 * half + 128]
        here[8:10, subs] = src
        edge[4, subs] = jnp.where(at_top, src[0], src[1])


def append_kernel(here, edge, _, out, __, sems):
    copies = [
        pltpu.make_async_copy(here, out.at[:10], sems.at[0]),
        pltpu.make_async_copy(edge, out.at[10:], sems.at[1]),
    ]
    for copy in copies:
        copy.start()
    for copy in copies:
        copy.wait()


def choose_kernel(here, pair, _, forward, backward, __):
    first = lax.axis_index("tm") % 2 == 0
    forward[:8] = jnp.where(first, pair[:8], here[:8])
    forward[8:12] = jnp.where(first, pair[10:14], here[10:14])
    backward[:2] = jnp.where(first, here[8:10], pair[8:10])
    backward[2] = jnp.where(first, here[14], pair[14])


def pack_kernel(here, pair, before, after, packed):
    first = lax.axis_index("tm") % 2 == 0
    one = jnp.where(first, here[...], pair[...])
    two = jnp.where(first, pair[...], here[...])
    packed[:8] = before[:8]
    packed[30:34] = before[8:12]
    for k, src in ((1, one), (2, two)):
        packed[8 * k : 8 * k + 8] = src[:8]
        packed[30 + 4 * k : 34 + 4 * k] = src[10:14]
    for t, src in enumerate((one[8:10], two[8:10], after[:2])):
        packed[24 + 2 * t : 26 + 2 * t] = src
    for t, src in enumerate((one[14], two[14], after[2])):
        packed[42 + t] = src


def preact_kernel(own, other, filters, wide, ups, pre, band, ext):
    member = lax.axis_index("height") % CORES
    even = member == 0
    above = jnp.where(even, own[30:45], other[30:45])
    below = jnp.where(even, other[30:45], own[30:45])
    for f in range(6):
        base = f * HIGH
        band[pl.ds(base + 2 + 4 * member, 4)] = own[4 * f : 4 * f + 4]
        band[pl.ds(base + 6 - 4 * member, 4)] = other[4 * f : 4 * f + 4]
        band[base : base + 2] = above[2 * f : 2 * f + 2]
        band[base + ROWS + 2 : base + ROWS + 4] = below[2 * f : 2 * f + 2]
    for t in range(3):
        base, unit = t * HALF_HIGH, 24 + 2 * t
        for half in range(2):
            lanes = slice(128 * half, 128 * half + 128)
            subs = slice(16 * half, 16 * half + 16)
            ext[pl.ds(base + 1 + 2 * member, 2), :, lanes] = own[unit : unit + 2, subs]
            ext[pl.ds(base + 3 - 2 * member, 2), :, lanes] = other[unit : unit + 2, subs]
            ext[base, :, lanes] = above[12 + t, subs]
            ext[base + HALF_HIGH - 1, :, lanes] = below[12 + t, subs]
    units = ext.shape[0]
    flat = ext[...].reshape(units * 16, 256)
    shift = one_hot(units * 16, units * 16, lambda r: jnp.where(r % 16 == 15, -1, r + 1))
    ups[0] = flat.reshape(units, 16, 256)
    ups[1] = mm(shift, flat).astype(BF16).reshape(units, 16, 256)

    def column(r):
        s, unit, w = r // 128, (r // 16) % 8, 2 * (r % 16) + r // 128 - 1
        return jnp.where((w >= 0) & (w < 32), unit * 32 + w, -1)

    matrix = one_hot(512, 256, column)
    for g in range(band.shape[0] // 8):
        moved = mm(matrix, band[8 * g : 8 * g + 8].reshape(256, 128)).astype(BF16)
        for s in range(4):
            piece = moved[128 * s : 128 * s + 128].reshape(8, 16, 128)
            wide[8 * g : 8 * g + 8, :, s * 128 : (s + 1) * 128] = piece
    total = jnp.zeros((FRAMES, SPAN, 16, 2 * OWN), F32)
    for a in range(3):
        tops = [(a + f) * HIGH for f in range(FRAMES)]
        win = jnp.concatenate([wide[x : x + SPAN + 1] for x in tops], 0)
        prod = mm(win.reshape(FRAMES * (SPAN + 1) * 16, 512), filters[a, :, : 4 * OWN])
        prod = prod.reshape(FRAMES, SPAN + 1, 16, 4 * OWN)
        total = total + prod[:, :SPAN, :, : 2 * OWN] + prod[:, 1:, :, 2 * OWN :]
        win = jnp.concatenate([wide[x + 2 : x + 2 + SPAN] for x in tops], 0)
        prod = mm(win.reshape(FRAMES * SPAN * 16, 512), filters[a, :, 4 * OWN :])
        total = total + prod.reshape(FRAMES, SPAN, 16, 2 * OWN)
    for f in range(FRAMES):
        for r in range(SPAN):
            pre[f % 2, r % 2, f // 2, r // 2] = total[f, r]


def gradient_kernel(second, ups, pre, wide, grad, parts):
    group = lax.axis_index("height") // CORES
    first_band = group == 0
    last_band = group == lax.axis_size("height") // CORES - 1
    even, odd = {}, {}
    offset = 0
    for (t, h, w), taps in CLASSES:
        tops = [(t + q) * HALF_HIGH + h for q in range(2)]
        lhs = jnp.concatenate([ups[w, x : x + HALF] for x in tops], 0).reshape(32 * HALF, 256)
        prod = mm(lhs, second[:, offset : offset + len(taps) * OWN])
        offset += len(taps) * OWN
        total, step = (odd, 1) if w else (even, 2)
        for k in range(0, len(taps), step):
            key = taps[k][1][:2]
            piece = prod[:, k * OWN : (k + step) * OWN]
            total[key] = total[key] + piece if key in total else piece
    blank = jnp.zeros((32 * HALF, OWN), F32)
    for (fp, ip), act in even.items():
        act = act + jnp.concatenate([blank, odd[fp, ip]], 1)
        x = pre[fp, ip].reshape(32 * HALF, 2 * OWN)
        sig = jax.nn.sigmoid(x)
        g = (act * sig * (1.0 + x * (1.0 - sig))).reshape(2, HALF, 16, 2 * OWN)
        for q in range(2):
            for p in range(HALF):
                piece, r = g[q, p], 2 * p + ip
                if r == 0:
                    piece = jnp.where(first_band, 0.0, piece)
                if r == SPAN - 1:
                    piece = jnp.where(last_band, 0.0, piece)
                grad[2 * q + fp, r] = piece.astype(BF16)
    turned = grad[:, 1 : 1 + ROWS].reshape(FRAMES * ROWS * 16, 2 * OWN).T
    strips = []
    for a in range(3):
        for b in range(3):
            tops = [(a + f) * HIGH + 1 + b for f in range(FRAMES)]
            win = jnp.concatenate([wide[x : x + ROWS] for x in tops], 0)
            prod = mm(turned, win.reshape(FRAMES * ROWS * 16, 512))
            for c in range(3):
                piece = prod[:OWN, 128 * c : 128 * c + 128]
                piece = piece + prod[OWN:, 128 * c + 128 : 128 * c + 256]
                strips.append(piece.astype(BF16))
    strips.append(jnp.zeros_like(strips[0]))
    row = lax.broadcasted_iota(jnp.int32, (256, 256), 0)
    col = lax.broadcasted_iota(jnp.int32, (256, 256), 1)
    x, tap, z, e = col // 128, (col // 64) % 2, (col // 4) % 16, col % 4
    order = jnp.where(tap * 128 + 8 * z + 4 * x + e == row, 1.0, 0.0).astype(BF16)
    blocks = OWN // 8
    for k in range(7):
        pairs = [jnp.concatenate(strips[i : i + 2], 1) for i in (4 * k, 4 * k + 2)]
        pairs = [mm(pair, order).reshape(blocks, 8, 256) for pair in pairs]
        both = jnp.concatenate(pairs, 1).astype(BF16)
        for x in range(2):
            parts[x * blocks : (x + 1) * blocks, k] = both[:, :, 128 * x : 128 * x + 128]


def sum_turn_kernel(parts, _, out):
    blank = jnp.zeros((16, 128), F32)
    blocks = parts.shape[0] // 2
    halves = []
    for x in range(2):
        total = parts[x * blocks].astype(F32)
        for i in range(1, blocks):
            total = total + parts[x * blocks + i].astype(F32)
        halves += [total.reshape(112, 128), blank]
    flat = jnp.concatenate(halves, 0).T
    for i in range(16):
        z = (i + 8) % 16
        rows = [(tap * 64 + z * 4, x) for x in range(2) for tap in range(2)]
        block = [flat[r : r + 4, 128 * x : 128 * x + 128] for r, x in rows]
        out[i] = jnp.concatenate(block, 0).astype(BF16)


def finish_kernel(scale, parts, out, mark):
    total = parts[0].astype(F32)
    for i in range(1, parts.shape[0]):
        total = total + parts[i].astype(F32)
    total = total * scale
    for k in range(27):
        lanes = slice(8 * (k // 2), 8 * (k // 2) + 8)
        rows = [8 * x + 4 * (k % 2) for x in range(2)]
        out[k] = jnp.concatenate([total[r : r + 4, lanes] for r in rows], 1)
    mark[...] = jnp.zeros_like(mark)


def clip_kernel(grad, following, flat, keep, send, wide, filters):
    for ab in range(9):
        for slot, s in enumerate(MIDDLE):
            for jp in range(2):
                c = jp + 2 - s
                if 0 <= c <= 2:
                    piece = flat[:, (ab * 3 + c) * 128 : (ab * 3 + c + 1) * 128]
                else:
                    piece = jnp.zeros((OWN, 128), BF16)
                filters[ab, slot * OWN : (slot + 1) * OWN, jp * 128 : (jp + 1) * 128] = piece
    lane = lax.broadcasted_iota(jnp.int32, (192, 2 * OWN), 1)
    up = one_hot(192, 192, lambda r: jnp.where(r % 16 == 15, -1, r + 1))
    down = one_hot(192, 192, lambda r: jnp.where(r % 16 == 0, -1, r - 1))
    for f in range(FRAMES + 2):
        src = grad[f] if f < FRAMES else following[f - FRAMES]
        wide[f * SPAN : (f + 1) * SPAN, :, : 2 * OWN] = src
    for g in range(0, (FRAMES + 2) * SPAN, 12):
        block = wide[g : g + 12, :, : 2 * OWN].reshape(192, 2 * OWN)
        moved = jnp.where(lane < OWN, mm(up, block), mm(down, block)).astype(BF16)
        wide[g : g + 12, :, 2 * OWN :] = moved.reshape(12, 16, 2 * OWN)
    total = jnp.zeros((FRAMES * ROWS * 16, 256), F32)
    for a in range(3):
        for b in range(3):
            tops = [(f + 2 - a) * SPAN + 2 - b for f in range(FRAMES)]
            win = jnp.concatenate([wide[x : x + ROWS] for x in tops], 0)
            total = total + mm(win.reshape(FRAMES * ROWS * 16, 4 * OWN), filters[a * 3 + b])
    total = total.reshape(FRAMES, ROWS, 16, 256)
    first = lax.axis_index("tm") % 2 == 0
    keep[...] = jnp.where(first, total[:2], total[2:])
    send[...] = jnp.where(first, total[2:], total[:2]).astype(BF16)


def halve_kernel(kept, got, keep, send):
    total = kept[...] + got[...].astype(F32)
    even = lax.axis_index("height") % CORES == 0
    keep[...] = jnp.where(even, total[:, :4], total[:, 4:])
    send[...] = jnp.where(even, total[:, 4:], total[:, :4])


def join_kernel(kept, got, _, out):
    total = (kept[...] + got[...]).astype(BF16).reshape(128, 256)
    low = one_hot(256, 128, lambda r: jnp.where(r % 2 == 0, (r // 32) * 16 + (r % 32) // 2, -1))
    high = one_hot(256, 128, lambda r: jnp.where(r % 2 == 1, (r // 32) * 16 + (r % 32) // 2, -1))
    moved = mm(low, total[:, :128]) + mm(high, total[:, 128:])
    out[...] = moved.astype(BF16).reshape(out.shape)


def inside(pairs, count):
    return [(i, k) for i, k in pairs if 0 <= k < count]


def body(clip, first_filter, second_filter, upstream):
    frames, rows, width, cin = clip.shape
    chans = first_filter.shape[4]
    tms, heights = lax.axis_size("tm"), lax.axis_size("height")
    lines = tms // 2
    siblings = [(i, i ^ 1) for i in range(heights)]
    blocks = [(t, t ^ 1) for t in range(tms)]

    here, edge = call(
        stack_kernel,
        [shaped((10, 32, 128), BF16), shaped((5, 32, 128), BF16)],
        [clip, upstream],
        fetch=(0, 1),
    )
    near_pairs = inside([(i, i + 1 if i % 2 else i - 1) for i in range(heights)], heights)
    edge = lax.ppermute(edge, "height", near_pairs)

    second = jnp.swapaxes(second_filter, 3, 4).reshape(27, chans // heights, chans)
    (pieces,) = call(
        filter_pieces_kernel,
        [shaped((heights, chans // heights, 27 * OWN), BF16)],
        [second],
        fetch=(0,),
        flops=2 * 27 * 16 * 256 * 128,
    )

    here, pieces = call(
        append_kernel,
        [shaped((15, 32, 128), BF16), shaped(pieces.shape, BF16)],
        [here, edge, pieces],
        scratch=[pltpu.SemaphoreType.DMA((2,))],
        idle=(0, 1, 2),
        alias={2: 1},
    )
    pair = lax.ppermute(here, "tm", blocks)
    forward, backward, pieces = call(
        choose_kernel,
        [shaped((12, 32, 128), BF16), shaped((3, 32, 128), BF16), shaped(pieces.shape, BF16)],
        [here, pair, pieces],
        fetch=(1,),
        idle=(2,),
        alias={2: 2},
    )
    second = lax.all_to_all(pieces, "height", 0, 0).reshape(chans, 27 * OWN)
    forth = inside([(t, t + 2) for t in range(tms)], tms)
    back = inside([(t, t - 2) for t in range(tms)], tms)
    before = lax.ppermute(forward, "tm", forth)
    after = lax.ppermute(backward, "tm", back)

    first = first_filter.reshape(27 * cin, chans)
    band, flat = call(
        own_filter_kernel,
        [shaped((3, 512, 6 * OWN), BF16), shaped((OWN, 27 * cin), BF16)],
        [first],
        fetch=(0,),
        flops=3 * 27 * 128 * 256 * 128,
    )

    (packed,) = call(
        pack_kernel, [shaped((45, 32, 128), BF16)], [here, pair, before, after], fetch=(1, 2, 3)
    )
    other = lax.ppermute(packed, "height", siblings)

    units, up_units = 6 * HIGH, 3 * HALF_HIGH
    wide, ups, pre = call(
        preact_kernel,
        [
            shaped((units, 16, 512), BF16),
            shaped((2, up_units, 16, 256), BF16),
            shaped((2, 2, 2, HALF, 16, 2 * OWN), F32),
        ],
        [packed, other, band],
        scratch=[pltpu.VMEM((units, 32, 128), BF16), pltpu.VMEM((up_units, 16, 256), BF16)],
        fetch=(1,),
        flops=2 * 640 * 9 * 512 * 128,
    )
    grad_pre, parts = call(
        gradient_kernel,
        [shaped((FRAMES, SPAN, 16, 2 * OWN), BF16), shaped((heights, 7, 16, cin), BF16)],
        [second, ups, pre, wide],
        fetch=(0,),
        flops=2 * 512 * 9 * 512 * 128,
    )

    planes = [
        [(2 * z + x) * heights + CORES * g + core for x in range(2) for g in range(heights // 2)]
        for z in range(lines)
        for core in range(CORES)
    ]
    parts = lax.all_to_all(parts, ("tm", "height"), 0, 0, axis_index_groups=planes)
    following = lax.ppermute(grad_pre[:2], "tm", back)
    keep, send = call(
        clip_kernel,
        [shaped((2, ROWS, 16, 2 * cin), F32), shaped((2, ROWS, 16, 2 * cin), BF16)],
        [grad_pre, following, flat],
        scratch=[
            pltpu.VMEM(((FRAMES + 2) * SPAN, 16, 4 * OWN), BF16),
            pltpu.VMEM((9, 4 * OWN, 2 * cin), BF16),
        ],
        fetch=(1,),
        flops=2 * 512 * 9 * 256 * 256,
    )

    (sums,) = call(
        sum_turn_kernel,
        [shaped((lines, 16, 128), BF16)],
        [parts, send],
        fetch=(0,),
        idle=(1,),
    )
    columns = [[2 * ((i + 8) % lines) + x for i in range(lines)] for x in range(2)]
    summed = lax.all_to_all(sums, "tm", 0, 0, axis_index_groups=columns)
    got = lax.ppermute(send, "tm", blocks)
    keep, send = call(
        halve_kernel,
        [shaped((2, rows, 16, 2 * cin), F32)] * 2,
        [keep, got],
        fetch=(1,),
    )
    got = lax.ppermute(send, "height", siblings)
    count = frames * tms * rows * heights * width
    grad_filter, mark = call(
        functools.partial(finish_kernel, 1.0 / float(count) ** 0.5),
        [shaped((27, cin // tms, chans // heights), F32), shaped((8, 128), F32)],
        [summed],
        fetch=(0,),
    )
    (grad_clip,) = call(
        join_kernel,
        [shaped(clip.shape, BF16)],
        [keep, got, mark],
        fetch=(1,),
        idle=(2,),
    )
    grad_filter = grad_filter.reshape(3, 3, 3, cin // tms, chans // heights)
    return (grad_clip, grad_filter)


def solution(mesh):
    in_specs = (
        P("tm", "height", None, None),
        P(),
        P(None, None, None, None, "height"),
        P("tm", "height", None, None),
    )
    out_specs = (P("tm", "height", None, None), P(None, None, None, "tm", "height"))
    return jax.shard_map(body, mesh=mesh, in_specs=in_specs, out_specs=out_specs, check_vma=False)
```

```python
import functools

import jax
import jax.numpy as jnp
from jax import lax
from jax.experimental import pallas as pl
from jax.experimental.pallas import tpu as pltpu
from jax.sharding import PartitionSpec as P

F32, BF16 = jnp.float32, jnp.bfloat16
CORES = 2
OWN = 64
FRAMES = 4
ROWS, SPAN = 8, 10
HIGH, HALF_HIGH, HALF = ROWS + 4, ROWS // 2 + 2, SPAN // 2
MIDDLE = (1, 2, 3, 0)

LONG = {0: ((2, 0),), 1: ((0, 0), (1, 1))}
WIDE = {0: ((1, 0), (2, 1)), 1: ((0, 1),)}


def shift_classes():
    classes = []
    for t in (1, 0):
        for h in (1, 0):
            for w in (0, 1):
                taps = tuple(
                    ((a, b, c), (fp, ip, jp))
                    for a, fp in LONG[t]
                    for b, ip in LONG[h]
                    for c, jp in WIDE[w]
                )
                classes.append(((t, h, w), taps))
    return classes


CLASSES = shift_classes()
TAP_ORDER = [tap for _, taps in CLASSES for tap, _ in taps]


def mm(lhs, rhs):
    return jnp.dot(lhs, rhs, preferred_element_type=F32)


def one_hot(rows, cols, column_of):
    row = lax.broadcasted_iota(jnp.int32, (rows, cols), 0)
    col = lax.broadcasted_iota(jnp.int32, (rows, cols), 1)
    return jnp.where(column_of(row) == col, 1.0, 0.0).astype(BF16)


def call(kernel, out, args, scratch=(), idle=(), alias=None, flops=0, limit=16):
    spec = pl.BlockSpec(memory_space=pltpu.VMEM)
    far = pl.BlockSpec(memory_space=pl.ANY)
    moved = sum(x.size * x.dtype.itemsize for x in list(args) + list(out))
    return pl.pallas_call(
        kernel,
        out_shape=tuple(out),
        in_specs=[far if i in idle else spec for i in range(len(args))],
        out_specs=tuple([far if i in (alias or {}).values() else spec for i in range(len(out))]),
        input_output_aliases=dict(alias or {}),
        scratch_shapes=list(scratch),
        compiler_params=pltpu.CompilerParams(vmem_limit_bytes=limit * 1024 * 1024),
        cost_estimate=pl.CostEstimate(flops=flops, bytes_accessed=moved, transcendentals=0),
    )(*args)


def shaped(shape, dtype):
    return jax.ShapeDtypeStruct(shape, dtype)


def own_channel(place, x, core):
    return (2 * (place // 8) + core) * 16 + 8 * x + place % 8


def filter_pieces_kernel(second, out):
    taps, depth, chans = second.shape
    x = lax.axis_index("tm") % 2
    row = lax.broadcasted_iota(jnp.int32, (chans, 2 * OWN), 0)
    col = lax.broadcasted_iota(jnp.int32, (chans, 2 * OWN), 1)
    order = jnp.where(own_channel(col % OWN, x, col // OWN) == row, 1.0, 0.0).astype(BF16)
    moved = mm(second[...].reshape(taps * depth, chans), order).astype(BF16)
    moved = moved.reshape(taps, depth, 2 * OWN)
    for place in range(0, len(TAP_ORDER), 2):
        pair = TAP_ORDER[place : place + 2]
        for core in range(CORES):
            lanes = slice(core * OWN, (core + 1) * OWN)
            piece = jnp.concatenate([moved[a * 9 + b * 3 + c, :, lanes] for a, b, c in pair], 1)
            for p in range(core, out.shape[0], CORES):
                out[p, :, place * OWN : place * OWN + piece.shape[1]] = piece


def own_filter_kernel(first, band, flat):
    chans = first.shape[1]
    x, core = lax.axis_index("tm") % 2, lax.axis_index("height") % CORES
    row = lax.broadcasted_iota(jnp.int32, (chans, 2 * OWN), 0)
    col = lax.broadcasted_iota(jnp.int32, (chans, 2 * OWN), 1)
    pick = jnp.where(own_channel(col % OWN, x, core) == row, 1.0, 0.0).astype(BF16)
    twice = mm(first[...], pick)
    lane = lax.broadcasted_iota(jnp.int32, (128, 2 * OWN), 1)
    for ab in range(9):
        lanes = slice((ab % 3) * 128, (ab % 3 + 1) * 128)
        for s in range(4):
            left = twice[(ab * 3 + s) * 128 : (ab * 3 + s + 1) * 128] if s < 3 else 0.0
            right = twice[(ab * 3 + s - 1) * 128 : (ab * 3 + s) * 128] if s > 0 else 0.0
            both = jnp.where(lane < OWN, left, right)
            band[ab // 3, s * 128 : (s + 1) * 128, lanes] = both.astype(BF16)
    row = lax.broadcasted_iota(jnp.int32, (OWN, chans), 0)
    col = lax.broadcasted_iota(jnp.int32, (OWN, chans), 1)
    pick = jnp.where(own_channel(row, x, core) == col, 1.0, 0.0).astype(BF16)
    flat[...] = lax.dot_general(
        pick, first[...], (((1,), (1,)), ((), ())), preferred_element_type=F32
    ).astype(BF16)


def stack_kernel(clip, up, here, edge):
    at_top = lax.axis_index("height") % CORES == 0
    for f in range(2):
        here[4 * f : 4 * f + 4] = clip[f]
        edge[2 * f : 2 * f + 2] = jnp.where(at_top, clip[f, :2], clip[f, 2:])
    for half in range(2):
        subs = slice(16 * half, 16 * half + 16)
        src = up[0, :, :, 128 * half : 128 * half + 128]
        here[8:10, subs] = src
        edge[4, subs] = jnp.where(at_top, src[0], src[1])


def append_kernel(here, edge, _, out, __, sems):
    copies = [
        pltpu.make_async_copy(here, out.at[:10], sems.at[0]),
        pltpu.make_async_copy(edge, out.at[10:], sems.at[1]),
    ]
    for copy in copies:
        copy.start()
    for copy in copies:
        copy.wait()


def choose_kernel(here, pair, _, forward, backward, __):
    first = lax.axis_index("tm") % 2 == 0
    forward[:8] = jnp.where(first, pair[:8], here[:8])
    forward[8:12] = jnp.where(first, pair[10:14], here[10:14])
    backward[:2] = jnp.where(first, here[8:10], pair[8:10])
    backward[2] = jnp.where(first, here[14], pair[14])


def pack_kernel(here, pair, before, after, packed):
    first = lax.axis_index("tm") % 2 == 0
    one = jnp.where(first, here[...], pair[...])
    two = jnp.where(first, pair[...], here[...])
    packed[:8] = before[:8]
    packed[30:34] = before[8:12]
    for k, src in ((1, one), (2, two)):
        packed[8 * k : 8 * k + 8] = src[:8]
        packed[30 + 4 * k : 34 + 4 * k] = src[10:14]
    for t, src in enumerate((one[8:10], two[8:10], after[:2])):
        packed[24 + 2 * t : 26 + 2 * t] = src
    for t, src in enumerate((one[14], two[14], after[2])):
        packed[42 + t] = src


def preact_kernel(own, other, filters, wide, ups, pre, band, ext):
    member = lax.axis_index("height") % CORES
    even = member == 0
    above = jnp.where(even, own[30:45], other[30:45])
    below = jnp.where(even, other[30:45], own[30:45])
    for f in range(6):
        base = f * HIGH
        band[pl.ds(base + 2 + 4 * member, 4)] = own[4 * f : 4 * f + 4]
        band[pl.ds(base + 6 - 4 * member, 4)] = other[4 * f : 4 * f + 4]
        band[base : base + 2] = above[2 * f : 2 * f + 2]
        band[base + ROWS + 2 : base + ROWS + 4] = below[2 * f : 2 * f + 2]
    for t in range(3):
        base, unit = t * HALF_HIGH, 24 + 2 * t
        for half in range(2):
            lanes = slice(128 * half, 128 * half + 128)
            subs = slice(16 * half, 16 * half + 16)
            ext[pl.ds(base + 1 + 2 * member, 2), :, lanes] = own[unit : unit + 2, subs]
            ext[pl.ds(base + 3 - 2 * member, 2), :, lanes] = other[unit : unit + 2, subs]
            ext[base, :, lanes] = above[12 + t, subs]
            ext[base + HALF_HIGH - 1, :, lanes] = below[12 + t, subs]
    units = ext.shape[0]
    flat = ext[...].reshape(units * 16, 256)
    shift = one_hot(units * 16, units * 16, lambda r: jnp.where(r % 16 == 15, -1, r + 1))
    ups[0] = flat.reshape(units, 16, 256)
    ups[1] = mm(shift, flat).astype(BF16).reshape(units, 16, 256)

    def column(r):
        s, unit, w = r // 128, (r // 16) % 8, 2 * (r % 16) + r // 128 - 1
        return jnp.where((w >= 0) & (w < 32), unit * 32 + w, -1)

    matrix = one_hot(512, 256, column)
    for g in range(band.shape[0] // 8):
        moved = mm(matrix, band[8 * g : 8 * g + 8].reshape(256, 128)).astype(BF16)
        for s in range(4):
            piece = moved[128 * s : 128 * s + 128].reshape(8, 16, 128)
            wide[8 * g : 8 * g + 8, :, s * 128 : (s + 1) * 128] = piece
    total = jnp.zeros((FRAMES, SPAN, 16, 2 * OWN), F32)
    for a in range(3):
        tops = [(a + f) * HIGH for f in range(FRAMES)]
        win = jnp.concatenate([wide[x : x + SPAN + 1] for x in tops], 0)
        prod = mm(win.reshape(FRAMES * (SPAN + 1) * 16, 512), filters[a, :, : 4 * OWN])
        prod = prod.reshape(FRAMES, SPAN + 1, 16, 4 * OWN)
        total = total + prod[:, :SPAN, :, : 2 * OWN] + prod[:, 1:, :, 2 * OWN :]
        win = jnp.concatenate([wide[x + 2 : x + 2 + SPAN] for x in tops], 0)
        prod = mm(win.reshape(FRAMES * SPAN * 16, 512), filters[a, :, 4 * OWN :])
        total = total + prod.reshape(FRAMES, SPAN, 16, 2 * OWN)
    for f in range(FRAMES):
        for r in range(SPAN):
            pre[f % 2, r % 2, f // 2, r // 2] = total[f, r]


def gradient_kernel(second, ups, pre, wide, grad, parts):
    group = lax.axis_index("height") // CORES
    first_band = group == 0
    last_band = group == lax.axis_size("height") // CORES - 1
    even, odd = {}, {}
    offset = 0
    for (t, h, w), taps in CLASSES:
        tops = [(t + q) * HALF_HIGH + h for q in range(2)]
        lhs = jnp.concatenate([ups[w, x : x + HALF] for x in tops], 0).reshape(32 * HALF, 256)
        prod = mm(lhs, second[:, offset : offset + len(taps) * OWN])
        offset += len(taps) * OWN
        total, step = (odd, 1) if w else (even, 2)
        for k in range(0, len(taps), step):
            key = taps[k][1][:2]
            piece = prod[:, k * OWN : (k + step) * OWN]
            total[key] = total[key] + piece if key in total else piece
    blank = jnp.zeros((32 * HALF, OWN), F32)
    for (fp, ip), act in even.items():
        act = act + jnp.concatenate([blank, odd[fp, ip]], 1)
        x = pre[fp, ip].reshape(32 * HALF, 2 * OWN)
        sig = jax.nn.sigmoid(x)
        g = (act * sig * (1.0 + x * (1.0 - sig))).reshape(2, HALF, 16, 2 * OWN)
        for q in range(2):
            for p in range(HALF):
                piece, r = g[q, p], 2 * p + ip
                if r == 0:
                    piece = jnp.where(first_band, 0.0, piece)
                if r == SPAN - 1:
                    piece = jnp.where(last_band, 0.0, piece)
                grad[2 * q + fp, r] = piece.astype(BF16)
    turned = grad[:, 1 : 1 + ROWS].reshape(FRAMES * ROWS * 16, 2 * OWN).T
    strips = []
    for a in range(3):
        for b in range(3):
            tops = [(a + f) * HIGH + 1 + b for f in range(FRAMES)]
            win = jnp.concatenate([wide[x : x + ROWS] for x in tops], 0)
            prod = mm(turned, win.reshape(FRAMES * ROWS * 16, 512))
            for c in range(3):
                piece = prod[:OWN, 128 * c : 128 * c + 128]
                piece = piece + prod[OWN:, 128 * c + 128 : 128 * c + 256]
                strips.append(piece.astype(BF16))
    strips.append(jnp.zeros_like(strips[0]))
    row = lax.broadcasted_iota(jnp.int32, (256, 256), 0)
    col = lax.broadcasted_iota(jnp.int32, (256, 256), 1)
    x, tap, z, e = col // 128, (col // 64) % 2, (col // 4) % 16, col % 4
    order = jnp.where(tap * 128 + 8 * z + 4 * x + e == row, 1.0, 0.0).astype(BF16)
    blocks = OWN // 8
    for k in range(7):
        pairs = [jnp.concatenate(strips[i : i + 2], 1) for i in (4 * k, 4 * k + 2)]
        pairs = [mm(pair, order).reshape(blocks, 8, 256) for pair in pairs]
        both = jnp.concatenate(pairs, 1).astype(BF16)
        for x in range(2):
            parts[x * blocks : (x + 1) * blocks, k] = both[:, :, 128 * x : 128 * x + 128]


def sum_turn_kernel(parts, _, out):
    blank = jnp.zeros((16, 128), F32)
    blocks = parts.shape[0] // 2
    halves = []
    for x in range(2):
        total = parts[x * blocks].astype(F32)
        for i in range(1, blocks):
            total = total + parts[x * blocks + i].astype(F32)
        halves += [total.reshape(112, 128), blank]
    flat = jnp.concatenate(halves, 0).T
    for i in range(16):
        z = (i + 8) % 16
        rows = [(tap * 64 + z * 4, x) for x in range(2) for tap in range(2)]
        block = [flat[r : r + 4, 128 * x : 128 * x + 128] for r, x in rows]
        out[i] = jnp.concatenate(block, 0).astype(BF16)


def finish_kernel(scale, parts, _, out):
    total = parts[0].astype(F32)
    for i in range(1, parts.shape[0]):
        total = total + parts[i].astype(F32)
    total = total * scale
    for k in range(27):
        lanes = slice(8 * (k // 2), 8 * (k // 2) + 8)
        rows = [8 * x + 4 * (k % 2) for x in range(2)]
        out[k] = jnp.concatenate([total[r : r + 4, lanes] for r in rows], 1)


def clip_kernel(grad, following, flat, keep, send, wide, filters):
    for ab in range(9):
        for slot, s in enumerate(MIDDLE):
            for jp in range(2):
                c = jp + 2 - s
                if 0 <= c <= 2:
                    piece = flat[:, (ab * 3 + c) * 128 : (ab * 3 + c + 1) * 128]
                else:
                    piece = jnp.zeros((OWN, 128), BF16)
                filters[ab, slot * OWN : (slot + 1) * OWN, jp * 128 : (jp + 1) * 128] = piece
    lane = lax.broadcasted_iota(jnp.int32, (192, 2 * OWN), 1)
    up = one_hot(192, 192, lambda r: jnp.where(r % 16 == 15, -1, r + 1))
    down = one_hot(192, 192, lambda r: jnp.where(r % 16 == 0, -1, r - 1))
    for f in range(FRAMES + 2):
        src = grad[f] if f < FRAMES else following[f - FRAMES]
        wide[f * SPAN : (f + 1) * SPAN, :, : 2 * OWN] = src
    for g in range(0, (FRAMES + 2) * SPAN, 12):
        block = wide[g : g + 12, :, : 2 * OWN].reshape(192, 2 * OWN)
        moved = jnp.where(lane < OWN, mm(up, block), mm(down, block)).astype(BF16)
        wide[g : g + 12, :, 2 * OWN :] = moved.reshape(12, 16, 2 * OWN)
    total = jnp.zeros((FRAMES * ROWS * 16, 256), F32)
    for a in range(3):
        for b in range(3):
            tops = [(f + 2 - a) * SPAN + 2 - b for f in range(FRAMES)]
            win = jnp.concatenate([wide[x : x + ROWS] for x in tops], 0)
            total = total + mm(win.reshape(FRAMES * ROWS * 16, 4 * OWN), filters[a * 3 + b])
    total = total.reshape(FRAMES, ROWS, 16, 256)
    first = lax.axis_index("tm") % 2 == 0
    keep[...] = jnp.where(first, total[:2], total[2:])
    send[...] = jnp.where(first, total[2:], total[:2]).astype(BF16)


def halve_kernel(kept, got, keep, send):
    total = kept[...] + got[...].astype(F32)
    even = lax.axis_index("height") % CORES == 0
    keep[...] = jnp.where(even, total[:, :4], total[:, 4:])
    send[...] = jnp.where(even, total[:, 4:], total[:, :4])


def join_kernel(kept, got, out, mark):
    total = (kept[...] + got[...]).astype(BF16).reshape(128, 256)
    low = one_hot(256, 128, lambda r: jnp.where(r % 2 == 0, (r // 32) * 16 + (r % 32) // 2, -1))
    high = one_hot(256, 128, lambda r: jnp.where(r % 2 == 1, (r // 32) * 16 + (r % 32) // 2, -1))
    moved = mm(low, total[:, :128]) + mm(high, total[:, 128:])
    out[...] = moved.astype(BF16).reshape(out.shape)
    mark[...] = jnp.zeros_like(mark)


def inside(pairs, count):
    return [(i, k) for i, k in pairs if 0 <= k < count]


def body(clip, first_filter, second_filter, upstream):
    frames, rows, width, cin = clip.shape
    chans = first_filter.shape[4]
    tms, heights = lax.axis_size("tm"), lax.axis_size("height")
    lines = tms // 2
    siblings = [(i, i ^ 1) for i in range(heights)]
    blocks = [(t, t ^ 1) for t in range(tms)]

    here, edge = call(
        stack_kernel,
        [shaped((10, 32, 128), BF16), shaped((5, 32, 128), BF16)],
        [clip, upstream],
    )
    near_pairs = inside([(i, i + 1 if i % 2 else i - 1) for i in range(heights)], heights)
    edge = lax.ppermute(edge, "height", near_pairs)

    second = jnp.swapaxes(second_filter, 3, 4).reshape(27, chans // heights, chans)
    (pieces,) = call(
        filter_pieces_kernel,
        [shaped((heights, chans // heights, 27 * OWN), BF16)],
        [second],
        flops=2 * 27 * 16 * 256 * 128,
    )

    here, pieces = call(
        append_kernel,
        [shaped((15, 32, 128), BF16), shaped(pieces.shape, BF16)],
        [here, edge, pieces],
        scratch=[pltpu.SemaphoreType.DMA((2,))],
        idle=(0, 1, 2),
        alias={2: 1},
    )
    pair = lax.ppermute(here, "tm", blocks)
    forward, backward, pieces = call(
        choose_kernel,
        [shaped((12, 32, 128), BF16), shaped((3, 32, 128), BF16), shaped(pieces.shape, BF16)],
        [here, pair, pieces],
        idle=(2,),
        alias={2: 2},
    )
    second = lax.all_to_all(pieces, "height", 0, 0).reshape(chans, 27 * OWN)
    forth = inside([(t, t + 2) for t in range(tms)], tms)
    back = inside([(t, t - 2) for t in range(tms)], tms)
    before = lax.ppermute(forward, "tm", forth)
    after = lax.ppermute(backward, "tm", back)

    first = first_filter.reshape(27 * cin, chans)
    band, flat = call(
        own_filter_kernel,
        [shaped((3, 512, 6 * OWN), BF16), shaped((OWN, 27 * cin), BF16)],
        [first],
        flops=3 * 27 * 128 * 256 * 128,
    )

    (packed,) = call(
        pack_kernel, [shaped((45, 32, 128), BF16)], [here, pair, before, after]
    )
    other = lax.ppermute(packed, "height", siblings)

    units, up_units = 6 * HIGH, 3 * HALF_HIGH
    wide, ups, pre = call(
        preact_kernel,
        [
            shaped((units, 16, 512), BF16),
            shaped((2, up_units, 16, 256), BF16),
            shaped((2, 2, 2, HALF, 16, 2 * OWN), F32),
        ],
        [packed, other, band],
        scratch=[pltpu.VMEM((units, 32, 128), BF16), pltpu.VMEM((up_units, 16, 256), BF16)],
        flops=2 * 640 * 9 * 512 * 128,
    )
    grad_pre, parts = call(
        gradient_kernel,
        [shaped((FRAMES, SPAN, 16, 2 * OWN), BF16), shaped((heights, 7, 16, cin), BF16)],
        [second, ups, pre, wide],
        flops=2 * 512 * 9 * 512 * 128,
    )

    planes = [
        [(2 * z + x) * heights + CORES * g + core for x in range(2) for g in range(heights // 2)]
        for z in range(lines)
        for core in range(CORES)
    ]
    parts = lax.all_to_all(parts, ("tm", "height"), 0, 0, axis_index_groups=planes)
    following = lax.ppermute(grad_pre[:2], "tm", back)
    keep, send = call(
        clip_kernel,
        [shaped((2, ROWS, 16, 2 * cin), F32), shaped((2, ROWS, 16, 2 * cin), BF16)],
        [grad_pre, following, flat],
        scratch=[
            pltpu.VMEM(((FRAMES + 2) * SPAN, 16, 4 * OWN), BF16),
            pltpu.VMEM((9, 4 * OWN, 2 * cin), BF16),
        ],
        flops=2 * 512 * 9 * 256 * 256,
    )

    (sums,) = call(
        sum_turn_kernel,
        [shaped((lines, 16, 128), BF16)],
        [parts, send],
        idle=(1,),
    )
    columns = [[2 * ((i + 8) % lines) + x for i in range(lines)] for x in range(2)]
    summed = lax.all_to_all(sums, "tm", 0, 0, axis_index_groups=columns)
    got = lax.ppermute(send, "tm", blocks)
    keep, send = call(
        halve_kernel,
        [shaped((2, rows, 16, 2 * cin), F32)] * 2,
        [keep, got],
    )
    got = lax.ppermute(send, "height", siblings)
    grad_clip, mark = call(
        join_kernel, [shaped(clip.shape, BF16), shaped((8, 128), F32)], [keep, got]
    )
    count = frames * tms * rows * heights * width
    (grad_filter,) = call(
        functools.partial(finish_kernel, 1.0 / float(count) ** 0.5),
        [shaped((27, cin // tms, chans // heights), F32)],
        [summed, mark],
        idle=(1,),
    )
    grad_filter = grad_filter.reshape(3, 3, 3, cin // tms, chans // heights)
    return (grad_clip, grad_filter)


def solution(mesh):
    in_specs = (
        P("tm", "height", None, None),
        P(),
        P(None, None, None, None, "height"),
        P("tm", "height", None, None),
    )
    out_specs = (P("tm", "height", None, None), P(None, None, None, "tm", "height"))
    return jax.shard_map(body, mesh=mesh, in_specs=in_specs, out_specs=out_specs, check_vma=False)
```

```python
import functools

import jax
import jax.numpy as jnp
from jax import lax
from jax.experimental import pallas as pl
from jax.experimental.pallas import tpu as pltpu
from jax.sharding import PartitionSpec as P

F32, BF16 = jnp.float32, jnp.bfloat16
CORES = 2
OWN = 64
FRAMES = 4
ROWS, SPAN = 8, 10
HIGH, HALF_HIGH, HALF = ROWS + 4, ROWS // 2 + 2, SPAN // 2
MIDDLE = (1, 2, 3, 0)

LONG = {0: ((2, 0),), 1: ((0, 0), (1, 1))}
WIDE = {0: ((1, 0), (2, 1)), 1: ((0, 1),)}


def shift_classes():
    classes = []
    for t in (1, 0):
        for h in (1, 0):
            for w in (0, 1):
                taps = tuple(
                    ((a, b, c), (fp, ip, jp))
                    for a, fp in LONG[t]
                    for b, ip in LONG[h]
                    for c, jp in WIDE[w]
                )
                classes.append(((t, h, w), taps))
    return classes


CLASSES = shift_classes()
TAP_ORDER = [tap for _, taps in CLASSES for tap, _ in taps]


def mm(lhs, rhs):
    return jnp.dot(lhs, rhs, preferred_element_type=F32)


def one_hot(rows, cols, column_of):
    row = lax.broadcasted_iota(jnp.int32, (rows, cols), 0)
    col = lax.broadcasted_iota(jnp.int32, (rows, cols), 1)
    return jnp.where(column_of(row) == col, 1.0, 0.0).astype(BF16)


def call(kernel, out, args, scratch=(), idle=(), alias=None, flops=0, limit=16):
    spec = pl.BlockSpec(memory_space=pltpu.VMEM)
    far = pl.BlockSpec(memory_space=pl.ANY)
    moved = sum(x.size * x.dtype.itemsize for x in list(args) + list(out))
    return pl.pallas_call(
        kernel,
        out_shape=tuple(out),
        in_specs=[far if i in idle else spec for i in range(len(args))],
        out_specs=tuple([far if i in (alias or {}).values() else spec for i in range(len(out))]),
        input_output_aliases=dict(alias or {}),
        scratch_shapes=list(scratch),
        compiler_params=pltpu.CompilerParams(vmem_limit_bytes=limit * 1024 * 1024),
        cost_estimate=pl.CostEstimate(flops=flops, bytes_accessed=moved, transcendentals=0),
    )(*args)


def shaped(shape, dtype):
    return jax.ShapeDtypeStruct(shape, dtype)


def own_channel(place, x, core):
    return (2 * (place // 8) + core) * 16 + 8 * x + place % 8


def filter_pieces_kernel(second, out):
    taps, depth, chans = second.shape
    x = lax.axis_index("tm") % 2
    row = lax.broadcasted_iota(jnp.int32, (chans, 2 * OWN), 0)
    col = lax.broadcasted_iota(jnp.int32, (chans, 2 * OWN), 1)
    order = jnp.where(own_channel(col % OWN, x, col // OWN) == row, 1.0, 0.0).astype(BF16)
    moved = mm(second[...].reshape(taps * depth, chans), order).astype(BF16)
    moved = moved.reshape(taps, depth, 2 * OWN)
    for place in range(0, len(TAP_ORDER), 2):
        pair = TAP_ORDER[place : place + 2]
        for core in range(CORES):
            lanes = slice(core * OWN, (core + 1) * OWN)
            piece = jnp.concatenate([moved[a * 9 + b * 3 + c, :, lanes] for a, b, c in pair], 1)
            for p in range(core, out.shape[0], CORES):
                out[p, :, place * OWN : place * OWN + piece.shape[1]] = piece


def own_filter_kernel(first, band, flat):
    chans = first.shape[1]
    x, core = lax.axis_index("tm") % 2, lax.axis_index("height") % CORES
    row = lax.broadcasted_iota(jnp.int32, (chans, 2 * OWN), 0)
    col = lax.broadcasted_iota(jnp.int32, (chans, 2 * OWN), 1)
    pick = jnp.where(own_channel(col % OWN, x, core) == row, 1.0, 0.0).astype(BF16)
    twice = mm(first[...], pick)
    lane = lax.broadcasted_iota(jnp.int32, (128, 2 * OWN), 1)
    for ab in range(9):
        lanes = slice((ab % 3) * 128, (ab % 3 + 1) * 128)
        for s in range(4):
            left = twice[(ab * 3 + s) * 128 : (ab * 3 + s + 1) * 128] if s < 3 else 0.0
            right = twice[(ab * 3 + s - 1) * 128 : (ab * 3 + s) * 128] if s > 0 else 0.0
            both = jnp.where(lane < OWN, left, right)
            band[ab // 3, s * 128 : (s + 1) * 128, lanes] = both.astype(BF16)
    row = lax.broadcasted_iota(jnp.int32, (OWN, chans), 0)
    col = lax.broadcasted_iota(jnp.int32, (OWN, chans), 1)
    pick = jnp.where(own_channel(row, x, core) == col, 1.0, 0.0).astype(BF16)
    flat[...] = lax.dot_general(
        pick, first[...], (((1,), (1,)), ((), ())), preferred_element_type=F32
    ).astype(BF16)


def stack_kernel(clip, up, here, edge):
    at_top = lax.axis_index("height") % CORES == 0
    for f in range(2):
        here[4 * f : 4 * f + 4] = clip[f]
        edge[2 * f : 2 * f + 2] = jnp.where(at_top, clip[f, :2], clip[f, 2:])
    for half in range(2):
        subs = slice(16 * half, 16 * half + 16)
        src = up[0, :, :, 128 * half : 128 * half + 128]
        here[8:10, subs] = src
        edge[4, subs] = jnp.where(at_top, src[0], src[1])


def append_kernel(here, edge, _, out, __, sems):
    copies = [
        pltpu.make_async_copy(here, out.at[:10], sems.at[0]),
        pltpu.make_async_copy(edge, out.at[10:], sems.at[1]),
    ]
    for copy in copies:
        copy.start()
    for copy in copies:
        copy.wait()


def choose_kernel(here, pair, _, forward, backward, __):
    first = lax.axis_index("tm") % 2 == 0
    forward[:8] = jnp.where(first, pair[:8], here[:8])
    forward[8:12] = jnp.where(first, pair[10:14], here[10:14])
    backward[:2] = jnp.where(first, here[8:10], pair[8:10])
    backward[2] = jnp.where(first, here[14], pair[14])


def pack_kernel(here, pair, before, after, packed):
    first = lax.axis_index("tm") % 2 == 0
    one = jnp.where(first, here[...], pair[...])
    two = jnp.where(first, pair[...], here[...])
    packed[:8] = before[:8]
    packed[30:34] = before[8:12]
    for k, src in ((1, one), (2, two)):
        packed[8 * k : 8 * k + 8] = src[:8]
        packed[30 + 4 * k : 34 + 4 * k] = src[10:14]
    for t, src in enumerate((one[8:10], two[8:10], after[:2])):
        packed[24 + 2 * t : 26 + 2 * t] = src
    for t, src in enumerate((one[14], two[14], after[2])):
        packed[42 + t] = src


def preact_kernel(own, other, filters, wide, ups, pre, band, ext):
    member = lax.axis_index("height") % CORES
    even = member == 0
    above = jnp.where(even, own[30:45], other[30:45])
    below = jnp.where(even, other[30:45], own[30:45])
    for f in range(6):
        base = f * HIGH
        band[pl.ds(base + 2 + 4 * member, 4)] = own[4 * f : 4 * f + 4]
        band[pl.ds(base + 6 - 4 * member, 4)] = other[4 * f : 4 * f + 4]
        band[base : base + 2] = above[2 * f : 2 * f + 2]
        band[base + ROWS + 2 : base + ROWS + 4] = below[2 * f : 2 * f + 2]
    for t in range(3):
        base, unit = t * HALF_HIGH, 24 + 2 * t
        for half in range(2):
            lanes = slice(128 * half, 128 * half + 128)
            subs = slice(16 * half, 16 * half + 16)
            ext[pl.ds(base + 1 + 2 * member, 2), :, lanes] = own[unit : unit + 2, subs]
            ext[pl.ds(base + 3 - 2 * member, 2), :, lanes] = other[unit : unit + 2, subs]
            ext[base, :, lanes] = above[12 + t, subs]
            ext[base + HALF_HIGH - 1, :, lanes] = below[12 + t, subs]
    units = ext.shape[0]
    flat = ext[...].reshape(units * 16, 256)
    shift = one_hot(units * 16, units * 16, lambda r: jnp.where(r % 16 == 15, -1, r + 1))
    ups[0] = flat.reshape(units, 16, 256)
    ups[1] = mm(shift, flat).astype(BF16).reshape(units, 16, 256)

    def column(r):
        s, unit, w = r // 128, (r // 16) % 8, 2 * (r % 16) + r // 128 - 1
        return jnp.where((w >= 0) & (w < 32), unit * 32 + w, -1)

    matrix = one_hot(512, 256, column)
    for g in range(band.shape[0] // 8):
        moved = mm(matrix, band[8 * g : 8 * g + 8].reshape(256, 128)).astype(BF16)
        for s in range(4):
            piece = moved[128 * s : 128 * s + 128].reshape(8, 16, 128)
            wide[8 * g : 8 * g + 8, :, s * 128 : (s + 1) * 128] = piece
    total = jnp.zeros((FRAMES, SPAN, 16, 2 * OWN), F32)
    for a in range(3):
        tops = [(a + f) * HIGH for f in range(FRAMES)]
        win = jnp.concatenate([wide[x : x + SPAN + 1] for x in tops], 0)
        prod = mm(win.reshape(FRAMES * (SPAN + 1) * 16, 512), filters[a, :, : 4 * OWN])
        prod = prod.reshape(FRAMES, SPAN + 1, 16, 4 * OWN)
        total = total + prod[:, :SPAN, :, : 2 * OWN] + prod[:, 1:, :, 2 * OWN :]
        win = jnp.concatenate([wide[x + 2 : x + 2 + SPAN] for x in tops], 0)
        prod = mm(win.reshape(FRAMES * SPAN * 16, 512), filters[a, :, 4 * OWN :])
        total = total + prod.reshape(FRAMES, SPAN, 16, 2 * OWN)
    for f in range(FRAMES):
        for r in range(SPAN):
            pre[f % 2, r % 2, f // 2, r // 2] = total[f, r]


def gradient_kernel(second, ups, pre, wide, grad, parts):
    group = lax.axis_index("height") // CORES
    first_band = group == 0
    last_band = group == lax.axis_size("height") // CORES - 1
    even, odd = {}, {}
    offset = 0
    for (t, h, w), taps in CLASSES:
        tops = [(t + q) * HALF_HIGH + h for q in range(2)]
        lhs = jnp.concatenate([ups[w, x : x + HALF] for x in tops], 0).reshape(32 * HALF, 256)
        prod = mm(lhs, second[:, offset : offset + len(taps) * OWN])
        offset += len(taps) * OWN
        total, step = (odd, 1) if w else (even, 2)
        for k in range(0, len(taps), step):
            key = taps[k][1][:2]
            piece = prod[:, k * OWN : (k + step) * OWN]
            total[key] = total[key] + piece if key in total else piece
    blank = jnp.zeros((32 * HALF, OWN), F32)
    for (fp, ip), act in even.items():
        act = act + jnp.concatenate([blank, odd[fp, ip]], 1)
        x = pre[fp, ip].reshape(32 * HALF, 2 * OWN)
        sig = jax.nn.sigmoid(x)
        g = (act * sig * (1.0 + x * (1.0 - sig))).reshape(2, HALF, 16, 2 * OWN)
        for q in range(2):
            for p in range(HALF):
                piece, r = g[q, p], 2 * p + ip
                if r == 0:
                    piece = jnp.where(first_band, 0.0, piece)
                if r == SPAN - 1:
                    piece = jnp.where(last_band, 0.0, piece)
                grad[2 * q + fp, r] = piece.astype(BF16)
    turned = grad[:, 1 : 1 + ROWS].reshape(FRAMES * ROWS * 16, 2 * OWN).T
    blank = jnp.zeros((2 * OWN, 128), BF16)
    turned = jnp.concatenate([blank, turned, blank], 1)
    sums = {}
    for pair in (0, 2, 4):
        taps = [a for a in range(3) if 0 <= pair - a + 1 <= FRAMES]
        lhs = [turned[:, (pair - a + 1) * 128 : (pair - a + 3) * 128] for a in taps]
        lhs = jnp.concatenate(lhs, 0)
        for b in range(3):
            tops = [(pair + f) * HIGH + 1 + b for f in range(2)]
            win = jnp.concatenate([wide[x : x + ROWS] for x in tops], 0)
            prod = mm(lhs, win.reshape(256, 512))
            for k, a in enumerate(taps):
                rows = prod[k * 2 * OWN : (k + 1) * 2 * OWN]
                sums[a, b] = sums[a, b] + rows if (a, b) in sums else rows
    strips = []
    for a in range(3):
        for b in range(3):
            for c in range(3):
                piece = sums[a, b][:OWN, 128 * c : 128 * c + 128]
                piece = piece + sums[a, b][OWN:, 128 * c + 128 : 128 * c + 256]
                strips.append(piece.astype(BF16))
    strips.append(jnp.zeros_like(strips[0]))
    row = lax.broadcasted_iota(jnp.int32, (256, 256), 0)
    col = lax.broadcasted_iota(jnp.int32, (256, 256), 1)
    x, tap, z, e = col // 128, (col // 64) % 2, (col // 4) % 16, col % 4
    order = jnp.where(tap * 128 + 8 * z + 4 * x + e == row, 1.0, 0.0).astype(BF16)
    pairs = [jnp.concatenate(strips[i : i + 2], 1) for i in range(0, 28, 2)]
    moved = mm(jnp.concatenate(pairs, 0), order)
    blocks = OWN // 8
    for k in range(7):
        both = [moved[i * OWN : (i + 1) * OWN].reshape(blocks, 8, 256) for i in (2 * k, 2 * k + 1)]
        both = jnp.concatenate(both, 1).astype(BF16)
        for x in range(2):
            parts[x * blocks : (x + 1) * blocks, k] = both[:, :, 128 * x : 128 * x + 128]


def sum_turn_kernel(parts, _, out):
    blank = jnp.zeros((16, 128), F32)
    blocks = parts.shape[0] // 2
    halves = []
    for x in range(2):
        total = parts[x * blocks].astype(F32)
        for i in range(1, blocks):
            total = total + parts[x * blocks + i].astype(F32)
        halves += [total.reshape(112, 128), blank]
    flat = jnp.concatenate(halves, 0).T
    for i in range(16):
        z = (i + 8) % 16
        rows = [(tap * 64 + z * 4, x) for x in range(2) for tap in range(2)]
        block = [flat[r : r + 4, 128 * x : 128 * x + 128] for r, x in rows]
        out[i] = jnp.concatenate(block, 0).astype(BF16)


def finish_kernel(scale, parts, _, out):
    total = parts[0].astype(F32)
    for i in range(1, parts.shape[0]):
        total = total + parts[i].astype(F32)
    total = total * scale
    for k in range(27):
        lanes = slice(8 * (k // 2), 8 * (k // 2) + 8)
        rows = [8 * x + 4 * (k % 2) for x in range(2)]
        out[k] = jnp.concatenate([total[r : r + 4, lanes] for r in rows], 1)


def clip_kernel(grad, following, flat, keep, send, wide, filters):
    for ab in range(9):
        for slot, s in enumerate(MIDDLE):
            for jp in range(2):
                c = jp + 2 - s
                if 0 <= c <= 2:
                    piece = flat[:, (ab * 3 + c) * 128 : (ab * 3 + c + 1) * 128]
                else:
                    piece = jnp.zeros((OWN, 128), BF16)
                filters[ab, slot * OWN : (slot + 1) * OWN, jp * 128 : (jp + 1) * 128] = piece
    lane = lax.broadcasted_iota(jnp.int32, (192, 2 * OWN), 1)
    up = one_hot(192, 192, lambda r: jnp.where(r % 16 == 15, -1, r + 1))
    down = one_hot(192, 192, lambda r: jnp.where(r % 16 == 0, -1, r - 1))
    for f in range(FRAMES + 2):
        src = grad[f] if f < FRAMES else following[f - FRAMES]
        wide[f * SPAN : (f + 1) * SPAN, :, : 2 * OWN] = src
    for g in range(0, (FRAMES + 2) * SPAN, 12):
        block = wide[g : g + 12, :, : 2 * OWN].reshape(192, 2 * OWN)
        moved = jnp.where(lane < OWN, mm(up, block), mm(down, block)).astype(BF16)
        wide[g : g + 12, :, 2 * OWN :] = moved.reshape(12, 16, 2 * OWN)
    total = jnp.zeros((FRAMES * ROWS * 16, 256), F32)
    for a in range(3):
        for b in range(3):
            tops = [(f + 2 - a) * SPAN + 2 - b for f in range(FRAMES)]
            win = jnp.concatenate([wide[x : x + ROWS] for x in tops], 0)
            total = total + mm(win.reshape(FRAMES * ROWS * 16, 4 * OWN), filters[a * 3 + b])
    total = total.reshape(FRAMES, ROWS, 16, 256)
    first = lax.axis_index("tm") % 2 == 0
    keep[...] = jnp.where(first, total[:2], total[2:])
    send[...] = jnp.where(first, total[2:], total[:2]).astype(BF16)


def halve_kernel(kept, got, keep, send):
    total = kept[...] + got[...].astype(F32)
    even = lax.axis_index("height") % CORES == 0
    keep[...] = jnp.where(even, total[:, :4], total[:, 4:])
    send[...] = jnp.where(even, total[:, 4:], total[:, :4])


def join_kernel(kept, got, out, mark):
    total = (kept[...] + got[...]).astype(BF16).reshape(128, 256)
    low = one_hot(256, 128, lambda r: jnp.where(r % 2 == 0, (r // 32) * 16 + (r % 32) // 2, -1))
    high = one_hot(256, 128, lambda r: jnp.where(r % 2 == 1, (r // 32) * 16 + (r % 32) // 2, -1))
    moved = mm(low, total[:, :128]) + mm(high, total[:, 128:])
    out[...] = moved.astype(BF16).reshape(out.shape)
    mark[...] = jnp.zeros_like(mark)


def inside(pairs, count):
    return [(i, k) for i, k in pairs if 0 <= k < count]


def body(clip, first_filter, second_filter, upstream):
    frames, rows, width, cin = clip.shape
    chans = first_filter.shape[4]
    tms, heights = lax.axis_size("tm"), lax.axis_size("height")
    lines = tms // 2
    siblings = [(i, i ^ 1) for i in range(heights)]
    blocks = [(t, t ^ 1) for t in range(tms)]

    here, edge = call(
        stack_kernel,
        [shaped((10, 32, 128), BF16), shaped((5, 32, 128), BF16)],
        [clip, upstream],
    )
    near_pairs = inside([(i, i + 1 if i % 2 else i - 1) for i in range(heights)], heights)
    edge = lax.ppermute(edge, "height", near_pairs)

    second = jnp.swapaxes(second_filter, 3, 4).reshape(27, chans // heights, chans)
    (pieces,) = call(
        filter_pieces_kernel,
        [shaped((heights, chans // heights, 27 * OWN), BF16)],
        [second],
        flops=2 * 27 * 16 * 256 * 128,
    )

    here, pieces = call(
        append_kernel,
        [shaped((15, 32, 128), BF16), shaped(pieces.shape, BF16)],
        [here, edge, pieces],
        scratch=[pltpu.SemaphoreType.DMA((2,))],
        idle=(0, 1, 2),
        alias={2: 1},
    )
    pair = lax.ppermute(here, "tm", blocks)
    forward, backward, pieces = call(
        choose_kernel,
        [shaped((12, 32, 128), BF16), shaped((3, 32, 128), BF16), shaped(pieces.shape, BF16)],
        [here, pair, pieces],
        idle=(2,),
        alias={2: 2},
    )
    second = lax.all_to_all(pieces, "height", 0, 0).reshape(chans, 27 * OWN)
    forth = inside([(t, t + 2) for t in range(tms)], tms)
    back = inside([(t, t - 2) for t in range(tms)], tms)
    before = lax.ppermute(forward, "tm", forth)
    after = lax.ppermute(backward, "tm", back)

    first = first_filter.reshape(27 * cin, chans)
    band, flat = call(
        own_filter_kernel,
        [shaped((3, 512, 6 * OWN), BF16), shaped((OWN, 27 * cin), BF16)],
        [first],
        flops=3 * 27 * 128 * 256 * 128,
    )

    (packed,) = call(
        pack_kernel, [shaped((45, 32, 128), BF16)], [here, pair, before, after]
    )
    other = lax.ppermute(packed, "height", siblings)

    units, up_units = 6 * HIGH, 3 * HALF_HIGH
    wide, ups, pre = call(
        preact_kernel,
        [
            shaped((units, 16, 512), BF16),
            shaped((2, up_units, 16, 256), BF16),
            shaped((2, 2, 2, HALF, 16, 2 * OWN), F32),
        ],
        [packed, other, band],
        scratch=[pltpu.VMEM((units, 32, 128), BF16), pltpu.VMEM((up_units, 16, 256), BF16)],
        flops=2 * 640 * 9 * 512 * 128,
    )
    grad_pre, parts = call(
        gradient_kernel,
        [shaped((FRAMES, SPAN, 16, 2 * OWN), BF16), shaped((heights, 7, 16, cin), BF16)],
        [second, ups, pre, wide],
        flops=2 * 512 * 9 * 512 * 128,
    )

    planes = [
        [(2 * z + x) * heights + CORES * g + core for x in range(2) for g in range(heights // 2)]
        for z in range(lines)
        for core in range(CORES)
    ]
    parts = lax.all_to_all(parts, ("tm", "height"), 0, 0, axis_index_groups=planes)
    following = lax.ppermute(grad_pre[:2], "tm", back)
    keep, send = call(
        clip_kernel,
        [shaped((2, ROWS, 16, 2 * cin), F32), shaped((2, ROWS, 16, 2 * cin), BF16)],
        [grad_pre, following, flat],
        scratch=[
            pltpu.VMEM(((FRAMES + 2) * SPAN, 16, 4 * OWN), BF16),
            pltpu.VMEM((9, 4 * OWN, 2 * cin), BF16),
        ],
        flops=2 * 512 * 9 * 256 * 256,
    )

    (sums,) = call(
        sum_turn_kernel,
        [shaped((lines, 16, 128), BF16)],
        [parts, send],
        idle=(1,),
    )
    columns = [[2 * ((i + 8) % lines) + x for i in range(lines)] for x in range(2)]
    summed = lax.all_to_all(sums, "tm", 0, 0, axis_index_groups=columns)
    got = lax.ppermute(send, "tm", blocks)
    keep, send = call(
        halve_kernel,
        [shaped((2, rows, 16, 2 * cin), F32)] * 2,
        [keep, got],
    )
    got = lax.ppermute(send, "height", siblings)
    grad_clip, mark = call(
        join_kernel, [shaped(clip.shape, BF16), shaped((8, 128), F32)], [keep, got]
    )
    count = frames * tms * rows * heights * width
    (grad_filter,) = call(
        functools.partial(finish_kernel, 1.0 / float(count) ** 0.5),
        [shaped((27, cin // tms, chans // heights), F32)],
        [summed, mark],
        idle=(1,),
    )
    grad_filter = grad_filter.reshape(3, 3, 3, cin // tms, chans // heights)
    return (grad_clip, grad_filter)


def solution(mesh):
    in_specs = (
        P("tm", "height", None, None),
        P(),
        P(None, None, None, None, "height"),
        P("tm", "height", None, None),
    )
    out_specs = (P("tm", "height", None, None), P(None, None, None, "tm", "height"))
    return jax.shard_map(body, mesh=mesh, in_specs=in_specs, out_specs=out_specs, check_vma=False)
```

```python
import functools

import jax
import jax.numpy as jnp
from jax import lax
from jax.experimental import pallas as pl
from jax.experimental.pallas import tpu as pltpu
from jax.sharding import PartitionSpec as P

F32, BF16 = jnp.float32, jnp.bfloat16
CORES = 2
OWN = 64
FRAMES = 4
ROWS, SPAN = 8, 10
HIGH, HALF_HIGH, HALF = ROWS + 4, ROWS // 2 + 2, SPAN // 2
MIDDLE = (1, 2, 3, 0)

LONG = {0: ((2, 0),), 1: ((0, 0), (1, 1))}
WIDE = {0: ((1, 0), (2, 1)), 1: ((0, 1),)}


def shift_classes():
    classes = []
    for t in (1, 0):
        for h in (1, 0):
            for w in (0, 1):
                taps = tuple(
                    ((a, b, c), (fp, ip, jp))
                    for a, fp in LONG[t]
                    for b, ip in LONG[h]
                    for c, jp in WIDE[w]
                )
                classes.append(((t, h, w), taps))
    return classes


CLASSES = shift_classes()
TAP_ORDER = [tap for _, taps in CLASSES for tap, _ in taps]


def mm(lhs, rhs):
    return jnp.dot(lhs, rhs, preferred_element_type=F32)


def one_hot(rows, cols, column_of):
    row = lax.broadcasted_iota(jnp.int32, (rows, cols), 0)
    col = lax.broadcasted_iota(jnp.int32, (rows, cols), 1)
    return jnp.where(column_of(row) == col, 1.0, 0.0).astype(BF16)


def call(kernel, out, args, scratch=(), idle=(), alias=None, flops=0, limit=16):
    spec = pl.BlockSpec(memory_space=pltpu.VMEM)
    far = pl.BlockSpec(memory_space=pl.ANY)
    moved = sum(x.size * x.dtype.itemsize for x in list(args) + list(out))
    return pl.pallas_call(
        kernel,
        out_shape=tuple(out),
        in_specs=[far if i in idle else spec for i in range(len(args))],
        out_specs=tuple([far if i in (alias or {}).values() else spec for i in range(len(out))]),
        input_output_aliases=dict(alias or {}),
        scratch_shapes=list(scratch),
        compiler_params=pltpu.CompilerParams(vmem_limit_bytes=limit * 1024 * 1024),
        cost_estimate=pl.CostEstimate(flops=flops, bytes_accessed=moved, transcendentals=0),
    )(*args)


def shaped(shape, dtype):
    return jax.ShapeDtypeStruct(shape, dtype)


def own_channel(place, x, core):
    return (2 * (place // 8) + core) * 16 + 8 * x + place % 8


def filter_pieces_kernel(second, out):
    taps, depth, chans = second.shape
    x = lax.axis_index("tm") % 2
    row = lax.broadcasted_iota(jnp.int32, (chans, 2 * OWN), 0)
    col = lax.broadcasted_iota(jnp.int32, (chans, 2 * OWN), 1)
    order = jnp.where(own_channel(col % OWN, x, col // OWN) == row, 1.0, 0.0).astype(BF16)
    moved = mm(second[...].reshape(taps * depth, chans), order).astype(BF16)
    moved = moved.reshape(taps, depth, 2 * OWN)
    for place in range(0, len(TAP_ORDER), 2):
        pair = TAP_ORDER[place : place + 2]
        for core in range(CORES):
            lanes = slice(core * OWN, (core + 1) * OWN)
            piece = jnp.concatenate([moved[a * 9 + b * 3 + c, :, lanes] for a, b, c in pair], 1)
            for p in range(core, out.shape[0], CORES):
                out[p, :, place * OWN : place * OWN + piece.shape[1]] = piece


def own_filter_kernel(first, band, flat):
    chans = first.shape[1]
    x, core = lax.axis_index("tm") % 2, lax.axis_index("height") % CORES
    row = lax.broadcasted_iota(jnp.int32, (chans, 2 * OWN), 0)
    col = lax.broadcasted_iota(jnp.int32, (chans, 2 * OWN), 1)
    pick = jnp.where(own_channel(col % OWN, x, core) == row, 1.0, 0.0).astype(BF16)
    twice = mm(first[...], pick)
    lane = lax.broadcasted_iota(jnp.int32, (128, 2 * OWN), 1)
    for ab in range(9):
        lanes = slice((ab % 3) * 128, (ab % 3 + 1) * 128)
        for s in range(4):
            left = twice[(ab * 3 + s) * 128 : (ab * 3 + s + 1) * 128] if s < 3 else 0.0
            right = twice[(ab * 3 + s - 1) * 128 : (ab * 3 + s) * 128] if s > 0 else 0.0
            both = jnp.where(lane < OWN, left, right)
            band[ab // 3, s * 128 : (s + 1) * 128, lanes] = both.astype(BF16)
    row = lax.broadcasted_iota(jnp.int32, (OWN, chans), 0)
    col = lax.broadcasted_iota(jnp.int32, (OWN, chans), 1)
    pick = jnp.where(own_channel(row, x, core) == col, 1.0, 0.0).astype(BF16)
    flat[...] = lax.dot_general(
        pick, first[...], (((1,), (1,)), ((), ())), preferred_element_type=F32
    ).astype(BF16)


def stack_kernel(clip, up, here, edge):
    at_top = lax.axis_index("height") % CORES == 0
    for f in range(2):
        here[4 * f : 4 * f + 4] = clip[f]
        edge[2 * f : 2 * f + 2] = jnp.where(at_top, clip[f, :2], clip[f, 2:])
    for half in range(2):
        subs = slice(16 * half, 16 * half + 16)
        src = up[0, :, :, 128 * half : 128 * half + 128]
        here[8:10, subs] = src
        edge[4, subs] = jnp.where(at_top, src[0], src[1])


def append_kernel(here, edge, _, out, __, sems):
    copies = [
        pltpu.make_async_copy(here, out.at[:10], sems.at[0]),
        pltpu.make_async_copy(edge, out.at[10:], sems.at[1]),
    ]
    for copy in copies:
        copy.start()
    for copy in copies:
        copy.wait()


def choose_kernel(here, pair, _, forward, backward, __):
    first = lax.axis_index("tm") % 2 == 0
    forward[:8] = jnp.where(first, pair[:8], here[:8])
    forward[8:12] = jnp.where(first, pair[10:14], here[10:14])
    backward[:2] = jnp.where(first, here[8:10], pair[8:10])
    backward[2] = jnp.where(first, here[14], pair[14])


def pack_kernel(here, pair, before, after, packed):
    first = lax.axis_index("tm") % 2 == 0
    one = jnp.where(first, here[...], pair[...])
    two = jnp.where(first, pair[...], here[...])
    packed[:8] = before[:8]
    packed[30:34] = before[8:12]
    for k, src in ((1, one), (2, two)):
        packed[8 * k : 8 * k + 8] = src[:8]
        packed[30 + 4 * k : 34 + 4 * k] = src[10:14]
    for t, src in enumerate((one[8:10], two[8:10], after[:2])):
        packed[24 + 2 * t : 26 + 2 * t] = src
    for t, src in enumerate((one[14], two[14], after[2])):
        packed[42 + t] = src


def preact_kernel(own, other, filters, wide, ups, pre, band, ext):
    member = lax.axis_index("height") % CORES
    even = member == 0
    above = jnp.where(even, own[30:45], other[30:45])
    below = jnp.where(even, other[30:45], own[30:45])
    for f in range(6):
        base = f * HIGH
        band[pl.ds(base + 2 + 4 * member, 4)] = own[4 * f : 4 * f + 4]
        band[pl.ds(base + 6 - 4 * member, 4)] = other[4 * f : 4 * f + 4]
        band[base : base + 2] = above[2 * f : 2 * f + 2]
        band[base + ROWS + 2 : base + ROWS + 4] = below[2 * f : 2 * f + 2]
    for t in range(3):
        base, unit = t * HALF_HIGH, 24 + 2 * t
        for half in range(2):
            lanes = slice(128 * half, 128 * half + 128)
            subs = slice(16 * half, 16 * half + 16)
            ext[pl.ds(base + 1 + 2 * member, 2), :, lanes] = own[unit : unit + 2, subs]
            ext[pl.ds(base + 3 - 2 * member, 2), :, lanes] = other[unit : unit + 2, subs]
            ext[base, :, lanes] = above[12 + t, subs]
            ext[base + HALF_HIGH - 1, :, lanes] = below[12 + t, subs]
    units = ext.shape[0]
    flat = ext[...].reshape(units * 16, 256)
    shift = one_hot(units * 16, units * 16, lambda r: jnp.where(r % 16 == 15, -1, r + 1))
    ups[0] = flat.reshape(units, 16, 256)
    ups[1] = mm(shift, flat).astype(BF16).reshape(units, 16, 256)

    def column(r):
        s, unit, w = r // 128, (r // 16) % 8, 2 * (r % 16) + r // 128 - 1
        return jnp.where((w >= 0) & (w < 32), unit * 32 + w, -1)

    matrix = one_hot(512, 256, column)
    for g in range(band.shape[0] // 8):
        moved = mm(matrix, band[8 * g : 8 * g + 8].reshape(256, 128)).astype(BF16)
        for s in range(4):
            piece = moved[128 * s : 128 * s + 128].reshape(8, 16, 128)
            wide[8 * g : 8 * g + 8, :, s * 128 : (s + 1) * 128] = piece
    total = jnp.zeros((FRAMES, SPAN, 16, 2 * OWN), F32)
    for a in range(3):
        tops = [(a + f) * HIGH for f in range(FRAMES)]
        win = jnp.concatenate([wide[x : x + SPAN + 1] for x in tops], 0)
        prod = mm(win.reshape(FRAMES * (SPAN + 1) * 16, 512), filters[a, :, : 4 * OWN])
        prod = prod.reshape(FRAMES, SPAN + 1, 16, 4 * OWN)
        total = total + prod[:, :SPAN, :, : 2 * OWN] + prod[:, 1:, :, 2 * OWN :]
        win = jnp.concatenate([wide[x + 2 : x + 2 + SPAN] for x in tops], 0)
        prod = mm(win.reshape(FRAMES * SPAN * 16, 512), filters[a, :, 4 * OWN :])
        total = total + prod.reshape(FRAMES, SPAN, 16, 2 * OWN)
    for f in range(FRAMES):
        for r in range(SPAN):
            pre[f % 2, r % 2, f // 2, r // 2] = total[f, r]


def gradient_kernel(second, ups, pre, wide, grad, parts):
    group = lax.axis_index("height") // CORES
    first_band = group == 0
    last_band = group == lax.axis_size("height") // CORES - 1
    even, odd = {}, {}
    offset = 0
    for (t, h, w), taps in CLASSES:
        tops = [(t + q) * HALF_HIGH + h for q in range(2)]
        lhs = jnp.concatenate([ups[w, x : x + HALF] for x in tops], 0).reshape(32 * HALF, 256)
        prod = mm(lhs, second[:, offset : offset + len(taps) * OWN])
        offset += len(taps) * OWN
        total, step = (odd, 1) if w else (even, 2)
        for k in range(0, len(taps), step):
            key = taps[k][1][:2]
            piece = prod[:, k * OWN : (k + step) * OWN]
            total[key] = total[key] + piece if key in total else piece
    blank = jnp.zeros((32 * HALF, OWN), F32)
    for (fp, ip), act in even.items():
        act = act + jnp.concatenate([blank, odd[fp, ip]], 1)
        x = pre[fp, ip].reshape(32 * HALF, 2 * OWN)
        sig = jax.nn.sigmoid(x)
        g = (act * sig * (1.0 + x * (1.0 - sig))).reshape(2, HALF, 16, 2 * OWN)
        for q in range(2):
            for p in range(HALF):
                piece, r = g[q, p], 2 * p + ip
                if r == 0:
                    piece = jnp.where(first_band, 0.0, piece)
                if r == SPAN - 1:
                    piece = jnp.where(last_band, 0.0, piece)
                grad[2 * q + fp, r] = piece.astype(BF16)
    turned = grad[:, 1 : 1 + ROWS].reshape(FRAMES * ROWS * 16, 2 * OWN).T
    strips = []
    for a in range(3):
        for b in range(3):
            tops = [(a + f) * HIGH + 1 + b for f in range(FRAMES)]
            win = jnp.concatenate([wide[x : x + ROWS] for x in tops], 0)
            prod = mm(turned, win.reshape(FRAMES * ROWS * 16, 512))
            for c in range(3):
                piece = prod[:OWN, 128 * c : 128 * c + 128]
                piece = piece + prod[OWN:, 128 * c + 128 : 128 * c + 256]
                strips.append(piece.astype(BF16))
    strips.append(jnp.zeros_like(strips[0]))
    row = lax.broadcasted_iota(jnp.int32, (256, 256), 0)
    col = lax.broadcasted_iota(jnp.int32, (256, 256), 1)
    x, tap, z, e = col // 128, (col // 64) % 2, (col // 4) % 16, col % 4
    order = jnp.where(tap * 128 + 8 * z + 4 * x + e == row, 1.0, 0.0).astype(BF16)
    blocks = OWN // 8
    for k in range(7):
        pairs = [jnp.concatenate(strips[i : i + 2], 1) for i in (4 * k, 4 * k + 2)]
        pairs = [mm(pair, order).reshape(blocks, 8, 256) for pair in pairs]
        both = jnp.concatenate(pairs, 1).astype(BF16)
        for x in range(2):
            parts[x * blocks : (x + 1) * blocks, k] = both[:, :, 128 * x : 128 * x + 128]


def sum_turn_kernel(parts, _, out):
    blank = jnp.zeros((16, 128), F32)
    blocks = parts.shape[0] // 2
    halves = []
    for x in range(2):
        total = parts[x * blocks].astype(F32)
        for i in range(1, blocks):
            total = total + parts[x * blocks + i].astype(F32)
        halves += [total.reshape(112, 128), blank]
    flat = jnp.concatenate(halves, 0).T
    for i in range(16):
        z = (i + 11) % 16
        rows = [(tap * 64 + z * 4, x) for x in range(2) for tap in range(2)]
        block = [flat[r : r + 4, 128 * x : 128 * x + 128] for r, x in rows]
        out[i] = jnp.concatenate(block, 0).astype(BF16)


def finish_kernel(scale, parts, _, out):
    total = parts[0].astype(F32)
    for i in range(1, parts.shape[0]):
        total = total + parts[i].astype(F32)
    total = total * scale
    for k in range(27):
        lanes = slice(8 * (k // 2), 8 * (k // 2) + 8)
        rows = [8 * x + 4 * (k % 2) for x in range(2)]
        out[k] = jnp.concatenate([total[r : r + 4, lanes] for r in rows], 1)


def clip_kernel(grad, following, flat, keep, send, wide, filters):
    for ab in range(9):
        for slot, s in enumerate(MIDDLE):
            for jp in range(2):
                c = jp + 2 - s
                if 0 <= c <= 2:
                    piece = flat[:, (ab * 3 + c) * 128 : (ab * 3 + c + 1) * 128]
                else:
                    piece = jnp.zeros((OWN, 128), BF16)
                filters[ab, slot * OWN : (slot + 1) * OWN, jp * 128 : (jp + 1) * 128] = piece
    lane = lax.broadcasted_iota(jnp.int32, (192, 2 * OWN), 1)
    up = one_hot(192, 192, lambda r: jnp.where(r % 16 == 15, -1, r + 1))
    down = one_hot(192, 192, lambda r: jnp.where(r % 16 == 0, -1, r - 1))
    for f in range(FRAMES + 2):
        src = grad[f] if f < FRAMES else following[f - FRAMES]
        wide[f * SPAN : (f + 1) * SPAN, :, : 2 * OWN] = src
    for g in range(0, (FRAMES + 2) * SPAN, 12):
        block = wide[g : g + 12, :, : 2 * OWN].reshape(192, 2 * OWN)
        moved = jnp.where(lane < OWN, mm(up, block), mm(down, block)).astype(BF16)
        wide[g : g + 12, :, 2 * OWN :] = moved.reshape(12, 16, 2 * OWN)
    total = jnp.zeros((FRAMES * ROWS * 16, 256), F32)
    for a in range(3):
        for b in range(3):
            tops = [(f + 2 - a) * SPAN + 2 - b for f in range(FRAMES)]
            win = jnp.concatenate([wide[x : x + ROWS] for x in tops], 0)
            total = total + mm(win.reshape(FRAMES * ROWS * 16, 4 * OWN), filters[a * 3 + b])
    total = total.reshape(FRAMES, ROWS, 16, 256)
    first = lax.axis_index("tm") % 2 == 0
    keep[...] = jnp.where(first, total[:2], total[2:])
    send[...] = jnp.where(first, total[2:], total[:2]).astype(BF16)


def halve_kernel(kept, got, keep, send):
    total = kept[...] + got[...].astype(F32)
    even = lax.axis_index("height") % CORES == 0
    keep[...] = jnp.where(even, total[:, :4], total[:, 4:])
    send[...] = jnp.where(even, total[:, 4:], total[:, :4])


def join_kernel(kept, got, out, mark):
    total = (kept[...] + got[...]).astype(BF16).reshape(128, 256)
    low = one_hot(256, 128, lambda r: jnp.where(r % 2 == 0, (r // 32) * 16 + (r % 32) // 2, -1))
    high = one_hot(256, 128, lambda r: jnp.where(r % 2 == 1, (r // 32) * 16 + (r % 32) // 2, -1))
    moved = mm(low, total[:, :128]) + mm(high, total[:, 128:])
    out[...] = moved.astype(BF16).reshape(out.shape)
    mark[...] = jnp.zeros_like(mark)


def inside(pairs, count):
    return [(i, k) for i, k in pairs if 0 <= k < count]


def body(clip, first_filter, second_filter, upstream):
    frames, rows, width, cin = clip.shape
    chans = first_filter.shape[4]
    tms, heights = lax.axis_size("tm"), lax.axis_size("height")
    lines = tms // 2
    siblings = [(i, i ^ 1) for i in range(heights)]
    blocks = [(t, t ^ 1) for t in range(tms)]

    here, edge = call(
        stack_kernel,
        [shaped((10, 32, 128), BF16), shaped((5, 32, 128), BF16)],
        [clip, upstream],
    )
    near_pairs = inside([(i, i + 1 if i % 2 else i - 1) for i in range(heights)], heights)
    edge = lax.ppermute(edge, "height", near_pairs)

    second = jnp.swapaxes(second_filter, 3, 4).reshape(27, chans // heights, chans)
    (pieces,) = call(
        filter_pieces_kernel,
        [shaped((heights, chans // heights, 27 * OWN), BF16)],
        [second],
        flops=2 * 27 * 16 * 256 * 128,
    )

    here, pieces = call(
        append_kernel,
        [shaped((15, 32, 128), BF16), shaped(pieces.shape, BF16)],
        [here, edge, pieces],
        scratch=[pltpu.SemaphoreType.DMA((2,))],
        idle=(0, 1, 2),
        alias={2: 1},
    )
    pair = lax.ppermute(here, "tm", blocks)
    forward, backward, pieces = call(
        choose_kernel,
        [shaped((12, 32, 128), BF16), shaped((3, 32, 128), BF16), shaped(pieces.shape, BF16)],
        [here, pair, pieces],
        idle=(2,),
        alias={2: 2},
    )
    second = lax.all_to_all(pieces, "height", 0, 0).reshape(chans, 27 * OWN)
    forth = inside([(t, t + 2) for t in range(tms)], tms)
    back = inside([(t, t - 2) for t in range(tms)], tms)
    before = lax.ppermute(forward, "tm", forth)
    after = lax.ppermute(backward, "tm", back)

    first = first_filter.reshape(27 * cin, chans)
    band, flat = call(
        own_filter_kernel,
        [shaped((3, 512, 6 * OWN), BF16), shaped((OWN, 27 * cin), BF16)],
        [first],
        flops=3 * 27 * 128 * 256 * 128,
    )

    (packed,) = call(
        pack_kernel, [shaped((45, 32, 128), BF16)], [here, pair, before, after]
    )
    other = lax.ppermute(packed, "height", siblings)

    units, up_units = 6 * HIGH, 3 * HALF_HIGH
    wide, ups, pre = call(
        preact_kernel,
        [
            shaped((units, 16, 512), BF16),
            shaped((2, up_units, 16, 256), BF16),
            shaped((2, 2, 2, HALF, 16, 2 * OWN), F32),
        ],
        [packed, other, band],
        scratch=[pltpu.VMEM((units, 32, 128), BF16), pltpu.VMEM((up_units, 16, 256), BF16)],
        flops=2 * 640 * 9 * 512 * 128,
    )
    grad_pre, parts = call(
        gradient_kernel,
        [shaped((FRAMES, SPAN, 16, 2 * OWN), BF16), shaped((heights, 7, 16, cin), BF16)],
        [second, ups, pre, wide],
        flops=2 * 512 * 9 * 512 * 128,
    )

    planes = [
        [(2 * z + x) * heights + CORES * g + core for x in range(2) for g in range(heights // 2)]
        for z in range(lines)
        for core in range(CORES)
    ]
    parts = lax.all_to_all(parts, ("tm", "height"), 0, 0, axis_index_groups=planes)
    following = lax.ppermute(grad_pre[:2], "tm", back)
    keep, send = call(
        clip_kernel,
        [shaped((2, ROWS, 16, 2 * cin), F32), shaped((2, ROWS, 16, 2 * cin), BF16)],
        [grad_pre, following, flat],
        scratch=[
            pltpu.VMEM(((FRAMES + 2) * SPAN, 16, 4 * OWN), BF16),
            pltpu.VMEM((9, 4 * OWN, 2 * cin), BF16),
        ],
        flops=2 * 512 * 9 * 256 * 256,
    )

    (sums,) = call(
        sum_turn_kernel,
        [shaped((lines, 16, 128), BF16)],
        [parts, send],
        idle=(1,),
    )
    columns = [[2 * ((i + 11) % lines) + x for i in range(lines)] for x in range(2)]
    summed = lax.all_to_all(sums, "tm", 0, 0, axis_index_groups=columns)
    got = lax.ppermute(send, "tm", blocks)
    keep, send = call(
        halve_kernel,
        [shaped((2, rows, 16, 2 * cin), F32)] * 2,
        [keep, got],
    )
    got = lax.ppermute(send, "height", siblings)
    grad_clip, mark = call(
        join_kernel, [shaped(clip.shape, BF16), shaped((8, 128), F32)], [keep, got]
    )
    count = frames * tms * rows * heights * width
    (grad_filter,) = call(
        functools.partial(finish_kernel, 1.0 / float(count) ** 0.5),
        [shaped((27, cin // tms, chans // heights), F32)],
        [summed, mark],
        idle=(1,),
    )
    grad_filter = grad_filter.reshape(3, 3, 3, cin // tms, chans // heights)
    return (grad_clip, grad_filter)


def solution(mesh):
    in_specs = (
        P("tm", "height", None, None),
        P(),
        P(None, None, None, None, "height"),
        P("tm", "height", None, None),
    )
    out_specs = (P("tm", "height", None, None), P(None, None, None, "tm", "height"))
    return jax.shard_map(body, mesh=mesh, in_specs=in_specs, out_specs=out_specs, check_vma=False)
```

```python
import functools

import jax
import jax.numpy as jnp
from jax import lax
from jax.experimental import pallas as pl
from jax.experimental.pallas import tpu as pltpu
from jax.sharding import PartitionSpec as P

F32, BF16 = jnp.float32, jnp.bfloat16
CORES = 2
OWN = 64
FRAMES = 4
ROWS, SPAN = 8, 10
HIGH, HALF_HIGH, HALF = ROWS + 4, ROWS // 2 + 2, SPAN // 2
MIDDLE = (1, 2, 3, 0)

LONG = {0: ((2, 0),), 1: ((0, 0), (1, 1))}
WIDE = {0: ((1, 0), (2, 1)), 1: ((0, 1),)}


def shift_classes():
    classes = []
    for t in (1, 0):
        for h in (1, 0):
            for w in (0, 1):
                taps = tuple(
                    ((a, b, c), (fp, ip, jp))
                    for a, fp in LONG[t]
                    for b, ip in LONG[h]
                    for c, jp in WIDE[w]
                )
                classes.append(((t, h, w), taps))
    return classes


CLASSES = shift_classes()
TAP_ORDER = [tap for _, taps in CLASSES for tap, _ in taps]


def mm(lhs, rhs):
    return jnp.dot(lhs, rhs, preferred_element_type=F32)


def one_hot(rows, cols, column_of):
    row = lax.broadcasted_iota(jnp.int32, (rows, cols), 0)
    col = lax.broadcasted_iota(jnp.int32, (rows, cols), 1)
    return jnp.where(column_of(row) == col, 1.0, 0.0).astype(BF16)


def call(kernel, out, args, scratch=(), idle=(), alias=None, flops=0, limit=16):
    spec = pl.BlockSpec(memory_space=pltpu.VMEM)
    far = pl.BlockSpec(memory_space=pl.ANY)
    moved = sum(x.size * x.dtype.itemsize for x in list(args) + list(out))
    return pl.pallas_call(
        kernel,
        out_shape=tuple(out),
        in_specs=[far if i in idle else spec for i in range(len(args))],
        out_specs=tuple([far if i in (alias or {}).values() else spec for i in range(len(out))]),
        input_output_aliases=dict(alias or {}),
        scratch_shapes=list(scratch),
        compiler_params=pltpu.CompilerParams(vmem_limit_bytes=limit * 1024 * 1024),
        cost_estimate=pl.CostEstimate(flops=flops, bytes_accessed=moved, transcendentals=0),
    )(*args)


def shaped(shape, dtype):
    return jax.ShapeDtypeStruct(shape, dtype)


def own_channel(place, x, core):
    return (2 * (place >> 3) + core) * 16 + 8 * x + (place & 7)


def filter_pieces_kernel(second, out):
    taps, depth, chans = second.shape
    x = lax.axis_index("tm") % 2
    row = lax.broadcasted_iota(jnp.int32, (chans, 2 * OWN), 0)
    col = lax.broadcasted_iota(jnp.int32, (chans, 2 * OWN), 1)
    order = jnp.where(own_channel(col & (OWN - 1), x, col >> 6) == row, 1.0, 0.0).astype(BF16)
    moved = mm(second[...].reshape(taps * depth, chans), order).astype(BF16)
    moved = moved.reshape(taps, depth, 2 * OWN)
    for place in range(0, len(TAP_ORDER), 2):
        pair = TAP_ORDER[place : place + 2]
        for core in range(CORES):
            lanes = slice(core * OWN, (core + 1) * OWN)
            piece = jnp.concatenate([moved[a * 9 + b * 3 + c, :, lanes] for a, b, c in pair], 1)
            for p in range(core, out.shape[0], CORES):
                out[p, :, place * OWN : place * OWN + piece.shape[1]] = piece


def own_filter_kernel(first, band, flat):
    chans = first.shape[1]
    x, core = lax.axis_index("tm") % 2, lax.axis_index("height") % CORES
    row = lax.broadcasted_iota(jnp.int32, (chans, 2 * OWN), 0)
    col = lax.broadcasted_iota(jnp.int32, (chans, 2 * OWN), 1)
    pick = jnp.where(own_channel(col & (OWN - 1), x, core) == row, 1.0, 0.0).astype(BF16)
    twice = mm(first[...], pick)
    lane = lax.broadcasted_iota(jnp.int32, (128, 2 * OWN), 1)
    for ab in range(9):
        lanes = slice((ab % 3) * 128, (ab % 3 + 1) * 128)
        for s in range(4):
            left = twice[(ab * 3 + s) * 128 : (ab * 3 + s + 1) * 128] if s < 3 else 0.0
            right = twice[(ab * 3 + s - 1) * 128 : (ab * 3 + s) * 128] if s > 0 else 0.0
            both = jnp.where(lane < OWN, left, right)
            band[ab // 3, s * 128 : (s + 1) * 128, lanes] = both.astype(BF16)
    row = lax.broadcasted_iota(jnp.int32, (OWN, chans), 0)
    col = lax.broadcasted_iota(jnp.int32, (OWN, chans), 1)
    pick = jnp.where(own_channel(row, x, core) == col, 1.0, 0.0).astype(BF16)
    flat[...] = lax.dot_general(
        pick, first[...], (((1,), (1,)), ((), ())), preferred_element_type=F32
    ).astype(BF16)


def stack_kernel(clip, up, here, edge):
    at_top = lax.axis_index("height") % CORES == 0
    for f in range(2):
        here[4 * f : 4 * f + 4] = clip[f]
        edge[2 * f : 2 * f + 2] = jnp.where(at_top, clip[f, :2], clip[f, 2:])
    for half in range(2):
        subs = slice(16 * half, 16 * half + 16)
        src = up[0, :, :, 128 * half : 128 * half + 128]
        here[8:10, subs] = src
        edge[4, subs] = jnp.where(at_top, src[0], src[1])


def append_kernel(here, edge, _, out, __, sems):
    copies = [
        pltpu.make_async_copy(here, out.at[:10], sems.at[0]),
        pltpu.make_async_copy(edge, out.at[10:], sems.at[1]),
    ]
    for copy in copies:
        copy.start()
    for copy in copies:
        copy.wait()


def choose_kernel(here, pair, _, forward, backward, __):
    first = lax.axis_index("tm") % 2 == 0
    forward[:8] = jnp.where(first, pair[:8], here[:8])
    forward[8:12] = jnp.where(first, pair[10:14], here[10:14])
    backward[:2] = jnp.where(first, here[8:10], pair[8:10])
    backward[2] = jnp.where(first, here[14], pair[14])


def pack_kernel(here, pair, before, after, packed):
    first = lax.axis_index("tm") % 2 == 0
    one = jnp.where(first, here[...], pair[...])
    two = jnp.where(first, pair[...], here[...])
    packed[:8] = before[:8]
    packed[30:34] = before[8:12]
    for k, src in ((1, one), (2, two)):
        packed[8 * k : 8 * k + 8] = src[:8]
        packed[30 + 4 * k : 34 + 4 * k] = src[10:14]
    for t, src in enumerate((one[8:10], two[8:10], after[:2])):
        packed[24 + 2 * t : 26 + 2 * t] = src
    for t, src in enumerate((one[14], two[14], after[2])):
        packed[42 + t] = src


def preact_kernel(own, other, filters, wide, ups, pre, band, ext):
    member = lax.axis_index("height") % CORES
    even = member == 0
    above = jnp.where(even, own[30:45], other[30:45])
    below = jnp.where(even, other[30:45], own[30:45])
    for f in range(6):
        base = f * HIGH
        band[pl.ds(base + 2 + 4 * member, 4)] = own[4 * f : 4 * f + 4]
        band[pl.ds(base + 6 - 4 * member, 4)] = other[4 * f : 4 * f + 4]
        band[base : base + 2] = above[2 * f : 2 * f + 2]
        band[base + ROWS + 2 : base + ROWS + 4] = below[2 * f : 2 * f + 2]
    for t in range(3):
        base, unit = t * HALF_HIGH, 24 + 2 * t
        for half in range(2):
            lanes = slice(128 * half, 128 * half + 128)
            subs = slice(16 * half, 16 * half + 16)
            ext[pl.ds(base + 1 + 2 * member, 2), :, lanes] = own[unit : unit + 2, subs]
            ext[pl.ds(base + 3 - 2 * member, 2), :, lanes] = other[unit : unit + 2, subs]
            ext[base, :, lanes] = above[12 + t, subs]
            ext[base + HALF_HIGH - 1, :, lanes] = below[12 + t, subs]
    units = ext.shape[0]
    flat = ext[...].reshape(units * 16, 256)
    shift = one_hot(units * 16, units * 16, lambda r: jnp.where((r & 15) == 15, -1, r + 1))
    ups[0] = flat.reshape(units, 16, 256)
    ups[1] = mm(shift, flat).astype(BF16).reshape(units, 16, 256)

    def column(r):
        unit, w = (r >> 4) & 7, 2 * (r & 15) + (r >> 7) - 1
        return jnp.where((w >= 0) & (w < 32), unit * 32 + w, -1)

    matrix = one_hot(512, 256, column)
    for g in range(band.shape[0] // 8):
        moved = mm(matrix, band[8 * g : 8 * g + 8].reshape(256, 128)).astype(BF16)
        for s in range(4):
            piece = moved[128 * s : 128 * s + 128].reshape(8, 16, 128)
            wide[8 * g : 8 * g + 8, :, s * 128 : (s + 1) * 128] = piece
    total = jnp.zeros((FRAMES, SPAN, 16, 2 * OWN), F32)
    for a in range(3):
        tops = [(a + f) * HIGH for f in range(FRAMES)]
        win = jnp.concatenate([wide[x : x + SPAN + 1] for x in tops], 0)
        prod = mm(win.reshape(FRAMES * (SPAN + 1) * 16, 512), filters[a, :, : 4 * OWN])
        prod = prod.reshape(FRAMES, SPAN + 1, 16, 4 * OWN)
        total = total + prod[:, :SPAN, :, : 2 * OWN] + prod[:, 1:, :, 2 * OWN :]
        win = jnp.concatenate([wide[x + 2 : x + 2 + SPAN] for x in tops], 0)
        prod = mm(win.reshape(FRAMES * SPAN * 16, 512), filters[a, :, 4 * OWN :])
        total = total + prod.reshape(FRAMES, SPAN, 16, 2 * OWN)
    sig = jax.nn.sigmoid(total)
    total = sig * (1.0 + total * (1.0 - sig))
    for f in range(FRAMES):
        for r in range(SPAN):
            pre[f % 2, r % 2, f // 2, r // 2] = total[f, r]


def gradient_kernel(second, ups, pre, wide, grad, parts):
    group = lax.axis_index("height") // CORES
    first_band = group == 0
    last_band = group == lax.axis_size("height") // CORES - 1
    even, odd = {}, {}
    offset = 0
    for (t, h, w), taps in CLASSES:
        tops = [(t + q) * HALF_HIGH + h for q in range(2)]
        lhs = jnp.concatenate([ups[w, x : x + HALF] for x in tops], 0).reshape(32 * HALF, 256)
        prod = mm(lhs, second[:, offset : offset + len(taps) * OWN])
        offset += len(taps) * OWN
        total, step = (odd, 1) if w else (even, 2)
        for k in range(0, len(taps), step):
            key = taps[k][1][:2]
            piece = prod[:, k * OWN : (k + step) * OWN]
            total[key] = total[key] + piece if key in total else piece
    blank = jnp.zeros((32 * HALF, OWN), F32)
    for (fp, ip), act in even.items():
        act = act + jnp.concatenate([blank, odd[fp, ip]], 1)
        x = pre[fp, ip].reshape(32 * HALF, 2 * OWN)
        g = (act * x).reshape(2, HALF, 16, 2 * OWN)
        for q in range(2):
            for p in range(HALF):
                piece, r = g[q, p], 2 * p + ip
                if r == 0:
                    piece = jnp.where(first_band, 0.0, piece)
                if r == SPAN - 1:
                    piece = jnp.where(last_band, 0.0, piece)
                grad[2 * q + fp, r] = piece.astype(BF16)
    turned = grad[:, 1 : 1 + ROWS].reshape(FRAMES * ROWS * 16, 2 * OWN).T
    strips = []
    for a in range(3):
        for b in range(3):
            tops = [(a + f) * HIGH + 1 + b for f in range(FRAMES)]
            win = jnp.concatenate([wide[x : x + ROWS] for x in tops], 0)
            prod = mm(turned, win.reshape(FRAMES * ROWS * 16, 512))
            for c in range(3):
                piece = prod[:OWN, 128 * c : 128 * c + 128]
                piece = piece + prod[OWN:, 128 * c + 128 : 128 * c + 256]
                strips.append(piece.astype(BF16))
    strips.append(jnp.zeros_like(strips[0]))
    row = lax.broadcasted_iota(jnp.int32, (256, 256), 0)
    col = lax.broadcasted_iota(jnp.int32, (256, 256), 1)
    x, tap, z, e = col >> 7, (col >> 6) & 1, (col >> 2) & 15, col & 3
    order = jnp.where(tap * 128 + 8 * z + 4 * x + e == row, 1.0, 0.0).astype(BF16)
    blocks = OWN // 8
    for k in range(7):
        pairs = [jnp.concatenate(strips[i : i + 2], 1) for i in (4 * k, 4 * k + 2)]
        pairs = [mm(pair, order).reshape(blocks, 8, 256) for pair in pairs]
        both = jnp.concatenate(pairs, 1).astype(BF16)
        for x in range(2):
            parts[x * blocks : (x + 1) * blocks, k] = both[:, :, 128 * x : 128 * x + 128]


def sum_turn_kernel(parts, _, out):
    blank = jnp.zeros((16, 128), F32)
    blocks = parts.shape[0] // 2
    halves = []
    for x in range(2):
        total = parts[x * blocks].astype(F32)
        for i in range(1, blocks):
            total = total + parts[x * blocks + i].astype(F32)
        halves += [total.reshape(112, 128), blank]
    flat = jnp.concatenate(halves, 0).T
    for i in range(16):
        z = (i + 8) % 16
        rows = [(tap * 64 + z * 4, x) for x in range(2) for tap in range(2)]
        block = [flat[r : r + 4, 128 * x : 128 * x + 128] for r, x in rows]
        out[i] = jnp.concatenate(block, 0).astype(BF16)


def finish_kernel(scale, parts, _, out):
    total = parts[0].astype(F32)
    for i in range(1, parts.shape[0]):
        total = total + parts[i].astype(F32)
    total = total * scale
    for k in range(27):
        lanes = slice(8 * (k // 2), 8 * (k // 2) + 8)
        rows = [8 * x + 4 * (k % 2) for x in range(2)]
        out[k] = jnp.concatenate([total[r : r + 4, lanes] for r in rows], 1)


def clip_kernel(grad, following, flat, keep, send, wide, filters):
    for ab in range(9):
        for slot, s in enumerate(MIDDLE):
            for jp in range(2):
                c = jp + 2 - s
                if 0 <= c <= 2:
                    piece = flat[:, (ab * 3 + c) * 128 : (ab * 3 + c + 1) * 128]
                else:
                    piece = jnp.zeros((OWN, 128), BF16)
                filters[ab, slot * OWN : (slot + 1) * OWN, jp * 128 : (jp + 1) * 128] = piece
    lane = lax.broadcasted_iota(jnp.int32, (192, 2 * OWN), 1)
    up = one_hot(192, 192, lambda r: jnp.where((r & 15) == 15, -1, r + 1))
    down = one_hot(192, 192, lambda r: jnp.where((r & 15) == 0, -1, r - 1))
    for f in range(FRAMES + 2):
        src = grad[f] if f < FRAMES else following[f - FRAMES]
        wide[f * SPAN : (f + 1) * SPAN, :, : 2 * OWN] = src
    for g in range(0, (FRAMES + 2) * SPAN, 12):
        block = wide[g : g + 12, :, : 2 * OWN].reshape(192, 2 * OWN)
        moved = jnp.where(lane < OWN, mm(up, block), mm(down, block)).astype(BF16)
        wide[g : g + 12, :, 2 * OWN :] = moved.reshape(12, 16, 2 * OWN)
    total = jnp.zeros((FRAMES * ROWS * 16, 256), F32)
    for a in range(3):
        for b in range(3):
            tops = [(f + 2 - a) * SPAN + 2 - b for f in range(FRAMES)]
            win = jnp.concatenate([wide[x : x + ROWS] for x in tops], 0)
            total = total + mm(win.reshape(FRAMES * ROWS * 16, 4 * OWN), filters[a * 3 + b])
    total = total.reshape(FRAMES, ROWS, 16, 256)
    first = lax.axis_index("tm") % 2 == 0
    keep[...] = jnp.where(first, total[:2], total[2:])
    send[...] = jnp.where(first, total[2:], total[:2]).astype(BF16)


def halve_kernel(kept, got, keep, send):
    total = kept[...] + got[...].astype(F32)
    even = lax.axis_index("height") % CORES == 0
    keep[...] = jnp.where(even, total[:, :4], total[:, 4:])
    send[...] = jnp.where(even, total[:, 4:], total[:, :4])


def join_kernel(kept, got, out, mark):
    total = (kept[...] + got[...]).astype(BF16).reshape(128, 256)
    low = one_hot(256, 128, lambda r: jnp.where((r & 1) == 0, (r >> 5) * 16 + ((r & 31) >> 1), -1))
    high = one_hot(256, 128, lambda r: jnp.where((r & 1) == 1, (r >> 5) * 16 + ((r & 31) >> 1), -1))
    moved = mm(low, total[:, :128]) + mm(high, total[:, 128:])
    out[...] = moved.astype(BF16).reshape(out.shape)
    mark[...] = jnp.zeros_like(mark)


def inside(pairs, count):
    return [(i, k) for i, k in pairs if 0 <= k < count]


def body(clip, first_filter, second_filter, upstream):
    frames, rows, width, cin = clip.shape
    chans = first_filter.shape[4]
    tms, heights = lax.axis_size("tm"), lax.axis_size("height")
    lines = tms // 2
    siblings = [(i, i ^ 1) for i in range(heights)]
    blocks = [(t, t ^ 1) for t in range(tms)]

    here, edge = call(
        stack_kernel,
        [shaped((10, 32, 128), BF16), shaped((5, 32, 128), BF16)],
        [clip, upstream],
    )
    near_pairs = inside([(i, i + 1 if i % 2 else i - 1) for i in range(heights)], heights)
    edge = lax.ppermute(edge, "height", near_pairs)

    second = jnp.swapaxes(second_filter, 3, 4).reshape(27, chans // heights, chans)
    (pieces,) = call(
        filter_pieces_kernel,
        [shaped((heights, chans // heights, 27 * OWN), BF16)],
        [second],
        flops=2 * 27 * 16 * 256 * 128,
    )

    here, pieces = call(
        append_kernel,
        [shaped((15, 32, 128), BF16), shaped(pieces.shape, BF16)],
        [here, edge, pieces],
        scratch=[pltpu.SemaphoreType.DMA((2,))],
        idle=(0, 1, 2),
        alias={2: 1},
    )
    pair = lax.ppermute(here, "tm", blocks)
    forward, backward, pieces = call(
        choose_kernel,
        [shaped((12, 32, 128), BF16), shaped((3, 32, 128), BF16), shaped(pieces.shape, BF16)],
        [here, pair, pieces],
        idle=(2,),
        alias={2: 2},
    )
    second = lax.all_to_all(pieces, "height", 0, 0).reshape(chans, 27 * OWN)
    forth = inside([(t, t + 2) for t in range(tms)], tms)
    back = inside([(t, t - 2) for t in range(tms)], tms)
    before = lax.ppermute(forward, "tm", forth)
    after = lax.ppermute(backward, "tm", back)

    first = first_filter.reshape(27 * cin, chans)
    band, flat = call(
        own_filter_kernel,
        [shaped((3, 512, 6 * OWN), BF16), shaped((OWN, 27 * cin), BF16)],
        [first],
        flops=3 * 27 * 128 * 256 * 128,
    )

    (packed,) = call(
        pack_kernel, [shaped((45, 32, 128), BF16)], [here, pair, before, after]
    )
    other = lax.ppermute(packed, "height", siblings)

    units, up_units = 6 * HIGH, 3 * HALF_HIGH
    wide, ups, pre = call(
        preact_kernel,
        [
            shaped((units, 16, 512), BF16),
            shaped((2, up_units, 16, 256), BF16),
            shaped((2, 2, 2, HALF, 16, 2 * OWN), F32),
        ],
        [packed, other, band],
        scratch=[pltpu.VMEM((units, 32, 128), BF16), pltpu.VMEM((up_units, 16, 256), BF16)],
        flops=2 * 640 * 9 * 512 * 128,
    )
    grad_pre, parts = call(
        gradient_kernel,
        [shaped((FRAMES, SPAN, 16, 2 * OWN), BF16), shaped((heights, 7, 16, cin), BF16)],
        [second, ups, pre, wide],
        flops=2 * 512 * 9 * 512 * 128,
    )

    planes = [
        [(2 * z + x) * heights + CORES * g + core for x in range(2) for g in range(heights // 2)]
        for z in range(lines)
        for core in range(CORES)
    ]
    parts = lax.all_to_all(parts, ("tm", "height"), 0, 0, axis_index_groups=planes)
    following = lax.ppermute(grad_pre[:2], "tm", back)
    keep, send = call(
        clip_kernel,
        [shaped((2, ROWS, 16, 2 * cin), F32), shaped((2, ROWS, 16, 2 * cin), BF16)],
        [grad_pre, following, flat],
        scratch=[
            pltpu.VMEM(((FRAMES + 2) * SPAN, 16, 4 * OWN), BF16),
            pltpu.VMEM((9, 4 * OWN, 2 * cin), BF16),
        ],
        flops=2 * 512 * 9 * 256 * 256,
    )

    (sums,) = call(
        sum_turn_kernel,
        [shaped((lines, 16, 128), BF16)],
        [parts, send],
        idle=(1,),
    )
    columns = [[2 * ((i + 8) % lines) + x for i in range(lines)] for x in range(2)]
    summed = lax.all_to_all(sums, "tm", 0, 0, axis_index_groups=columns)
    got = lax.ppermute(send, "tm", blocks)
    keep, send = call(
        halve_kernel,
        [shaped((2, rows, 16, 2 * cin), F32)] * 2,
        [keep, got],
    )
    got = lax.ppermute(send, "height", siblings)
    grad_clip, mark = call(
        join_kernel, [shaped(clip.shape, BF16), shaped((8, 128), F32)], [keep, got]
    )
    count = frames * tms * rows * heights * width
    (grad_filter,) = call(
        functools.partial(finish_kernel, 1.0 / float(count) ** 0.5),
        [shaped((27, cin // tms, chans // heights), F32)],
        [summed, mark],
        idle=(1,),
    )
    grad_filter = grad_filter.reshape(3, 3, 3, cin // tms, chans // heights)
    return (grad_clip, grad_filter)


def solution(mesh):
    in_specs = (
        P("tm", "height", None, None),
        P(),
        P(None, None, None, None, "height"),
        P("tm", "height", None, None),
    )
    out_specs = (P("tm", "height", None, None), P(None, None, None, "tm", "height"))
    return jax.shard_map(body, mesh=mesh, in_specs=in_specs, out_specs=out_specs, check_vma=False)
```

```python
import functools

import jax
import jax.numpy as jnp
from jax import lax
from jax.experimental import pallas as pl
from jax.experimental.pallas import tpu as pltpu
from jax.sharding import PartitionSpec as P

F32, BF16 = jnp.float32, jnp.bfloat16
CORES = 2
OWN = 64
FRAMES = 4
ROWS, SPAN = 8, 10
HIGH, HALF_HIGH, HALF = ROWS + 4, ROWS // 2 + 2, SPAN // 2
MIDDLE = (1, 2, 3, 0)

LONG = {0: ((2, 0),), 1: ((0, 0), (1, 1))}
WIDE = {0: ((1, 0), (2, 1)), 1: ((0, 1),)}


def shift_classes():
    classes = []
    for t in (1, 0):
        for h in (1, 0):
            for w in (0, 1):
                taps = tuple(
                    ((a, b, c), (fp, ip, jp))
                    for a, fp in LONG[t]
                    for b, ip in LONG[h]
                    for c, jp in WIDE[w]
                )
                classes.append(((t, h, w), taps))
    return classes


CLASSES = shift_classes()
TAP_ORDER = [tap for _, taps in CLASSES for tap, _ in taps]


def mm(lhs, rhs):
    return jnp.dot(lhs, rhs, preferred_element_type=F32)


def one_hot(rows, cols, column_of):
    row = lax.broadcasted_iota(jnp.int32, (rows, cols), 0)
    col = lax.broadcasted_iota(jnp.int32, (rows, cols), 1)
    return jnp.where(column_of(row) == col, 1.0, 0.0).astype(BF16)


def call(kernel, out, args, scratch=(), idle=(), alias=None, flops=0, limit=16):
    spec = pl.BlockSpec(memory_space=pltpu.VMEM)
    far = pl.BlockSpec(memory_space=pl.ANY)
    moved = sum(x.size * x.dtype.itemsize for x in list(args) + list(out))
    return pl.pallas_call(
        kernel,
        out_shape=tuple(out),
        in_specs=[far if i in idle else spec for i in range(len(args))],
        out_specs=tuple([far if i in (alias or {}).values() else spec for i in range(len(out))]),
        input_output_aliases=dict(alias or {}),
        scratch_shapes=list(scratch),
        compiler_params=pltpu.CompilerParams(vmem_limit_bytes=limit * 1024 * 1024),
        cost_estimate=pl.CostEstimate(flops=flops, bytes_accessed=moved, transcendentals=0),
    )(*args)


def shaped(shape, dtype):
    return jax.ShapeDtypeStruct(shape, dtype)


def own_channel(place, x, core):
    return (2 * (place >> 3) + core) * 16 + 8 * x + (place & 7)


def filter_pieces_kernel(second, out):
    taps, depth, chans = second.shape
    x = lax.axis_index("tm") % 2
    row = lax.broadcasted_iota(jnp.int32, (chans, 2 * OWN), 0)
    col = lax.broadcasted_iota(jnp.int32, (chans, 2 * OWN), 1)
    order = jnp.where(own_channel(col & (OWN - 1), x, col >> 6) == row, 1.0, 0.0).astype(BF16)
    moved = mm(second[...].reshape(taps * depth, chans), order).astype(BF16)
    moved = moved.reshape(taps, depth, 2 * OWN)
    for place in range(0, len(TAP_ORDER), 2):
        pair = TAP_ORDER[place : place + 2]
        for core in range(CORES):
            lanes = slice(core * OWN, (core + 1) * OWN)
            piece = jnp.concatenate([moved[a * 9 + b * 3 + c, :, lanes] for a, b, c in pair], 1)
            for p in range(core, out.shape[0], CORES):
                out[p, :, place * OWN : place * OWN + piece.shape[1]] = piece


def own_filter_kernel(first, band, flat):
    chans = first.shape[1]
    x, core = lax.axis_index("tm") % 2, lax.axis_index("height") % CORES
    row = lax.broadcasted_iota(jnp.int32, (chans, 2 * OWN), 0)
    col = lax.broadcasted_iota(jnp.int32, (chans, 2 * OWN), 1)
    pick = jnp.where(own_channel(col & (OWN - 1), x, core) == row, 1.0, 0.0).astype(BF16)
    twice = mm(first[...], pick)
    lane = lax.broadcasted_iota(jnp.int32, (128, 2 * OWN), 1)
    for ab in range(9):
        lanes = slice((ab % 3) * 128, (ab % 3 + 1) * 128)
        for s in range(4):
            left = twice[(ab * 3 + s) * 128 : (ab * 3 + s + 1) * 128] if s < 3 else 0.0
            right = twice[(ab * 3 + s - 1) * 128 : (ab * 3 + s) * 128] if s > 0 else 0.0
            both = jnp.where(lane < OWN, left, right)
            band[ab // 3, s * 128 : (s + 1) * 128, lanes] = both.astype(BF16)
    row = lax.broadcasted_iota(jnp.int32, (OWN, chans), 0)
    col = lax.broadcasted_iota(jnp.int32, (OWN, chans), 1)
    pick = jnp.where(own_channel(row, x, core) == col, 1.0, 0.0).astype(BF16)
    flat[...] = lax.dot_general(
        pick, first[...], (((1,), (1,)), ((), ())), preferred_element_type=F32
    ).astype(BF16)


def stack_kernel(clip, up, here, edge):
    at_top = lax.axis_index("height") % CORES == 0
    for f in range(2):
        here[4 * f : 4 * f + 4] = clip[f]
        edge[2 * f : 2 * f + 2] = jnp.where(at_top, clip[f, :2], clip[f, 2:])
    for half in range(2):
        subs = slice(16 * half, 16 * half + 16)
        src = up[0, :, :, 128 * half : 128 * half + 128]
        here[8:10, subs] = src
        edge[4, subs] = jnp.where(at_top, src[0], src[1])


def append_kernel(here, edge, _, out, __, sems):
    copies = [
        pltpu.make_async_copy(here, out.at[:10], sems.at[0]),
        pltpu.make_async_copy(edge, out.at[10:], sems.at[1]),
    ]
    for copy in copies:
        copy.start()
    for copy in copies:
        copy.wait()


def choose_kernel(here, pair, _, forward, backward, __):
    first = lax.axis_index("tm") % 2 == 0
    forward[:8] = jnp.where(first, pair[:8], here[:8])
    forward[8:12] = jnp.where(first, pair[10:14], here[10:14])
    backward[:2] = jnp.where(first, here[8:10], pair[8:10])
    backward[2] = jnp.where(first, here[14], pair[14])


def pack_kernel(here, pair, before, after, packed):
    first = lax.axis_index("tm") % 2 == 0
    one = jnp.where(first, here[...], pair[...])
    two = jnp.where(first, pair[...], here[...])
    packed[:8] = before[:8]
    packed[30:34] = before[8:12]
    for k, src in ((1, one), (2, two)):
        packed[8 * k : 8 * k + 8] = src[:8]
        packed[30 + 4 * k : 34 + 4 * k] = src[10:14]
    for t, src in enumerate((one[8:10], two[8:10], after[:2])):
        packed[24 + 2 * t : 26 + 2 * t] = src
    for t, src in enumerate((one[14], two[14], after[2])):
        packed[42 + t] = src


def preact_kernel(own, other, filters, wide, ups, pre, band, ext):
    member = lax.axis_index("height") % CORES
    even = member == 0
    above = jnp.where(even, own[30:45], other[30:45])
    below = jnp.where(even, other[30:45], own[30:45])
    for f in range(6):
        base = f * HIGH
        band[pl.ds(base + 2 + 4 * member, 4)] = own[4 * f : 4 * f + 4]
        band[pl.ds(base + 6 - 4 * member, 4)] = other[4 * f : 4 * f + 4]
        band[base : base + 2] = above[2 * f : 2 * f + 2]
        band[base + ROWS + 2 : base + ROWS + 4] = below[2 * f : 2 * f + 2]
    for t in range(3):
        base, unit = t * HALF_HIGH, 24 + 2 * t
        for half in range(2):
            lanes = slice(128 * half, 128 * half + 128)
            subs = slice(16 * half, 16 * half + 16)
            ext[pl.ds(base + 1 + 2 * member, 2), :, lanes] = own[unit : unit + 2, subs]
            ext[pl.ds(base + 3 - 2 * member, 2), :, lanes] = other[unit : unit + 2, subs]
            ext[base, :, lanes] = above[12 + t, subs]
            ext[base + HALF_HIGH - 1, :, lanes] = below[12 + t, subs]
    units = ext.shape[0]
    flat = ext[...].reshape(units * 16, 256)
    shift = one_hot(units * 16, units * 16, lambda r: jnp.where((r & 15) == 15, -1, r + 1))
    ups[0] = flat.reshape(units, 16, 256)
    ups[1] = mm(shift, flat).astype(BF16).reshape(units, 16, 256)

    def column(r):
        unit, w = (r >> 4) & 7, 2 * (r & 15) + (r >> 7) - 1
        return jnp.where((w >= 0) & (w < 32), unit * 32 + w, -1)

    matrix = one_hot(512, 256, column)
    for g in range(band.shape[0] // 8):
        moved = mm(matrix, band[8 * g : 8 * g + 8].reshape(256, 128)).astype(BF16)
        for s in range(4):
            piece = moved[128 * s : 128 * s + 128].reshape(8, 16, 128)
            wide[8 * g : 8 * g + 8, :, s * 128 : (s + 1) * 128] = piece
    total = jnp.zeros((FRAMES, SPAN, 16, 2 * OWN), F32)
    for a in range(3):
        tops = [(a + f) * HIGH for f in range(FRAMES)]
        win = jnp.concatenate([wide[x : x + SPAN + 1] for x in tops], 0)
        prod = mm(win.reshape(FRAMES * (SPAN + 1) * 16, 512), filters[a, :, : 4 * OWN])
        prod = prod.reshape(FRAMES, SPAN + 1, 16, 4 * OWN)
        total = total + prod[:, :SPAN, :, : 2 * OWN] + prod[:, 1:, :, 2 * OWN :]
        win = jnp.concatenate([wide[x + 2 : x + 2 + SPAN] for x in tops], 0)
        prod = mm(win.reshape(FRAMES * SPAN * 16, 512), filters[a, :, 4 * OWN :])
        total = total + prod.reshape(FRAMES, SPAN, 16, 2 * OWN)
    sig = jax.nn.sigmoid(total)
    total = sig * (1.0 + total * (1.0 - sig))
    for f in range(FRAMES):
        for r in range(SPAN):
            pre[f % 2, r % 2, f // 2, r // 2] = total[f, r]


def gradient_kernel(second, ups, pre, wide, grad, parts):
    group = lax.axis_index("height") // CORES
    first_band = group == 0
    last_band = group == lax.axis_size("height") // CORES - 1
    even, odd = {}, {}
    offset = 0
    for (t, h, w), taps in CLASSES:
        tops = [(t + q) * HALF_HIGH + h for q in range(2)]
        lhs = jnp.concatenate([ups[w, x : x + HALF] for x in tops], 0).reshape(32 * HALF, 256)
        prod = mm(lhs, second[:, offset : offset + len(taps) * OWN])
        offset += len(taps) * OWN
        total, step = (odd, 1) if w else (even, 2)
        for k in range(0, len(taps), step):
            key = taps[k][1][:2]
            piece = prod[:, k * OWN : (k + step) * OWN]
            total[key] = total[key] + piece if key in total else piece
    blank = jnp.zeros((32 * HALF, OWN), F32)
    for (fp, ip), act in even.items():
        act = act + jnp.concatenate([blank, odd[fp, ip]], 1)
        x = pre[fp, ip].reshape(32 * HALF, 2 * OWN)
        g = (act * x).reshape(2, HALF, 16, 2 * OWN)
        for q in range(2):
            for p in range(HALF):
                piece, r = g[q, p], 2 * p + ip
                if r == 0:
                    piece = jnp.where(first_band, 0.0, piece)
                if r == SPAN - 1:
                    piece = jnp.where(last_band, 0.0, piece)
                grad[2 * q + fp, r] = piece.astype(BF16)
    turned = grad[:, 1 : 1 + ROWS].reshape(FRAMES * ROWS * 16, 2 * OWN).T
    strips = []
    for a in range(3):
        for b in range(3):
            tops = [(a + f) * HIGH + 1 + b for f in range(FRAMES)]
            win = jnp.concatenate([wide[x : x + ROWS] for x in tops], 0)
            prod = mm(turned, win.reshape(FRAMES * ROWS * 16, 512))
            for c in range(3):
                piece = prod[:OWN, 128 * c : 128 * c + 128]
                piece = piece + prod[OWN:, 128 * c + 128 : 128 * c + 256]
                strips.append(piece.astype(BF16))
    strips.append(jnp.zeros_like(strips[0]))
    row = lax.broadcasted_iota(jnp.int32, (256, 256), 0)
    col = lax.broadcasted_iota(jnp.int32, (256, 256), 1)
    x, tap, z, e = col >> 7, (col >> 6) & 1, (col >> 2) & 15, col & 3
    order = jnp.where(tap * 128 + 8 * z + 4 * x + e == row, 1.0, 0.0).astype(BF16)
    blocks = OWN // 8
    for k in range(7):
        pairs = [jnp.concatenate(strips[i : i + 2], 1) for i in (4 * k, 4 * k + 2)]
        pairs = [mm(pair, order).reshape(blocks, 8, 256) for pair in pairs]
        both = jnp.concatenate(pairs, 1).astype(BF16)
        for x in range(2):
            parts[x * blocks : (x + 1) * blocks, k] = both[:, :, 128 * x : 128 * x + 128]


def sum_turn_kernel(parts, _, out):
    blank = jnp.zeros((16, 128), F32)
    blocks = parts.shape[0] // 2
    halves = []
    for x in range(2):
        total = parts[x * blocks].astype(F32)
        for i in range(1, blocks):
            total = total + parts[x * blocks + i].astype(F32)
        halves += [total.reshape(112, 128), blank]
    flat = jnp.concatenate(halves, 0).T
    for i in range(16):
        z = (i + 8) % 16
        rows = [(tap * 64 + z * 4, x) for x in range(2) for tap in range(2)]
        block = [flat[r : r + 4, 128 * x : 128 * x + 128] for r, x in rows]
        out[i] = jnp.concatenate(block, 0).astype(BF16)


def finish_kernel(scale, parts, _, out):
    total = parts[0].astype(F32)
    for i in range(1, parts.shape[0]):
        total = total + parts[i].astype(F32)
    total = total * scale
    for k in range(27):
        lanes = slice(8 * (k // 2), 8 * (k // 2) + 8)
        rows = [8 * x + 4 * (k % 2) for x in range(2)]
        out[k] = jnp.concatenate([total[r : r + 4, lanes] for r in rows], 1)


def clip_kernel(grad, following, flat, keep, send, wide, filters):
    for ab in range(9):
        for slot, s in enumerate(MIDDLE):
            for jp in range(2):
                c = jp + 2 - s
                if 0 <= c <= 2:
                    piece = flat[:, (ab * 3 + c) * 128 : (ab * 3 + c + 1) * 128]
                else:
                    piece = jnp.zeros((OWN, 128), BF16)
                filters[ab, slot * OWN : (slot + 1) * OWN, jp * 128 : (jp + 1) * 128] = piece
    lane = lax.broadcasted_iota(jnp.int32, (192, 2 * OWN), 1)
    up = one_hot(192, 192, lambda r: jnp.where((r & 15) == 15, -1, r + 1))
    down = one_hot(192, 192, lambda r: jnp.where((r & 15) == 0, -1, r - 1))
    for f in range(FRAMES + 2):
        src = grad[f] if f < FRAMES else following[f - FRAMES]
        wide[f * SPAN : (f + 1) * SPAN, :, : 2 * OWN] = src
    for g in range(0, (FRAMES + 2) * SPAN, 12):
        block = wide[g : g + 12, :, : 2 * OWN].reshape(192, 2 * OWN)
        moved = jnp.where(lane < OWN, mm(up, block), mm(down, block)).astype(BF16)
        wide[g : g + 12, :, 2 * OWN :] = moved.reshape(12, 16, 2 * OWN)
    total = jnp.zeros((FRAMES * ROWS * 16, 256), F32)
    for a in range(3):
        for b in range(3):
            tops = [(f + 2 - a) * SPAN + 2 - b for f in range(FRAMES)]
            win = jnp.concatenate([wide[x : x + ROWS] for x in tops], 0)
            total = total + mm(win.reshape(FRAMES * ROWS * 16, 4 * OWN), filters[a * 3 + b])
    total = total.reshape(FRAMES, ROWS, 16, 256)
    even = lax.axis_index("height") % CORES == 0
    keep[...] = jnp.where(even, total[:, :4], total[:, 4:])
    send[...] = jnp.where(even, total[:, 4:], total[:, :4])


def halve_kernel(kept, got, keep, send):
    total = kept[...] + got[...]
    first = lax.axis_index("tm") % 2 == 0
    keep[...] = jnp.where(first, total[:2], total[2:])
    send[...] = jnp.where(first, total[2:], total[:2]).astype(BF16)


def join_kernel(kept, got, out, mark):
    total = (kept[...] + got[...].astype(F32)).astype(BF16).reshape(128, 256)
    low = one_hot(256, 128, lambda r: jnp.where((r & 1) == 0, (r >> 5) * 16 + ((r & 31) >> 1), -1))
    high = one_hot(256, 128, lambda r: jnp.where((r & 1) == 1, (r >> 5) * 16 + ((r & 31) >> 1), -1))
    moved = mm(low, total[:, :128]) + mm(high, total[:, 128:])
    out[...] = moved.astype(BF16).reshape(out.shape)
    mark[...] = jnp.zeros_like(mark)


def inside(pairs, count):
    return [(i, k) for i, k in pairs if 0 <= k < count]


def body(clip, first_filter, second_filter, upstream):
    frames, rows, width, cin = clip.shape
    chans = first_filter.shape[4]
    tms, heights = lax.axis_size("tm"), lax.axis_size("height")
    lines = tms // 2
    siblings = [(i, i ^ 1) for i in range(heights)]
    blocks = [(t, t ^ 1) for t in range(tms)]

    here, edge = call(
        stack_kernel,
        [shaped((10, 32, 128), BF16), shaped((5, 32, 128), BF16)],
        [clip, upstream],
    )
    near_pairs = inside([(i, i + 1 if i % 2 else i - 1) for i in range(heights)], heights)
    edge = lax.ppermute(edge, "height", near_pairs)

    second = jnp.swapaxes(second_filter, 3, 4).reshape(27, chans // heights, chans)
    (pieces,) = call(
        filter_pieces_kernel,
        [shaped((heights, chans // heights, 27 * OWN), BF16)],
        [second],
        flops=2 * 27 * 16 * 256 * 128,
    )

    here, pieces = call(
        append_kernel,
        [shaped((15, 32, 128), BF16), shaped(pieces.shape, BF16)],
        [here, edge, pieces],
        scratch=[pltpu.SemaphoreType.DMA((2,))],
        idle=(0, 1, 2),
        alias={2: 1},
    )
    pair = lax.ppermute(here, "tm", blocks)
    forward, backward, pieces = call(
        choose_kernel,
        [shaped((12, 32, 128), BF16), shaped((3, 32, 128), BF16), shaped(pieces.shape, BF16)],
        [here, pair, pieces],
        idle=(2,),
        alias={2: 2},
    )
    second = lax.all_to_all(pieces, "height", 0, 0).reshape(chans, 27 * OWN)
    forth = inside([(t, t + 2) for t in range(tms)], tms)
    back = inside([(t, t - 2) for t in range(tms)], tms)
    before = lax.ppermute(forward, "tm", forth)
    after = lax.ppermute(backward, "tm", back)

    first = first_filter.reshape(27 * cin, chans)
    band, flat = call(
        own_filter_kernel,
        [shaped((3, 512, 6 * OWN), BF16), shaped((OWN, 27 * cin), BF16)],
        [first],
        flops=3 * 27 * 128 * 256 * 128,
    )

    (packed,) = call(
        pack_kernel, [shaped((45, 32, 128), BF16)], [here, pair, before, after]
    )
    other = lax.ppermute(packed, "height", siblings)

    units, up_units = 6 * HIGH, 3 * HALF_HIGH
    wide, ups, pre = call(
        preact_kernel,
        [
            shaped((units, 16, 512), BF16),
            shaped((2, up_units, 16, 256), BF16),
            shaped((2, 2, 2, HALF, 16, 2 * OWN), F32),
        ],
        [packed, other, band],
        scratch=[pltpu.VMEM((units, 32, 128), BF16), pltpu.VMEM((up_units, 16, 256), BF16)],
        flops=2 * 640 * 9 * 512 * 128,
    )
    grad_pre, parts = call(
        gradient_kernel,
        [shaped((FRAMES, SPAN, 16, 2 * OWN), BF16), shaped((heights, 7, 16, cin), BF16)],
        [second, ups, pre, wide],
        flops=2 * 512 * 9 * 512 * 128,
    )

    planes = [
        [(2 * z + x) * heights + CORES * g + core for x in range(2) for g in range(heights // 2)]
        for z in range(lines)
        for core in range(CORES)
    ]
    parts = lax.all_to_all(parts, ("tm", "height"), 0, 0, axis_index_groups=planes)
    following = lax.ppermute(grad_pre[:2], "tm", back)
    keep, send = call(
        clip_kernel,
        [shaped((FRAMES, rows, 16, 2 * cin), F32)] * 2,
        [grad_pre, following, flat],
        scratch=[
            pltpu.VMEM(((FRAMES + 2) * SPAN, 16, 4 * OWN), BF16),
            pltpu.VMEM((9, 4 * OWN, 2 * cin), BF16),
        ],
        flops=2 * 512 * 9 * 256 * 256,
    )

    (sums,) = call(
        sum_turn_kernel,
        [shaped((lines, 16, 128), BF16)],
        [parts, send],
        idle=(1,),
    )
    columns = [[2 * ((i + 8) % lines) + x for i in range(lines)] for x in range(2)]
    summed = lax.all_to_all(sums, "tm", 0, 0, axis_index_groups=columns)
    got = lax.ppermute(send, "height", siblings)
    keep, send = call(
        halve_kernel,
        [shaped((2, rows, 16, 2 * cin), F32), shaped((2, rows, 16, 2 * cin), BF16)],
        [keep, got],
    )
    got = lax.ppermute(send, "tm", blocks)
    grad_clip, mark = call(
        join_kernel, [shaped(clip.shape, BF16), shaped((8, 128), F32)], [keep, got]
    )
    count = frames * tms * rows * heights * width
    (grad_filter,) = call(
        functools.partial(finish_kernel, 1.0 / float(count) ** 0.5),
        [shaped((27, cin // tms, chans // heights), F32)],
        [summed, mark],
        idle=(1,),
    )
    grad_filter = grad_filter.reshape(3, 3, 3, cin // tms, chans // heights)
    return (grad_clip, grad_filter)


def solution(mesh):
    in_specs = (
        P("tm", "height", None, None),
        P(),
        P(None, None, None, None, "height"),
        P("tm", "height", None, None),
    )
    out_specs = (P("tm", "height", None, None), P(None, None, None, "tm", "height"))
    return jax.shard_map(body, mesh=mesh, in_specs=in_specs, out_specs=out_specs, check_vma=False)
```
